256 devices in a mesh: seq: 64 (over x, z, core), head: 4 (over y).
Axes of the slice: x: 4, y: 4, z: 8, core: 2. Of those that a mesh axis runs over, the one named last changes fastest.
Arguments:
- queries: bfloat16 [32768, 2048], P('seq', 'head'), may hold values from -128 to 128
- out_grad: bfloat16 [32768, 2048], P('seq', 'head'), may hold values from -6 to 6
- neighbours: bfloat16 [2048, 128, 4096], P('seq', None, 'head'), may hold values from -400 to 400
- placement: int32 [512, 2], P('seq'), may hold values from 0 to 2047, as said below
Outputs:
- attended: bfloat16 [32768, 2048], P('seq', 'head')
- query_grad: bfloat16 [32768, 2048], P('seq', 'head')
The draws below stay inside these ranges and needn't reach their ends.
Inputs may be any that keep to these rules, and one draw needn't show every extreme that they name: placement[c, n] is the slot holding the n-th neighbour of span c; slot s is stored on index s // 32 of seq, and no slot is named twice. The 16 entries of one index of seq (aligned blocks of 8 rows) name at most 1 slots of one owner, and some index names exactly 1 of some owner; some owner has all its 32 slots named.
All inputs are finite; a program needn't handle non-finite values.
Results may differ from the reference program's by a relative error of at most 0.019.
The reference program's roundings to bfloat16 on the way count: a program that leaves them out, or rounds other values in their place, can miss the bound.
Values may be sent and summed in bfloat16 or wider, within the bound.
No kernel may reach another device: no remote copies, remote signals or barrier semaphores. Data moves between devices by JAX's collectives and lax.ppermute only.
A program may use at most 128 MiB of HBM per device.

```python
import math
from functools import partial
import jax
import jax.numpy as jnp
from jax import lax

D = 4096
HEADS = 16
HD = 128
SPAN = 64
R = 128
CH_DEV = 8
ITEMS_DEV = 16
SLOTS_DEV = 32
TOKENS = 32768
SPANS = 512
SLOTS = 2048
HQ = 2048
N_SEQ = 64


def draw_queries(key, part):
    key = jax.random.fold_in(key, 21)
    base_key = jax.random.fold_in(key, 0)
    values = jax.random.normal(base_key, (TOKENS, HQ), jnp.float32)
    return values.astype(jnp.bfloat16)


def draw_neighbours(key, part):
    key = jax.random.fold_in(key, 31)
    base_key, row_key, col_key = jax.random.split(key, 3)
    values = jax.random.truncated_normal(base_key, -4.0, 4.0, (SLOTS, R, D), jnp.float32)
    col_scale = jnp.exp(jax.random.uniform(col_key, (1, 1, D), jnp.float32, 0.0, math.log(10.0)))
    row_scale = jnp.exp(jax.random.uniform(row_key, (SLOTS, R, 1), jnp.float32, 0.0, math.log(10.0)))
    scaled = values * row_scale * col_scale
    return scaled.astype(jnp.bfloat16)


def draw_placement(key, part):
    key = jax.random.fold_in(key, 41)
    perm_key, score_key, shift_key = jax.random.split(key, 3)
    hot_count = N_SEQ // 4
    cold_count = N_SEQ - hot_count
    half_items = ITEMS_DEV // 2
    others = (1 + jax.random.permutation(perm_key, N_SEQ - 2)).astype(jnp.int32)
    hot_owners = jnp.concatenate([jnp.array([0, N_SEQ - 1], jnp.int32), others[:hot_count - 2]])
    cold_owners = others[hot_count - 2:]
    item_index = jnp.arange(ITEMS_DEV, dtype=jnp.int32)
    scores = jax.random.randint(score_key, (N_SEQ, ITEMS_DEV), 0, 1 << 20) * ITEMS_DEV + item_index[None, :]
    ranking = jnp.argsort(jnp.argsort(scores, axis=1), axis=1).astype(jnp.int32)
    device = jnp.arange(N_SEQ, dtype=jnp.int32)[:, None]
    hot_pick = hot_owners[(device + ranking) % hot_count]
    cold_pick = cold_owners[(device + ranking - half_items) % cold_count]
    owners = jnp.where(ranking < half_items, hot_pick, cold_pick).reshape(-1).astype(jnp.int32)
    total_items = N_SEQ * ITEMS_DEV
    counts = jnp.sum((owners[None, :] == jnp.arange(N_SEQ, dtype=jnp.int32)[:, None]).astype(jnp.int32), axis=1)
    starts = jnp.cumsum(counts) - counts
    sorted_index = jnp.argsort(owners, stable=True)
    sorted_rank = jnp.arange(total_items, dtype=jnp.int32) - starts[owners[sorted_index]]
    slot_ranks = jnp.zeros((total_items,), jnp.int32).at[sorted_index].set(sorted_rank.astype(jnp.int32))
    shifts = jax.random.randint(shift_key, (N_SEQ,), 0, SLOTS_DEV)
    local_slot = (slot_ranks + shifts[owners]) % SLOTS_DEV
    return (owners * SLOTS_DEV + local_slot).reshape(SPANS, 2).astype(jnp.int32)


def block_scale(stream_key, dims, shards, least, high):
    def one(dim, parts):
        steps = jax.random.uniform(jax.random.fold_in(jax.random.fold_in(stream_key, 6), dim), (parts,), jnp.float32, least / len(shards), high / len(shards))
        return jnp.repeat(jnp.exp(steps), dims[dim] // parts).reshape((-1,) + (1,) * (len(dims) - dim - 1))

    loudness = one(*shards[0])
    for cut in shards[1:]:
        loudness = loudness * one(*cut)
    return loudness


def scatter_about(rng, extent, scale, bound, shards=(), held_as=jnp.bfloat16):
    values = scale * jax.random.normal(rng, extent, jnp.float32)
    if shards:
        values = values * block_scale(rng, extent, shards, -0.22, 0.18)
    return jnp.clip(values, -bound, bound).astype(held_as)


def setup_inputs(seed: int = 0) -> dict:
    streams_of = jax.random.split(jax.random.key(seed), 5)
    queries = draw_queries(jax.random.fold_in(streams_of[4], 71), 0)
    out_grad = scatter_about(streams_of[1], (TOKENS, HQ), 1.0, 6.0, ((0, 64), (1, 4)))
    neighbours = draw_neighbours(jax.random.fold_in(streams_of[4], 71), 0)
    placement = draw_placement(jax.random.fold_in(streams_of[4], 71), 0)
    return {"queries": queries, "out_grad": out_grad, "neighbours": neighbours, "placement": placement}


def rounded(value):
    return lax.optimization_barrier(value.astype(jnp.bfloat16)).astype(jnp.float32)

def span_block(arrays, neighbours):
    span_queries, grad_spans, slot_pairs = arrays
    scale_factor = 1.0 / math.sqrt(HD)
    stored = neighbours[slot_pairs].astype(jnp.float32)
    row_scale = lax.rsqrt(lax.optimization_barrier(jnp.sum(stored * stored, axis=-1)) / D + 1e-06)
    normed = (stored * row_scale[..., None]).reshape(stored.shape[:3] + (HEADS, 2, HD))
    key_rows = rounded(normed[..., 0, :])
    query_float = span_queries.astype(jnp.float32)
    cond_scores = jnp.einsum('bnrhd,bthd->bnrht', key_rows, query_float) * scale_factor
    cond_weights = rounded(jax.nn.softmax(cond_scores, axis=-1))
    conditioned = jnp.einsum('bnrht,bthd->bnrhd', cond_weights, query_float)
    value_rows = rounded(normed[..., 1, :] + conditioned)
    scores = jnp.einsum('bthd,bnrhd->bnthr', query_float, key_rows) * scale_factor
    row_top = rounded(lax.optimization_barrier(jnp.max(scores, axis=-1)))
    exponent = jnp.exp(scores - row_top[..., None])
    row_total = rounded(lax.optimization_barrier(jnp.sum(exponent, axis=-1)))
    partial_out = rounded(jnp.einsum('bnthr,bnrhd->bnthd', rounded(exponent), value_rows))
    highest = lax.optimization_barrier(jnp.max(row_top, axis=1, keepdims=True))
    factor = jnp.exp(row_top - highest)
    weight = rounded(factor / lax.optimization_barrier(jnp.sum(factor * row_total, axis=1, keepdims=True)))
    attended = lax.optimization_barrier(jnp.sum(weight[..., None] * partial_out, axis=1)).astype(jnp.bfloat16)
    grad_float = grad_spans.astype(jnp.float32)
    products = lax.optimization_barrier(jnp.sum(grad_float[:, None] * partial_out, axis=-1))
    delta = rounded(lax.optimization_barrier(jnp.sum(weight * products, axis=1)))
    prob_grad = jnp.einsum('bthd,bnrhd->bnthr', grad_float, value_rows)
    term_a = rounded(jnp.einsum('bnthr,bnrhd->bnthd', rounded(exponent * prob_grad), key_rows))
    term_b = rounded(jnp.einsum('bnthr,bnrhd->bnthd', rounded(exponent), key_rows))
    query_terms = weight[..., None] * (term_a - delta[:, None, :, :, None] * term_b) * scale_factor
    query_grad = lax.optimization_barrier(jnp.sum(query_terms, axis=1)).astype(jnp.bfloat16)
    return (attended, query_grad)

def reference(queries, out_grad, neighbours, placement):
    span_queries = queries.reshape(N_SEQ, CH_DEV, SPAN, HEADS, HD)
    grad_spans = out_grad.reshape(N_SEQ, CH_DEV, SPAN, HEADS, HD)
    slot_pairs = placement.reshape(N_SEQ, CH_DEV, 2)
    attended, query_grad = lax.map(partial(span_block, neighbours=neighbours), (span_queries, grad_spans, slot_pairs))
    return (attended.reshape(TOKENS, HQ), query_grad.reshape(TOKENS, HQ))
```

```python
import math

import jax
import jax.numpy as jnp
from jax import lax
from jax.sharding import PartitionSpec as P

D = 4096
HD = 128
SPAN = 64
R = 128
BF = jnp.bfloat16
F32 = jnp.float32


def swap(rows):
    return lax.all_to_all(rows, "seq", split_axis=0, concat_axis=0, tiled=True)


def encode(span_queries, stored, row_scale):
    batch = stored.shape[0]
    heads_here = span_queries.shape[1]
    scale_factor = 1.0 / math.sqrt(HD)
    normed = stored.astype(F32) * row_scale[:, :, None]
    normed = normed.reshape(batch, R, heads_here, 2, HD)
    key_rows = normed[:, :, :, 0, :].astype(BF)
    cond_scores = (
        jnp.einsum("irhd,ihtd->irht", key_rows, span_queries, preferred_element_type=F32)
        * scale_factor
    )
    cond_weights = jax.nn.softmax(cond_scores, axis=-1).astype(BF)
    conditioned = jnp.einsum(
        "irht,ihtd->irhd", cond_weights, span_queries, preferred_element_type=F32
    )
    value_rows = (normed[:, :, :, 1, :] + conditioned).astype(BF)
    return key_rows, value_rows


def attend(span_queries, key_rows, value_rows):
    scale_factor = 1.0 / math.sqrt(HD)
    scores = (
        jnp.einsum("ihtd,irhd->ihtr", span_queries, key_rows, preferred_element_type=F32)
        * scale_factor
    )
    row_top = jnp.max(scores, axis=-1).astype(BF)
    exponent = jnp.exp(scores - lax.optimization_barrier(row_top).astype(F32)[..., None])
    row_total = jnp.sum(exponent, axis=-1).astype(BF)
    low = exponent.astype(BF)
    partial_out = jnp.einsum(
        "ihtr,irhd->ihtd", low, value_rows, preferred_element_type=F32
    ).astype(BF)
    term_b = jnp.einsum("ihtr,irhd->ihtd", low, key_rows, preferred_element_type=F32).astype(BF)
    return exponent, row_top, row_total, partial_out, term_b


def back_term(exponent, key_rows, value_rows, grad_rows):
    prob_grad = jnp.einsum("ihtd,irhd->ihtr", grad_rows, value_rows, preferred_element_type=F32)
    return jnp.einsum(
        "ihtr,irhd->ihtd", (exponent * prob_grad).astype(BF), key_rows, preferred_element_type=F32
    ).astype(BF)


def local(queries, out_grad, neighbours, placement):
    n = lax.axis_size("seq")
    width = queries.shape[1]
    heads = width // HD
    spans = placement.shape[0]
    slots = neighbours.shape[0]
    scale_factor = 1.0 / math.sqrt(HD)
    unit = SPAN * heads // n
    blocks = SPAN // unit
    all_spans, all_slots = n * spans, n * slots

    def to_pieces(rows):
        cut = rows.reshape(spans, blocks, unit, heads, HD)
        return cut.transpose(3, 1, 0, 2, 4).reshape(n, spans * unit, HD)

    pair = lax.all_gather(placement, "seq", axis=0, tiled=True)
    square_sums = jnp.sum(jnp.square(neighbours.astype(F32)), axis=-1)
    row_scale = lax.rsqrt(lax.psum(square_sums, "head") / D + 1e-06)

    first = swap(jnp.stack([to_pieces(queries), to_pieces(out_grad)], axis=1))
    first = first.reshape(n, 2, spans, unit * HD)
    q_piece = first[:, 0].reshape(all_spans, unit * HD)
    g_piece = first[:, 1].reshape(all_spans, unit * HD)

    slot_ids = jnp.arange(all_slots, dtype=jnp.int32)
    hit_a = (pair[:, 0][:, None] == slot_ids[None, :]).astype(BF)
    hit_b = (pair[:, 1][:, None] == slot_ids[None, :]).astype(BF)
    hit = hit_a + hit_b

    def to_owners(piece):
        picked = jnp.einsum("cs,cw->sw", hit, piece, preferred_element_type=F32).astype(BF)
        got = swap(picked.reshape(n, slots * unit, HD))
        got = got.reshape(n, slots, unit, HD).transpose(1, 0, 2, 3)
        return got.reshape(slots, heads, SPAN, HD)

    slot_queries = to_owners(q_piece)
    slot_grads = to_owners(g_piece)
    key_rows, value_rows = encode(slot_queries, neighbours, row_scale)
    exponent, top, total, partial_out, term_b = attend(slot_queries, key_rows, value_rows)

    def by_piece(rows):
        return rows.reshape(slots, n, unit * HD).transpose(1, 0, 2).reshape(n, slots * unit, HD)

    def stat_rows(rows):
        return rows.reshape(slots, n, unit).transpose(1, 0, 2).reshape(n, 1, slots * unit)

    back = swap(
        jnp.concatenate([by_piece(partial_out), stat_rows(top), stat_rows(total)], axis=1)
    )
    term_a = back_term(exponent, key_rows, value_rows, slot_grads)

    got_part = back[:, : slots * unit].reshape(all_slots, unit * HD)
    got_stat = back[:, slots * unit :].reshape(n, 2, slots, unit)
    got_stat = got_stat.transpose(0, 2, 1, 3).reshape(all_slots, 2 * unit)

    def pick(mask, rows):
        return jnp.einsum("cs,sw->cw", mask, rows, preferred_element_type=F32)

    part = [pick(m, got_part).reshape(all_spans, unit, HD) for m in (hit_a, hit_b)]
    stat = [pick(m, got_stat).reshape(all_spans, 2, unit) for m in (hit_a, hit_b)]
    tops = [s[:, 0] for s in stat]
    totals = [s[:, 1] for s in stat]
    highest = jnp.maximum(tops[0], tops[1])
    factor = [jnp.exp(t - highest) for t in tops]
    denominator = factor[0] * totals[0] + factor[1] * totals[1]
    low = [lax.optimization_barrier((f / denominator).astype(BF)) for f in factor]
    weight = [v.astype(F32) for v in low]
    attended = (weight[0][..., None] * part[0] + weight[1][..., None] * part[1]).astype(BF)
    grads = g_piece.reshape(all_spans, unit, HD).astype(F32)
    products = [jnp.sum(grads * p, axis=-1) for p in part]
    delta = (weight[0] * products[0] + weight[1] * products[1]).astype(BF)
    w_slot = jnp.einsum("cs,cw->sw", hit_a, low[0], preferred_element_type=F32) + jnp.einsum(
        "cs,cw->sw", hit_b, low[1], preferred_element_type=F32
    )
    d_slot = jnp.einsum("cs,cw->sw", hit, delta, preferred_element_type=F32)
    wd = jnp.stack(
        [w_slot.astype(BF).reshape(n, slots * unit), d_slot.astype(BF).reshape(n, slots * unit)],
        axis=1,
    )
    wd = swap(wd).reshape(n, 2, slots, unit).transpose(1, 2, 0, 3).reshape(2, slots, heads, SPAN)
    wd = wd.astype(F32)[..., None]
    terms = (
        wd[0] * (term_a.astype(F32) - wd[1] * term_b.astype(F32)) * scale_factor
    ).astype(BF)
    got_terms = swap(by_piece(terms)).reshape(all_slots, unit * HD)
    query_grad = pick(hit, got_terms).astype(BF)
    final = jnp.stack(
        [
            attended.reshape(n, spans * unit, HD),
            query_grad.reshape(n, spans * unit, HD),
        ],
        axis=1,
    )
    final = swap(final).reshape(heads, blocks, 2, spans, unit, HD)
    final = final.transpose(2, 3, 1, 4, 0, 5).reshape(2, spans * SPAN, width)
    return final[0], final[1]


def solution(mesh):
    in_specs = (P("seq", "head"), P("seq", "head"), P("seq", None, "head"), P("seq", None))
    out_specs = (P("seq", "head"), P("seq", "head"))
    return jax.shard_map(local, mesh=mesh, in_specs=in_specs, out_specs=out_specs, check_vma=False)
```

```python
import functools
import math

import jax
import jax.numpy as jnp
from jax import lax
from jax.experimental import pallas as pl
from jax.experimental.pallas import tpu as pltpu
from jax.sharding import PartitionSpec as P

D = 4096
HD = 128
SPAN = 64
R = 128
N = 64
C = 8
S = 32
H = 4
U = 4
TB = SPAN // U
W = U * HD
SPANS = N * C
SLOTS = N * S
HALF = S // 2
SCALE = 1.0 / math.sqrt(HD)
BF = jnp.bfloat16
F32 = jnp.float32
MIB = 1 << 20


def iota(shape, dim):
    return lax.broadcasted_iota(jnp.int32, shape, dim)


def hot(mask):
    return jnp.where(mask, 1.0, 0.0).astype(BF)


def mm(a, b):
    return jnp.dot(a, b, preferred_element_type=F32)


def mm_t(a, b):
    return lax.dot_general(a, b, (((1,), (1,)), ((), ())), preferred_element_type=F32)


def t_mm(a, b):
    return lax.dot_general(a, b, (((0,), (0,)), ((), ())), preferred_element_type=F32)


def call(body, out_shape, flops=1e8, nbytes=4e6, vmem=40, **kw):
    return pl.pallas_call(
        body,
        out_shape=out_shape,
        compiler_params=pltpu.CompilerParams(vmem_limit_bytes=vmem * MIB),
        cost_estimate=pl.CostEstimate(
            flops=int(flops), bytes_accessed=int(nbytes), transcendentals=0
        ),
        **kw,
    )


def sds(shape, dtype):
    return jax.ShapeDtypeStruct(shape, dtype)


def token_row(piece_row):
    return (piece_row % C) * SPAN + ((piece_row // C) % U) * TB + piece_row // (U * C)


def prep_body(q_ref, g_ref, digits_ref, out_ref):
    size = C * SPAN
    order = hot(iota((size, size), 1) == token_row(iota((size, size), 0)))
    for base, ref in ((0, q_ref), (U * C, g_ref)):
        rows = mm(order, ref[...]).astype(BF)
        for h in range(H):
            out_ref[h * TB : (h + 1) * TB, base : base + U * C, :] = rows[
                :, h * HD : (h + 1) * HD
            ].reshape(TB, U * C, HD)
    out_ref[:, 2 * U * C :, :] = jnp.broadcast_to(digits_ref[...][None], (N, C, HD))


def final_body(in_ref, att_ref, qg_ref):
    size = C * SPAN
    order = hot(iota((size, size), 0) == token_row(iota((size, size), 1)))
    for base, ref in ((0, att_ref), (U * C, qg_ref)):
        cat = jnp.concatenate(
            [
                in_ref[h * TB : (h + 1) * TB, base : base + U * C, :].reshape(size, HD)
                for h in range(H)
            ],
            axis=1,
        )
        ref[...] = mm(order, cat).astype(BF)


def span_rows(block):
    wide = block.astype(F32)
    return [wide[:, u * C : (u + 1) * C, :].reshape(SPANS, HD) for u in range(U)]


def route_body(base, first_ref, out_ref, row_ref, col_ref, x_ref):
    digits = first_ref[:, 2 * U * C :, :].astype(F32).reshape(SPANS, HD)
    lane = iota((SPANS, HD), 1)
    slot_part = pltpu.roll(digits, HD - 2, 1)
    cols = jnp.where(lane < 2, digits * float(S) + slot_part, 0.0)
    cols = cols + jnp.where((lane >= 2) & (lane < 6), pltpu.roll(digits, 2, 1), 0.0)
    col_ref[...] = cols
    rows = jnp.transpose(cols)[:8]
    row_ref[...] = rows
    for u, part in enumerate(span_rows(first_ref[:, base : base + U * C, :])):
        x_ref[:, u * HD : (u + 1) * HD] = part.astype(BF)
    per = 8
    slot_a = rows[0:1]
    slot_b = rows[1:2]

    def step(j, _):
        ids = (iota((per * S, SPANS), 0) + j * (per * S)).astype(F32)
        hit = hot((ids == slot_a) | (ids == slot_b))
        got = mm(hit, x_ref[...]).astype(BF)
        at = pl.ds(pl.multiple_of(j * per, per), per)
        for u in range(U):
            out_ref[at, u * S : (u + 1) * S, :] = got[:, u * HD : (u + 1) * HD].reshape(
                per, S, HD
            )
        return 0

    lax.fori_loop(0, N // per, step, 0)


def swap_order():
    size = TB * HALF
    a, b = iota((size, size), 0), iota((size, size), 1)
    return hot((a // TB == b % TB) & (a % TB == b // TB))


def to_slots(order, src_ref, dst_ref):
    for h in range(H):
        pair, i = h // 2, h % 2
        for u in range(0, U, 2):
            block = jnp.concatenate(
                [
                    src_ref[h * TB : (h + 1) * TB, v, :, :].reshape(TB * HALF, HD)
                    for v in (u, u + 1)
                ],
                axis=1,
            )
            rows = mm(order, block).astype(BF)
            for j in range(2):
                lo = i * SPAN + (u + j) * TB
                dst_ref[:, pair, lo : lo + TB, i * HD : (i + 1) * HD] = rows[
                    :, j * HD : (j + 1) * HD
                ].reshape(HALF, TB, HD)


def forward_body(
    q_ref, nb_ref, rs_ref, e_ref, k_ref, v_ref, p_ref, b_ref, stat_ref, qs, pbs, tops, totals
):
    step = pl.program_id(0)
    order = swap_order()

    @pl.when(step == 0)
    def _():
        tops[...] = jnp.zeros_like(tops)
        totals[...] = jnp.zeros_like(totals)
        qs[...] = jnp.zeros_like(qs)

    to_slots(order, q_ref, qs)
    row = iota((2 * SPAN, HD), 0) % SPAN

    def slot(s, _):
        at = step * HALF + s
        scale = jnp.sum(
            jnp.where(iota((R, HD), 1) == at, rs_ref[...], 0.0), axis=1, keepdims=True
        )
        mark = iota((2 * SPAN, HD), 1) == (row // TB) * S + at
        for pair in range(H // 2):
            lo = 4 * pair * HD
            part = [
                nb_ref[s, :, lo + i * HD : lo + (i + 1) * HD].astype(F32) * scale
                for i in range(4)
            ]
            keys = [part[0].astype(BF), part[2].astype(BF)]
            key2 = jnp.concatenate(keys, axis=1)
            q2 = qs[s, pair]
            scores = mm_t(q2, key2) * SCALE
            split = scores.reshape(2, SPAN, R)
            cond = jnp.exp(split - jnp.max(split, axis=1, keepdims=True))
            cond = cond / jnp.sum(cond, axis=1, keepdims=True)
            cond = t_mm(cond.reshape(2 * SPAN, R).astype(BF), q2)
            values = [
                (part[2 * i + 1] + cond[:, i * HD : (i + 1) * HD]).astype(BF) for i in range(2)
            ]
            top = jnp.max(scores, axis=1, keepdims=True).astype(BF).astype(F32)
            expo = jnp.exp(scores - top)
            total = jnp.sum(expo, axis=1, keepdims=True)
            low = expo.astype(BF)
            e_ref[s, pair] = expo
            k_ref[s, pair] = key2
            v_ref[s, pair] = jnp.concatenate(values, axis=1)
            for i in range(2):
                pbs[s, 2 * pair + i] = mm(
                    low[i * SPAN : (i + 1) * SPAN], jnp.concatenate([values[i], keys[i]], axis=1)
                ).astype(BF)
            tops[pair] = jnp.where(mark, top, tops[pair])
            totals[pair] = jnp.where(mark, total, totals[pair])
        return 0

    lax.fori_loop(0, HALF, slot, 0, unroll=2)
    for h in range(H):
        for u in range(U):
            block = pbs[:, h, u * TB : (u + 1) * TB, :].reshape(HALF * TB, 2 * HD)
            rows = mm(order, block).astype(BF)
            for i, dst_ref in enumerate((p_ref, b_ref)):
                dst_ref[h * TB : (h + 1) * TB, u, :, :] = rows[
                    :, i * HD : (i + 1) * HD
                ].reshape(TB, HALF, HD)

    @pl.when(step == 1)
    def _():
        for h in range(H):
            lo = (h % 2) * SPAN
            for i, acc in enumerate((tops, totals)):
                rows = acc[h // 2, lo : lo + TB]
                for u in range(1, U):
                    rows = rows + acc[h // 2, lo + u * TB : lo + (u + 1) * TB]
                stat_ref[i, h * TB : (h + 1) * TB, :] = rows.astype(BF)


def backward_body(g_ref, e_ref, k_ref, v_ref, a_ref, gs, as_):
    order = swap_order()

    @pl.when(pl.program_id(0) == 0)
    def _():
        gs[...] = jnp.zeros_like(gs)

    to_slots(order, g_ref, gs)

    def slot(s, _):
        for pair in range(H // 2):
            grad = mm_t(gs[s, pair], v_ref[s, pair])
            both = mm((e_ref[s, pair] * grad).astype(BF), k_ref[s, pair]).astype(BF)
            for i in range(2):
                as_[s, 2 * pair + i] = both[i * SPAN : (i + 1) * SPAN, i * HD : (i + 1) * HD]
        return 0

    lax.fori_loop(0, HALF, slot, 0, unroll=2)
    for h in range(H):
        for u in range(0, U, 2):
            block = jnp.concatenate(
                [
                    as_[:, h, v * TB : (v + 1) * TB, :].reshape(HALF * TB, HD)
                    for v in (u, u + 1)
                ],
                axis=1,
            )
            rows = mm(order, block).astype(BF)
            for j in range(2):
                a_ref[h * TB : (h + 1) * TB, u + j, :, :] = rows[
                    :, j * HD : (j + 1) * HD
                ].reshape(TB, HALF, HD)


def choose_rows(in_ref, picks, out_refs, cat_ref):
    for u in range(U):
        cat_ref[:, u * HD : (u + 1) * HD] = in_ref[:, u * S : (u + 1) * S, :].reshape(SLOTS, HD)
    size = 128
    for cols, out_ref in zip(picks, out_refs):

        def step(i, _, cols=cols, out_ref=out_ref):
            at = pl.ds(pl.multiple_of(i * size, size), size)
            ids = iota((size, SLOTS), 1).astype(F32)
            mask = ids == cols[0][at, :]
            for col in cols[1:]:
                mask = mask | (ids == col[at, :])
            out_ref[at, :] = mm(hot(mask), cat_ref[...])
            return 0

        lax.fori_loop(0, SPANS // size, step, 0)


def combine_body(back_ref, first_ref, row_ref, col_ref, att_ref, wd_ref, cat, pa, pb, ca, cb):
    cols = col_ref[...]
    ca[...] = cols[:, 0:1]
    cb[...] = cols[:, 1:2]
    choose_rows(back_ref, ((ca,), (cb,)), (pa, pb), cat)
    lane = iota((SPANS, HD), 1)
    group = hot(iota((HD, HD), 0) // S == iota((HD, HD), 1))
    ungroup = hot(iota((HD, HD), 0) == iota((HD, HD), 1) // S)
    wide = hot(iota((HD, W), 0) == iota((HD, W), 1) // HD)
    stats = back_ref[:, U * S :, :].astype(F32).reshape(N * C, HD).astype(BF)

    def owner_stat(n, which):
        at = cols[:, 2 + n : 3 + n] * float(C) + float(which)
        rows = mm(hot(iota((SPANS, N * C), 1).astype(F32) == at), stats)
        rows = jnp.where((lane % S).astype(F32) == cols[:, 4 + n : 5 + n], rows, 0.0)
        return mm(rows.astype(BF), group)

    tops = [owner_stat(n, 0) for n in range(2)]
    totals = [owner_stat(n, 1) + jnp.where(lane >= U, 1.0, 0.0) for n in range(2)]
    highest = jnp.maximum(tops[0], tops[1])
    factor = [jnp.exp(t - highest) for t in tops]
    denominator = factor[0] * totals[0] + factor[1] * totals[1]
    low = [(f / denominator).astype(BF) for f in factor]
    attended = mm(low[0], wide) * pa[...] + mm(low[1], wide) * pb[...]
    grads = span_rows(first_ref[:, U * C : 2 * U * C, :])
    delta = jnp.zeros((SPANS, HD), F32)
    for u in range(U):
        part = jnp.sum(grads[u] * attended[:, u * HD : (u + 1) * HD], axis=1, keepdims=True)
        delta = jnp.where(lane == u, part, delta)
    delta = delta.astype(BF)
    for u in range(0, U, 2):
        att_ref[:, u * C : (u + 2) * C, :] = jnp.concatenate(
            [
                attended[:, v * HD : (v + 1) * HD].reshape(N, C, HD)
                for v in (u, u + 1)
            ],
            axis=1,
        ).astype(BF)

    sent = []
    for values in (low, [delta, delta]):
        rows = jnp.zeros((N, HD), F32)
        for n in range(2):
            spread = mm(values[n], ungroup)
            spread = jnp.where((lane % S).astype(F32) == cols[:, 4 + n : 5 + n], spread, 0.0)
            owners = hot(iota((N, SPANS), 0).astype(F32) == row_ref[2 + n : 3 + n, :])
            rows = rows + mm(owners, spread.astype(BF))
        sent.append(rows[:, None, :])
    place = iota((N, C, HD), 1)
    wd_ref[...] = jnp.where(
        place == 0, sent[0], jnp.where(place == 1, sent[1], 0.0)
    ).astype(BF)


def scale_body(wd_ref, a_ref, b_ref, out_ref):
    count = wd_ref.shape[0]
    flat = wd_ref[...].astype(F32).reshape(count * C, HD)
    cols = jnp.transpose(flat)
    for k in range(count):
        w = cols[:, k * C : k * C + 1]
        delta = cols[:, k * C + 1 : k * C + 2]
        out_ref[k] = (
            w * (a_ref[k].astype(F32) - delta * b_ref[k].astype(F32)) * SCALE
        ).astype(BF)


def sum_body(terms_ref, att_ref, col_ref, out_ref, cat, acc, ca, cb):
    cols = col_ref[...]
    ca[...] = cols[:, 0:1]
    cb[...] = cols[:, 1:2]
    choose_rows(terms_ref, ((ca, cb),), (acc,), cat)
    out_ref[:, : U * C, :] = att_ref[...]
    for u in range(0, U, 2):
        base = U * C + u * C
        out_ref[:, base : base + 2 * C, :] = jnp.concatenate(
            [acc[:, v * HD : (v + 1) * HD].reshape(N, C, HD) for v in (u, u + 1)], axis=1
        ).astype(BF)


def swap(rows):
    return lax.all_to_all(rows, "seq", split_axis=0, concat_axis=0, tiled=True)


def route(first, base):
    return call(
        functools.partial(route_body, base),
        (sds((N, U * S, HD), BF), sds((8, SPANS), F32), sds((SPANS, HD), F32)),
        scratch_shapes=[pltpu.VMEM((SPANS, W), BF)],
        flops=1.1e9,
    )(first)


def local(queries, out_grad, neighbours, placement):
    owner, place = placement // S, placement % S
    digits = jnp.concatenate([owner, place], axis=1).astype(BF)
    digits = jnp.pad(digits, ((0, 0), (0, HD - 4)))
    rows_in = 2 * U * C + C
    first = swap(
        call(prep_body, sds((N, rows_in, HD), BF), flops=5e8)(queries, out_grad, digits)
    )
    square_sums = jnp.sum(jnp.square(neighbours.astype(F32)), axis=-1)
    row_scale = lax.rsqrt(lax.psum(square_sums, "head") / D + 1e-06)
    row_scale = jnp.pad(row_scale.T, ((0, 0), (0, HD - S)))

    first, row_scale = lax.optimization_barrier((first, row_scale))
    q_send, rowv, colv = route(first, 0)
    got_q = swap(q_send)
    g_send = route(first, U * C)[0]
    g_send, got_q = lax.optimization_barrier((g_send, got_q))
    got_g = swap(g_send)

    def cut(rows):
        return rows.reshape(N, U, S, HD)

    half_piece = pl.BlockSpec((N, U, HALF, HD), lambda i: (0, 0, i, 0))
    by_slot = lambda *tail: pl.BlockSpec((HALF, H // 2) + tail, lambda i: (i, 0, 0, 0))
    whole = lambda *shape: pl.BlockSpec(shape, lambda i: (0,) * len(shape))
    diagonal = pltpu.VMEM((HALF, H // 2, 2 * SPAN, 2 * HD), BF)
    stat_acc = pltpu.VMEM((H // 2, 2 * SPAN, HD), F32)
    expo, keys, values, p_send, b_rows, stats = call(
        forward_body,
        (
            sds((S, H // 2, 2 * SPAN, R), F32),
            sds((S, H // 2, R, 2 * HD), BF),
            sds((S, H // 2, R, 2 * HD), BF),
            sds((N, U, S, HD), BF),
            sds((N, U, S, HD), BF),
            sds((2, N, HD), BF),
        ),
        grid=(2,),
        in_specs=[
            half_piece,
            pl.BlockSpec((HALF, R, 2 * H * HD), lambda i: (i, 0, 0)),
            whole(R, HD),
        ],
        out_specs=(
            by_slot(2 * SPAN, R),
            by_slot(R, 2 * HD),
            by_slot(R, 2 * HD),
            half_piece,
            half_piece,
            whole(2, N, HD),
        ),
        scratch_shapes=[
            diagonal,
            pltpu.VMEM((HALF, H, SPAN, 2 * HD), BF),
            stat_acc,
            stat_acc,
        ],
        flops=2e9,
        nbytes=3e7,
        vmem=56,
    )(cut(got_q), neighbours, row_scale)
    stats = jnp.pad(jnp.transpose(stats, (1, 0, 2)), ((0, 0), (0, C - 2), (0, 0)))
    back_send = jnp.concatenate([p_send.reshape(N, U * S, HD), stats], axis=1)
    back_send, got_g = lax.optimization_barrier((back_send, got_g))
    back = swap(back_send)
    a_rows = call(
        backward_body,
        sds((N, U, S, HD), BF),
        grid=(2,),
        in_specs=[half_piece, by_slot(2 * SPAN, R), by_slot(R, 2 * HD), by_slot(R, 2 * HD)],
        out_specs=half_piece,
        scratch_shapes=[diagonal, pltpu.VMEM((HALF, H, SPAN, HD), BF)],
        flops=1e9,
        nbytes=2e7,
        vmem=48,
    )(cut(got_g), expo, keys, values)

    back, a_rows = lax.optimization_barrier((back, a_rows))
    span_table = pltpu.VMEM((SPANS, W), F32)
    column = pltpu.VMEM((SPANS, 1), F32)
    cat = pltpu.VMEM((SLOTS, W), BF)
    attended, wd_send = call(
        combine_body,
        (sds((N, U * C, HD), BF), sds((N, C, HD), BF)),
        scratch_shapes=[cat, span_table, span_table, column, column],
        flops=2.2e9,
        vmem=48,
    )(back, first, rowv, colv)
    wd = swap(wd_send)
    group = 16
    k_block = lambda rows: pl.BlockSpec((group, rows, HD), lambda i: (i, 0, 0))
    terms = call(
        scale_body,
        sds((N, U * S, HD), BF),
        grid=(N // group,),
        in_specs=[k_block(C), k_block(U * S), k_block(U * S)],
        out_specs=k_block(U * S),
    )(wd, a_rows.reshape(N, U * S, HD), b_rows.reshape(N, U * S, HD))
    last = call(
        sum_body,
        sds((N, 2 * U * C, HD), BF),
        scratch_shapes=[cat, span_table, column, column],
        flops=1.1e9,
        vmem=48,
    )(swap(terms), attended, colv)
    return call(
        final_body, (sds(queries.shape, BF), sds(queries.shape, BF)), flops=5e8
    )(swap(last))


def solution(mesh):
    in_specs = (P("seq", "head"), P("seq", "head"), P("seq", None, "head"), P("seq", None))
    out_specs = (P("seq", "head"), P("seq", "head"))
    return jax.shard_map(local, mesh=mesh, in_specs=in_specs, out_specs=out_specs, check_vma=False)
```

```python
import functools
import math

import jax
import jax.numpy as jnp
from jax import lax
from jax.experimental import pallas as pl
from jax.experimental.pallas import tpu as pltpu
from jax.sharding import PartitionSpec as P

D = 4096
HD = 128
SPAN = 64
R = 128
N = 64
C = 8
S = 32
H = 4
U = 4
TB = SPAN // U
W = U * HD
SPANS = N * C
SLOTS = N * S
HALF = S // 2
SCALE = 1.0 / math.sqrt(HD)
BF = jnp.bfloat16
F32 = jnp.float32
MIB = 1 << 20


def iota(shape, dim):
    return lax.broadcasted_iota(jnp.int32, shape, dim)


def hot(mask):
    return jnp.where(mask, 1.0, 0.0).astype(BF)


def mm(a, b):
    return jnp.dot(a, b, preferred_element_type=F32)


def mm_t(a, b):
    return lax.dot_general(a, b, (((1,), (1,)), ((), ())), preferred_element_type=F32)


def t_mm(a, b):
    return lax.dot_general(a, b, (((0,), (0,)), ((), ())), preferred_element_type=F32)


def call(body, out_shape, flops=1e8, nbytes=4e6, vmem=20, **kw):
    return pl.pallas_call(
        body,
        out_shape=out_shape,
        compiler_params=pltpu.CompilerParams(vmem_limit_bytes=vmem * MIB),
        cost_estimate=pl.CostEstimate(
            flops=int(flops), bytes_accessed=int(nbytes), transcendentals=0
        ),
        **kw,
    )


def sds(shape, dtype):
    return jax.ShapeDtypeStruct(shape, dtype)


def token_row(piece_row):
    return (piece_row % C) * SPAN + ((piece_row // C) % U) * TB + piece_row // (U * C)


def prep_body(q_ref, g_ref, digits_ref, out_ref):
    size = C * SPAN
    order = hot(iota((size, size), 1) == token_row(iota((size, size), 0)))
    for base, ref in ((0, q_ref), (U * C, g_ref)):
        rows = mm(order, ref[...]).astype(BF)
        for h in range(H):
            out_ref[h * TB : (h + 1) * TB, base : base + U * C, :] = rows[
                :, h * HD : (h + 1) * HD
            ].reshape(TB, U * C, HD)
    out_ref[:, 2 * U * C :, :] = jnp.broadcast_to(digits_ref[...][None], (N, C, HD))


def final_body(in_ref, att_ref, qg_ref):
    size = C * SPAN
    order = hot(iota((size, size), 0) == token_row(iota((size, size), 1)))
    for base, ref in ((0, att_ref), (U * C, qg_ref)):
        cat = jnp.concatenate(
            [
                in_ref[h * TB : (h + 1) * TB, base : base + U * C, :].reshape(size, HD)
                for h in range(H)
            ],
            axis=1,
        )
        ref[...] = mm(order, cat).astype(BF)


def span_rows(block):
    wide = block.astype(F32)
    return [wide[:, u * C : (u + 1) * C, :].reshape(SPANS, HD) for u in range(U)]


def route_body(base, first_ref, out_ref, row_ref, col_ref, x_ref):
    digits = first_ref[:, 2 * U * C :, :].astype(F32).reshape(SPANS, HD)
    lane = iota((SPANS, HD), 1)
    slot_part = pltpu.roll(digits, HD - 2, 1)
    cols = jnp.where(lane < 2, digits * float(S) + slot_part, 0.0)
    cols = cols + jnp.where((lane >= 2) & (lane < 6), pltpu.roll(digits, 2, 1), 0.0)
    col_ref[...] = cols
    rows = jnp.transpose(cols)[:8]
    row_ref[...] = rows
    for u, part in enumerate(span_rows(first_ref[:, base : base + U * C, :])):
        x_ref[:, u * HD : (u + 1) * HD] = part.astype(BF)
    per = 8
    slot_a = rows[0:1]
    slot_b = rows[1:2]

    def step(j, _):
        ids = (iota((per * S, SPANS), 0) + j * (per * S)).astype(F32)
        hit = hot((ids == slot_a) | (ids == slot_b))
        got = mm(hit, x_ref[...]).astype(BF)
        at = pl.ds(pl.multiple_of(j * per, per), per)
        for u in range(U):
            out_ref[at, u * S : (u + 1) * S, :] = got[:, u * HD : (u + 1) * HD].reshape(
                per, S, HD
            )
        return 0

    lax.fori_loop(0, N // per, step, 0)


def swap_order():
    size = TB * HALF
    a, b = iota((size, size), 0), iota((size, size), 1)
    return hot((a // TB == b % TB) & (a % TB == b // TB))


def to_slots(order, src_ref, dst_ref):
    for h in range(H):
        pair, i = h // 2, h % 2
        for u in range(0, U, 2):
            block = jnp.concatenate(
                [
                    src_ref[h * TB : (h + 1) * TB, v, :, :].reshape(TB * HALF, HD)
                    for v in (u, u + 1)
                ],
                axis=1,
            )
            rows = mm(order, block).astype(BF)
            for j in range(2):
                lo = i * SPAN + (u + j) * TB
                dst_ref[:, pair, lo : lo + TB, i * HD : (i + 1) * HD] = rows[
                    :, j * HD : (j + 1) * HD
                ].reshape(HALF, TB, HD)


def forward_body(
    q_ref, nb_ref, rs_ref, e_ref, k_ref, v_ref, p_ref, b_ref, stat_ref, qs, pbs, tops, totals
):
    step = pl.program_id(0)
    order = swap_order()

    @pl.when(step == 0)
    def _():
        tops[...] = jnp.zeros_like(tops)
        totals[...] = jnp.zeros_like(totals)
        qs[...] = jnp.zeros_like(qs)

    to_slots(order, q_ref, qs)
    row = iota((2 * SPAN, HD), 0) % SPAN

    def slot(s, _):
        at = step * HALF + s
        scale = jnp.sum(
            jnp.where(iota((R, HD), 1) == at, rs_ref[...], 0.0), axis=1, keepdims=True
        )
        mark = iota((2 * SPAN, HD), 1) == (row // TB) * S + at
        for pair in range(H // 2):
            lo = 4 * pair * HD
            part = [
                nb_ref[s, :, lo + i * HD : lo + (i + 1) * HD].astype(F32) * scale
                for i in range(4)
            ]
            keys = [part[0].astype(BF), part[2].astype(BF)]
            key2 = jnp.concatenate(keys, axis=1)
            q2 = qs[s, pair]
            scores = mm_t(q2, key2) * SCALE
            split = scores.reshape(2, SPAN, R)
            cond = jnp.exp(split - jnp.max(split, axis=1, keepdims=True))
            cond = cond / jnp.sum(cond, axis=1, keepdims=True)
            cond = t_mm(cond.reshape(2 * SPAN, R).astype(BF), q2)
            values = [
                (part[2 * i + 1] + cond[:, i * HD : (i + 1) * HD]).astype(BF) for i in range(2)
            ]
            top = jnp.max(scores, axis=1, keepdims=True).astype(BF).astype(F32)
            expo = jnp.exp(scores - top)
            total = jnp.sum(expo, axis=1, keepdims=True)
            low = expo.astype(BF)
            e_ref[s, pair] = expo
            k_ref[s, pair] = key2
            v_ref[s, pair] = jnp.concatenate(values, axis=1)
            for i in range(2):
                pbs[s, 2 * pair + i] = mm(
                    low[i * SPAN : (i + 1) * SPAN], jnp.concatenate([values[i], keys[i]], axis=1)
                ).astype(BF)
            tops[pair] = jnp.where(mark, top, tops[pair])
            totals[pair] = jnp.where(mark, total, totals[pair])
        return 0

    lax.fori_loop(0, HALF, slot, 0, unroll=2)
    for h in range(H):
        for u in range(U):
            block = pbs[:, h, u * TB : (u + 1) * TB, :].reshape(HALF * TB, 2 * HD)
            rows = mm(order, block).astype(BF)
            for i, dst_ref in enumerate((p_ref, b_ref)):
                dst_ref[h * TB : (h + 1) * TB, u, :, :] = rows[
                    :, i * HD : (i + 1) * HD
                ].reshape(TB, HALF, HD)

    @pl.when(step == 1)
    def _():
        for h in range(H):
            lo = (h % 2) * SPAN
            for i, acc in enumerate((tops, totals)):
                rows = acc[h // 2, lo : lo + TB]
                for u in range(1, U):
                    rows = rows + acc[h // 2, lo + u * TB : lo + (u + 1) * TB]
                stat_ref[i, h * TB : (h + 1) * TB, :] = rows.astype(BF)


def backward_body(g_ref, e_ref, k_ref, v_ref, a_ref, gs, as_):
    order = swap_order()

    @pl.when(pl.program_id(0) == 0)
    def _():
        gs[...] = jnp.zeros_like(gs)

    to_slots(order, g_ref, gs)

    def slot(s, _):
        for pair in range(H // 2):
            grad = mm_t(gs[s, pair], v_ref[s, pair])
            both = mm((e_ref[s, pair] * grad).astype(BF), k_ref[s, pair]).astype(BF)
            for i in range(2):
                as_[s, 2 * pair + i] = both[i * SPAN : (i + 1) * SPAN, i * HD : (i + 1) * HD]
        return 0

    lax.fori_loop(0, HALF, slot, 0, unroll=2)
    for h in range(H):
        for u in range(0, U, 2):
            block = jnp.concatenate(
                [
                    as_[:, h, v * TB : (v + 1) * TB, :].reshape(HALF * TB, HD)
                    for v in (u, u + 1)
                ],
                axis=1,
            )
            rows = mm(order, block).astype(BF)
            for j in range(2):
                a_ref[h * TB : (h + 1) * TB, u + j, :, :] = rows[
                    :, j * HD : (j + 1) * HD
                ].reshape(TB, HALF, HD)


def choose_rows(in_ref, picks, out_refs, cat_ref):
    for u in range(U):
        cat_ref[:, u * HD : (u + 1) * HD] = in_ref[:, u * S : (u + 1) * S, :].reshape(SLOTS, HD)
    size = 128
    for cols, out_ref in zip(picks, out_refs):

        def step(i, _, cols=cols, out_ref=out_ref):
            at = pl.ds(pl.multiple_of(i * size, size), size)
            ids = iota((size, SLOTS), 1).astype(F32)
            mask = ids == cols[0][at, :]
            for col in cols[1:]:
                mask = mask | (ids == col[at, :])
            out_ref[at, :] = mm(hot(mask), cat_ref[...])
            return 0

        lax.fori_loop(0, SPANS // size, step, 0)


def product_body(back_ref, g_ref, out_ref):
    ones = jnp.ones((C, HD), BF)
    for k in range(back_ref.shape[0]):
        prod = back_ref[k, : U * S, :].astype(F32) * g_ref[k].astype(F32)
        high = prod.astype(BF)
        rest = (prod - high.astype(F32)).astype(BF)
        rows = mm_t(ones, high) + mm_t(ones, rest)
        part = rows.astype(BF).astype(F32)
        stats = back_ref[k, U * S :, :].astype(F32)
        row = iota((C, HD), 0)
        out_ref[k] = jnp.where(row == 2, part, jnp.where(row == 3, rows - part, stats)).astype(BF)


def weight_body(stat_ref, row_ref, col_ref, wd_ref, wts_ref, flat):
    cols = col_ref[...]
    lane = iota((SPANS, HD), 1)
    flat[...] = stat_ref[...].astype(F32).reshape(N * C, HD)
    stats = jnp.concatenate(
        [flat[pl.ds(i, N, stride=C), :].astype(BF) for i in range(4)], axis=1
    )
    row, col = iota((4 * HD, HD), 0), iota((4 * HD, HD), 1)
    stat = jnp.minimum(row // HD, 2)
    group = hot(stat * U + row % HD // S == col)
    slot_lane = (iota((SPANS, 4 * HD), 1) % S).astype(F32)
    tops, totals, products = [], [], []
    for n in range(2):
        owner = hot(iota((SPANS, N), 1).astype(F32) == cols[:, 2 + n : 3 + n])
        rows = mm(owner, stats)
        rows = jnp.where(slot_lane == cols[:, 4 + n : 5 + n], rows, 0.0).astype(BF)
        rows = mm(rows, group)
        tops.append(rows)
        totals.append(pltpu.roll(rows, HD - U, 1))
        products.append(pltpu.roll(rows, HD - 2 * U, 1))
    highest = jnp.maximum(tops[0], tops[1])
    factor = [jnp.exp(t - highest) for t in tops]
    denominator = factor[0] * totals[0] + factor[1] * totals[1]
    low = [jnp.where(lane < U, f / denominator, 0.0).astype(BF).astype(F32) for f in factor]
    delta = jnp.where(lane < U, low[0] * products[0] + low[1] * products[1], 0.0)
    wts_ref[...] = (low[0] + pltpu.roll(low[1], U, 1)).astype(BF)
    delta = pltpu.roll(delta, U, 1)
    spread = hot(iota((HD, 2 * HD), 0) == iota((HD, 2 * HD), 1) // S)
    out = jnp.zeros((N, 2 * HD), F32)
    for n in range(2):
        rows = mm((low[n] + delta).astype(BF), spread)
        rows = jnp.where(slot_lane[:, : 2 * HD] == cols[:, 4 + n : 5 + n], rows, 0.0)
        owners = hot(iota((N, SPANS), 0).astype(F32) == row_ref[2 + n : 3 + n, :])
        out = out + mm(owners, rows.astype(BF))
    place = iota((N, 2, HD), 1)
    wd_ref[...] = jnp.where(place == 0, out[:, None, :HD], out[:, None, HD:]).astype(BF)


def attended_body(back_ref, col_ref, wts_ref, att_ref, cat, pa, pb, ca, cb):
    cols = col_ref[...]
    ca[...] = cols[:, 0:1]
    cb[...] = cols[:, 1:2]
    choose_rows(back_ref, ((ca,), (cb,)), (pa, pb), cat)
    wide = hot(iota((HD, 2 * W), 0) == iota((HD, 2 * W), 1) // HD)
    weight = mm(wts_ref[...], wide)
    attended = weight[:, :W] * pa[...] + weight[:, W:] * pb[...]
    for u in range(0, U, 2):
        att_ref[:, u * C : (u + 2) * C, :] = jnp.concatenate(
            [
                attended[:, v * HD : (v + 1) * HD].reshape(N, C, HD)
                for v in (u, u + 1)
            ],
            axis=1,
        ).astype(BF)


def scale_body(wd_ref, a_ref, b_ref, out_ref):
    count = wd_ref.shape[0]
    flat = wd_ref[...].astype(F32).reshape(2 * count, HD)
    cols = jnp.transpose(flat)
    for k in range(count):
        w = cols[:, 2 * k : 2 * k + 1]
        delta = cols[:, 2 * k + 1 : 2 * k + 2]
        out_ref[k] = (
            w * (a_ref[k].astype(F32) - delta * b_ref[k].astype(F32)) * SCALE
        ).astype(BF)


def sum_body(terms_ref, att_ref, col_ref, out_ref, cat, acc, ca, cb):
    cols = col_ref[...]
    ca[...] = cols[:, 0:1]
    cb[...] = cols[:, 1:2]
    choose_rows(terms_ref, ((ca, cb),), (acc,), cat)
    out_ref[:, : U * C, :] = att_ref[...]
    for u in range(0, U, 2):
        base = U * C + u * C
        out_ref[:, base : base + 2 * C, :] = jnp.concatenate(
            [acc[:, v * HD : (v + 1) * HD].reshape(N, C, HD) for v in (u, u + 1)], axis=1
        ).astype(BF)


def swap(rows):
    return lax.all_to_all(rows, "seq", split_axis=0, concat_axis=0, tiled=True)


def route(first, base):
    return call(
        functools.partial(route_body, base),
        (sds((N, U * S, HD), BF), sds((8, SPANS), F32), sds((SPANS, HD), F32)),
        scratch_shapes=[pltpu.VMEM((SPANS, W), BF)],
        flops=1.1e9,
    )(first)


def local(queries, out_grad, neighbours, placement):
    owner, place = placement // S, placement % S
    digits = jnp.concatenate([owner, place], axis=1).astype(BF)
    digits = jnp.pad(digits, ((0, 0), (0, HD - 4)))
    rows_in = 2 * U * C + C
    first = swap(
        call(prep_body, sds((N, rows_in, HD), BF), flops=5e8)(queries, out_grad, digits)
    )
    square_sums = jnp.sum(jnp.square(neighbours.astype(F32)), axis=-1)
    row_scale = lax.rsqrt(lax.psum(square_sums, "head") / D + 1e-06)
    row_scale = jnp.pad(row_scale.T, ((0, 0), (0, HD - S)))

    first, row_scale = lax.optimization_barrier((first, row_scale))
    q_send, rowv, colv = route(first, 0)
    got_q = swap(q_send)
    g_send = route(first, U * C)[0]
    g_send, got_q = lax.optimization_barrier((g_send, got_q))
    got_g = swap(g_send)

    def cut(rows):
        return rows.reshape(N, U, S, HD)

    half_piece = pl.BlockSpec((N, U, HALF, HD), lambda i: (0, 0, i, 0))
    by_slot = lambda *tail: pl.BlockSpec((HALF, H // 2) + tail, lambda i: (i, 0, 0, 0))
    whole = lambda *shape: pl.BlockSpec(shape, lambda i: (0,) * len(shape))
    diagonal = pltpu.VMEM((HALF, H // 2, 2 * SPAN, 2 * HD), BF)
    stat_acc = pltpu.VMEM((H // 2, 2 * SPAN, HD), F32)
    expo, keys, values, p_send, b_rows, stats = call(
        forward_body,
        (
            sds((S, H // 2, 2 * SPAN, R), F32),
            sds((S, H // 2, R, 2 * HD), BF),
            sds((S, H // 2, R, 2 * HD), BF),
            sds((N, U, S, HD), BF),
            sds((N, U, S, HD), BF),
            sds((2, N, HD), BF),
        ),
        grid=(2,),
        in_specs=[
            half_piece,
            pl.BlockSpec((HALF, R, 2 * H * HD), lambda i: (i, 0, 0)),
            whole(R, HD),
        ],
        out_specs=(
            by_slot(2 * SPAN, R),
            by_slot(R, 2 * HD),
            by_slot(R, 2 * HD),
            half_piece,
            half_piece,
            whole(2, N, HD),
        ),
        scratch_shapes=[
            diagonal,
            pltpu.VMEM((HALF, H, SPAN, 2 * HD), BF),
            stat_acc,
            stat_acc,
        ],
        flops=2e9,
        nbytes=3e7,
        vmem=36,
    )(cut(got_q), neighbours, row_scale)
    stats = jnp.pad(jnp.transpose(stats, (1, 0, 2)), ((0, 0), (0, C - 2), (0, 0)))
    back_send = jnp.concatenate([p_send.reshape(N, U * S, HD), stats], axis=1)
    group = 16
    k_block = lambda rows: pl.BlockSpec((group, rows, HD), lambda i: (i, 0, 0))
    stat_block = pl.BlockSpec((group, C, HD), lambda i: (i, U * S // C, 0))
    back_send = call(
        product_body,
        sds((N, U * S + C, HD), BF),
        grid=(N // group,),
        in_specs=[k_block(U * S + C), k_block(U * S)],
        out_specs=stat_block,
        input_output_aliases={0: 0},
        vmem=16,
    )(back_send, got_g)
    back = swap(back_send)
    a_rows = call(
        backward_body,
        sds((N, U, S, HD), BF),
        grid=(2,),
        in_specs=[half_piece, by_slot(2 * SPAN, R), by_slot(R, 2 * HD), by_slot(R, 2 * HD)],
        out_specs=half_piece,
        scratch_shapes=[diagonal, pltpu.VMEM((HALF, H, SPAN, HD), BF)],
        flops=1e9,
        nbytes=2e7,
        vmem=26,
    )(cut(got_g), expo, keys, values)

    back, a_rows = lax.optimization_barrier((back, a_rows))
    span_table = pltpu.VMEM((SPANS, W), F32)
    column = pltpu.VMEM((SPANS, 1), F32)
    cat = pltpu.VMEM((SLOTS, W), BF)
    wd_send, wts = call(
        weight_body,
        (sds((N, 2, HD), BF), sds((SPANS, HD), BF)),
        grid=(1,),
        in_specs=[
            pl.BlockSpec((N, C, HD), lambda i: (0, U * S // C, 0)),
            whole(8, SPANS),
            whole(SPANS, HD),
        ],
        out_specs=(whole(N, 2, HD), whole(SPANS, HD)),
        scratch_shapes=[pltpu.VMEM((N * C, HD), F32)],
        vmem=20,
    )(back, rowv, colv)
    wd = swap(wd_send)
    attended = call(
        attended_body,
        sds((N, U * C, HD), BF),
        scratch_shapes=[cat, span_table, span_table, column, column],
        flops=2.2e9,
        vmem=24,
    )(back, colv, wts)
    terms = call(
        scale_body,
        sds((N, U * S, HD), BF),
        grid=(N // group,),
        in_specs=[pl.BlockSpec((group, 2, HD), lambda i: (i, 0, 0)), k_block(U * S), k_block(U * S)],
        out_specs=k_block(U * S),
        vmem=16,
    )(wd, a_rows.reshape(N, U * S, HD), b_rows.reshape(N, U * S, HD))
    last = call(
        sum_body,
        sds((N, 2 * U * C, HD), BF),
        scratch_shapes=[cat, span_table, column, column],
        flops=1.1e9,
        vmem=20,
    )(swap(terms), attended, colv)
    return call(
        final_body, (sds(queries.shape, BF), sds(queries.shape, BF)), flops=5e8
    )(swap(last))


def solution(mesh):
    in_specs = (P("seq", "head"), P("seq", "head"), P("seq", None, "head"), P("seq", None))
    out_specs = (P("seq", "head"), P("seq", "head"))
    return jax.shard_map(local, mesh=mesh, in_specs=in_specs, out_specs=out_specs, check_vma=False)
```

```python
import functools
import math

import jax
import jax.numpy as jnp
from jax import lax
from jax.experimental import pallas as pl
from jax.experimental.pallas import tpu as pltpu
from jax.sharding import PartitionSpec as P

D = 4096
HD = 128
SPAN = 64
R = 128
N = 64
C = 8
S = 32
H = 4
U = 4
TB = SPAN // U
W = U * HD
SPANS = N * C
SLOTS = N * S
HALF = S // 2
SCALE = 1.0 / math.sqrt(HD)
BF = jnp.bfloat16
F32 = jnp.float32
MIB = 1 << 20


def iota(shape, dim):
    return lax.broadcasted_iota(jnp.int32, shape, dim)


def hot(mask):
    return jnp.where(mask, 1.0, 0.0).astype(BF)


def mm(a, b):
    return jnp.dot(a, b, preferred_element_type=F32)


def mm_t(a, b):
    return lax.dot_general(a, b, (((1,), (1,)), ((), ())), preferred_element_type=F32)


def t_mm(a, b):
    return lax.dot_general(a, b, (((0,), (0,)), ((), ())), preferred_element_type=F32)


def call(body, out_shape, flops=1e8, nbytes=4e6, vmem=20, **kw):
    return pl.pallas_call(
        body,
        out_shape=out_shape,
        compiler_params=pltpu.CompilerParams(vmem_limit_bytes=vmem * MIB),
        cost_estimate=pl.CostEstimate(
            flops=int(flops), bytes_accessed=int(nbytes), transcendentals=0
        ),
        **kw,
    )


def sds(shape, dtype):
    return jax.ShapeDtypeStruct(shape, dtype)


def token_row(piece_row):
    return (piece_row % C) * SPAN + ((piece_row // C) % U) * TB + piece_row // (U * C)


def prep_body(q_ref, g_ref, digits_ref, out_ref, order):
    size = C * SPAN

    @pl.when(pl.program_id(0) == 0)
    def _():
        order[...] = hot(iota((size, size), 1) == token_row(iota((size, size), 0)))

    rows = mm(order[...], jnp.concatenate([q_ref[...], g_ref[...]], axis=1)).astype(BF)
    for i in range(2):
        out_ref[:, i * U * C : (i + 1) * U * C, :] = rows[:, i * HD : (i + 1) * HD].reshape(
            TB, U * C, HD
        )
    out_ref[:, 2 * U * C :, :] = jnp.broadcast_to(digits_ref[...][None], (TB, C, HD))


def final_body(in_ref, att_ref, qg_ref, order):
    size = C * SPAN

    @pl.when(pl.program_id(0) == 0)
    def _():
        order[...] = hot(iota((size, size), 0) == token_row(iota((size, size), 1)))

    both = jnp.concatenate(
        [in_ref[:, i * U * C : (i + 1) * U * C, :].reshape(size, HD) for i in range(2)], axis=1
    )
    both = mm(order[...], both).astype(BF)
    att_ref[...] = both[:, :HD]
    qg_ref[...] = both[:, HD:]


def span_rows(block):
    wide = block.astype(F32)
    return [wide[:, u * C : (u + 1) * C, :].reshape(SPANS, HD) for u in range(U)]


def route_body(base, first_ref, out_ref, row_ref, col_ref, x_ref):
    per = out_ref.shape[0]

    @pl.when(pl.program_id(0) == 0)
    def _():
        digits = first_ref[:, 2 * U * C :, :].astype(F32).reshape(SPANS, HD)
        lane = iota((SPANS, HD), 1)
        slot_part = pltpu.roll(digits, HD - 2, 1)
        cols = jnp.where(lane < 2, digits * float(S) + slot_part, 0.0)
        cols = cols + jnp.where((lane >= 2) & (lane < 6), pltpu.roll(digits, 2, 1), 0.0)
        col_ref[...] = cols
        row_ref[...] = jnp.transpose(cols)[:8]
        for u, part in enumerate(span_rows(first_ref[:, base : base + U * C, :])):
            x_ref[:, u * HD : (u + 1) * HD] = part.astype(BF)

    ids = (iota((per * S, SPANS), 0) + pl.program_id(0) * (per * S)).astype(F32)
    hit = hot((ids == row_ref[0:1, :]) | (ids == row_ref[1:2, :]))
    got = mm(hit, x_ref[...]).astype(BF)
    for u in range(U):
        out_ref[:, u * S : (u + 1) * S, :] = got[:, u * HD : (u + 1) * HD].reshape(per, S, HD)


def swap_order():
    size = TB * HALF
    a, b = iota((size, size), 0), iota((size, size), 1)
    return hot((a // TB == b % TB) & (a % TB == b // TB))


def to_slots(order, src_ref, dst_ref):
    for h in range(H):
        pair, i = h // 2, h % 2
        for u in range(0, U, 2):
            block = jnp.concatenate(
                [
                    src_ref[h * TB : (h + 1) * TB, v, :, :].reshape(TB * HALF, HD)
                    for v in (u, u + 1)
                ],
                axis=1,
            )
            rows = mm(order, block).astype(BF)
            for j in range(2):
                lo = i * SPAN + (u + j) * TB
                dst_ref[:, pair, lo : lo + TB, i * HD : (i + 1) * HD] = rows[
                    :, j * HD : (j + 1) * HD
                ].reshape(HALF, TB, HD)


def forward_body(
    q_ref, nb_ref, rs_ref, e_ref, k_ref, v_ref, pay_ref, b_ref, qs, pbs, tops, totals
):
    step = pl.program_id(0)
    order = swap_order()

    @pl.when(step == 0)
    def _():
        tops[...] = jnp.zeros_like(tops)
        totals[...] = jnp.zeros_like(totals)
        qs[...] = jnp.zeros_like(qs)

    to_slots(order, q_ref, qs)
    row = iota((2 * SPAN, HD), 0) % SPAN

    def slot(s, _):
        at = step * HALF + s
        scale = jnp.sum(
            jnp.where(iota((R, HD), 1) == at, rs_ref[...], 0.0), axis=1, keepdims=True
        )
        mark = iota((2 * SPAN, HD), 1) == (row // TB) * S + at
        for pair in range(H // 2):
            lo = 4 * pair * HD
            part = [
                nb_ref[s, :, lo + i * HD : lo + (i + 1) * HD].astype(F32) * scale
                for i in range(4)
            ]
            keys = [part[0].astype(BF), part[2].astype(BF)]
            key2 = jnp.concatenate(keys, axis=1)
            q2 = qs[s, pair]
            scores = mm_t(q2, key2) * SCALE
            split = scores.reshape(2, SPAN, R)
            cond = jnp.exp(split - jnp.max(split, axis=1, keepdims=True))
            cond = cond / jnp.sum(cond, axis=1, keepdims=True)
            cond = t_mm(cond.reshape(2 * SPAN, R).astype(BF), q2)
            values = [
                (part[2 * i + 1] + cond[:, i * HD : (i + 1) * HD]).astype(BF) for i in range(2)
            ]
            top = jnp.max(scores, axis=1, keepdims=True).astype(BF).astype(F32)
            expo = jnp.exp(scores - top)
            total = jnp.sum(expo, axis=1, keepdims=True)
            low = expo.astype(BF)
            e_ref[s, pair] = expo
            k_ref[s, pair] = key2
            v_ref[s, pair] = jnp.concatenate(values, axis=1)
            for i in range(2):
                pbs[s, 2 * pair + i] = mm(
                    low[i * SPAN : (i + 1) * SPAN], jnp.concatenate([values[i], keys[i]], axis=1)
                ).astype(BF)
            tops[pair] = jnp.where(mark, top, tops[pair])
            totals[pair] = jnp.where(mark, total, totals[pair])
        return 0

    lax.fori_loop(0, HALF, slot, 0, unroll=2)
    for h in range(H):
        for u in range(U):
            block = pbs[:, h, u * TB : (u + 1) * TB, :].reshape(HALF * TB, 2 * HD)
            rows = mm(order, block).astype(BF)
            at = pl.ds(pl.multiple_of(u * S + step * HALF, HALF), HALF)
            pay_ref[h * TB : (h + 1) * TB, at, :] = rows[:, :HD].reshape(TB, HALF, HD)
            b_ref[h * TB : (h + 1) * TB, u, :, :] = rows[:, HD:].reshape(TB, HALF, HD)

    @pl.when(step == 1)
    def _():
        place = iota((TB, C, HD), 1)
        for h in range(H):
            lo = (h % 2) * SPAN
            rows = []
            for acc in (tops, totals):
                total = acc[h // 2, lo : lo + TB]
                for u in range(1, U):
                    total = total + acc[h // 2, lo + u * TB : lo + (u + 1) * TB]
                rows.append(total[:, None, :])
            pay_ref[h * TB : (h + 1) * TB, U * S :, :] = jnp.where(
                place == 0, rows[0], jnp.where(place == 1, rows[1], 0.0)
            ).astype(BF)


def backward_body(g_ref, e_ref, k_ref, v_ref, a_ref, gs, as_):
    order = swap_order()

    @pl.when(pl.program_id(0) == 0)
    def _():
        gs[...] = jnp.zeros_like(gs)

    to_slots(order, g_ref, gs)

    def slot(s, _):
        for pair in range(H // 2):
            grad = mm_t(gs[s, pair], v_ref[s, pair])
            both = mm((e_ref[s, pair] * grad).astype(BF), k_ref[s, pair]).astype(BF)
            for i in range(2):
                as_[s, 2 * pair + i] = both[i * SPAN : (i + 1) * SPAN, i * HD : (i + 1) * HD]
        return 0

    lax.fori_loop(0, HALF, slot, 0, unroll=2)
    for h in range(H):
        for u in range(0, U, 2):
            block = jnp.concatenate(
                [
                    as_[:, h, v * TB : (v + 1) * TB, :].reshape(HALF * TB, HD)
                    for v in (u, u + 1)
                ],
                axis=1,
            )
            rows = mm(order, block).astype(BF)
            for j in range(2):
                a_ref[h * TB : (h + 1) * TB, u + j, :, :] = rows[
                    :, j * HD : (j + 1) * HD
                ].reshape(TB, HALF, HD)


def choose_rows(in_ref, picks, out_refs, cat_ref):
    for u in range(U):
        cat_ref[:, u * HD : (u + 1) * HD] = in_ref[:, u * S : (u + 1) * S, :].reshape(SLOTS, HD)
    size = 128
    for cols, out_ref in zip(picks, out_refs):

        def step(i, _, cols=cols, out_ref=out_ref):
            at = pl.ds(pl.multiple_of(i * size, size), size)
            ids = iota((size, SLOTS), 1).astype(F32)
            mask = ids == cols[0][at, :]
            for col in cols[1:]:
                mask = mask | (ids == col[at, :])
            out_ref[at, :] = mm(hot(mask), cat_ref[...])
            return 0

        lax.fori_loop(0, SPANS // size, step, 0)


def product_body(back_ref, g_ref, out_ref):
    size = U * S
    diagonal = iota((size, HD), 0) == iota((size, HD), 1)
    row = iota((C, HD), 0)
    for k in range(back_ref.shape[0]):
        prod = back_ref[k, :size, :].astype(F32) * g_ref[k].astype(F32)
        prod = jnp.where(diagonal, jnp.sum(prod, axis=1, keepdims=True), 0.0)
        rows = jnp.sum(prod, axis=0, keepdims=True)
        part = rows.astype(BF).astype(F32)
        stats = back_ref[k, size:, :].astype(F32)
        out_ref[k] = jnp.where(row == 2, part, jnp.where(row == 3, rows - part, stats)).astype(BF)


def weight_body(stat_ref, row_ref, col_ref, wd_ref, wts_ref, flat):
    cols = col_ref[...]
    lane = iota((SPANS, HD), 1)
    flat[...] = stat_ref[...].astype(F32).reshape(N * C, HD)
    stats = jnp.concatenate(
        [flat[pl.ds(i, N, stride=C), :].astype(BF) for i in range(4)], axis=1
    )
    row, col = iota((4 * HD, HD), 0), iota((4 * HD, HD), 1)
    stat = jnp.minimum(row // HD, 2)
    group = hot(stat * U + row % HD // S == col)
    slot_lane = (iota((SPANS, 4 * HD), 1) % S).astype(F32)
    tops, totals, products = [], [], []
    for n in range(2):
        owner = hot(iota((SPANS, N), 1).astype(F32) == cols[:, 2 + n : 3 + n])
        rows = mm(owner, stats)
        rows = jnp.where(slot_lane == cols[:, 4 + n : 5 + n], rows, 0.0).astype(BF)
        rows = mm(rows, group)
        tops.append(rows)
        totals.append(pltpu.roll(rows, HD - U, 1))
        products.append(pltpu.roll(rows, HD - 2 * U, 1))
    highest = jnp.maximum(tops[0], tops[1])
    factor = [jnp.exp(t - highest) for t in tops]
    denominator = factor[0] * totals[0] + factor[1] * totals[1]
    low = [jnp.where(lane < U, f / denominator, 0.0).astype(BF).astype(F32) for f in factor]
    delta = jnp.where(lane < U, low[0] * products[0] + low[1] * products[1], 0.0)
    wts_ref[...] = (low[0] + pltpu.roll(low[1], U, 1)).astype(BF)
    delta = pltpu.roll(delta, U, 1)
    spread = hot(iota((HD, 2 * HD), 0) == iota((HD, 2 * HD), 1) // S)
    out = jnp.zeros((N, 2 * HD), F32)
    for n in range(2):
        rows = mm((low[n] + delta).astype(BF), spread)
        rows = jnp.where(slot_lane[:, : 2 * HD] == cols[:, 4 + n : 5 + n], rows, 0.0)
        owners = hot(iota((N, SPANS), 0).astype(F32) == row_ref[2 + n : 3 + n, :])
        out = out + mm(owners, rows.astype(BF))
    place = iota((N, C, HD), 1)
    wd_ref[...] = jnp.where(
        place == 0, out[:, None, :HD], jnp.where(place == 1, out[:, None, HD:], 0.0)
    ).astype(BF)


def attended_body(back_ref, col_ref, wts_ref, att_ref, cat, pa, pb, ca, cb):
    cols = col_ref[...]
    ca[...] = cols[:, 0:1]
    cb[...] = cols[:, 1:2]
    choose_rows(back_ref, ((ca,), (cb,)), (pa, pb), cat)
    wide = hot(iota((HD, 2 * W), 0) == iota((HD, 2 * W), 1) // HD)
    weight = mm(wts_ref[...], wide)
    attended = weight[:, :W] * pa[...] + weight[:, W:] * pb[...]
    for u in range(0, U, 2):
        att_ref[:, u * C : (u + 2) * C, :] = jnp.concatenate(
            [
                attended[:, v * HD : (v + 1) * HD].reshape(N, C, HD)
                for v in (u, u + 1)
            ],
            axis=1,
        ).astype(BF)


def scale_body(wd_ref, a_ref, b_ref, out_ref):
    count = wd_ref.shape[0]
    flat = wd_ref[...].astype(F32).reshape(C * count, HD)
    cols = jnp.transpose(flat)
    for k in range(count):
        w = cols[:, C * k : C * k + 1]
        delta = cols[:, C * k + 1 : C * k + 2]
        out_ref[k] = (
            w * (a_ref[k].astype(F32) - delta * b_ref[k].astype(F32)) * SCALE
        ).astype(BF)


def sum_body(terms_ref, att_ref, col_ref, out_ref, cat, acc, ca, cb):
    cols = col_ref[...]
    ca[...] = cols[:, 0:1]
    cb[...] = cols[:, 1:2]
    choose_rows(terms_ref, ((ca, cb),), (acc,), cat)
    out_ref[:, : U * C, :] = att_ref[...]
    for u in range(0, U, 2):
        base = U * C + u * C
        out_ref[:, base : base + 2 * C, :] = jnp.concatenate(
            [acc[:, v * HD : (v + 1) * HD].reshape(N, C, HD) for v in (u, u + 1)], axis=1
        ).astype(BF)


def swap(rows):
    return lax.all_to_all(rows, "seq", split_axis=0, concat_axis=0, tiled=True)


def whole(*shape):
    return pl.BlockSpec(shape, lambda i: (0,) * len(shape))


def k_block(count, rows):
    return pl.BlockSpec((count, rows, HD), lambda i: (i, 0, 0))


def route(first, base):
    per = 8
    return call(
        functools.partial(route_body, base),
        (pltpu.HBM((N, U * S, HD), BF), sds((8, SPANS), F32), sds((SPANS, HD), F32)),
        grid=(N // per,),
        in_specs=[whole(*first.shape)],
        out_specs=(k_block(per, U * S), whole(8, SPANS), whole(SPANS, HD)),
        scratch_shapes=[pltpu.VMEM((SPANS, W), BF)],
        flops=1.1e9,
    )(first)


def local(queries, out_grad, neighbours, placement):
    owner, place = placement // S, placement % S
    digits = jnp.concatenate([owner, place], axis=1).astype(BF)
    digits = jnp.pad(digits, ((0, 0), (0, HD - 4)))
    rows_in = 2 * U * C + C
    order = pltpu.VMEM((C * SPAN, C * SPAN), BF)
    one_head = pl.BlockSpec((C * SPAN, HD), lambda i: (0, i))
    first = swap(
        call(
            prep_body,
            pltpu.HBM((N, rows_in, HD), BF),
            grid=(H,),
            in_specs=[one_head, one_head, whole(C, HD)],
            out_specs=k_block(TB, rows_in),
            scratch_shapes=[order],
            flops=5e8,
            vmem=60,
        )(queries, out_grad, digits)
    )
    square_sums = jnp.sum(jnp.square(neighbours.astype(F32)), axis=-1)
    row_scale = lax.rsqrt(lax.psum(square_sums, "head") / D + 1e-06)
    row_scale = jnp.pad(row_scale.T, ((0, 0), (0, HD - S)))

    first, row_scale = lax.optimization_barrier((first, row_scale))
    q_send, rowv, colv = route(first, 0)
    got_q = swap(q_send)
    g_send = route(first, U * C)[0]
    g_send, got_q = lax.optimization_barrier((g_send, got_q))
    got_g = swap(g_send)

    def cut(rows):
        return rows.reshape(N, U, S, HD)

    half_piece = pl.BlockSpec((N, U, HALF, HD), lambda i: (0, 0, i, 0))
    by_slot = lambda *tail: pl.BlockSpec((HALF, H // 2) + tail, lambda i: (i, 0, 0, 0))
    diagonal = pltpu.VMEM((HALF, H // 2, 2 * SPAN, 2 * HD), BF)
    stat_acc = pltpu.VMEM((H // 2, 2 * SPAN, HD), F32)
    expo, keys, values, back_send, b_rows = call(
        forward_body,
        (
            sds((S, H // 2, 2 * SPAN, R), F32),
            sds((S, H // 2, R, 2 * HD), BF),
            sds((S, H // 2, R, 2 * HD), BF),
            pltpu.HBM((N, U * S + C, HD), BF),
            sds((N, U, S, HD), BF),
        ),
        grid=(2,),
        in_specs=[
            half_piece,
            pl.BlockSpec((HALF, R, 2 * H * HD), lambda i: (i, 0, 0)),
            whole(R, HD),
        ],
        out_specs=(
            by_slot(2 * SPAN, R),
            by_slot(R, 2 * HD),
            by_slot(R, 2 * HD),
            whole(N, U * S + C, HD),
            half_piece,
        ),
        scratch_shapes=[
            diagonal,
            pltpu.VMEM((HALF, H, SPAN, 2 * HD), BF),
            stat_acc,
            stat_acc,
        ],
        flops=2e9,
        nbytes=3e7,
        vmem=36,
    )(cut(got_q), neighbours, row_scale)
    group = 16
    stat_block = pl.BlockSpec((group, C, HD), lambda i: (i, U * S // C, 0))
    back_send = call(
        product_body,
        pltpu.HBM((N, U * S + C, HD), BF),
        grid=(N // group,),
        in_specs=[k_block(group, U * S + C), k_block(group, U * S)],
        out_specs=stat_block,
        input_output_aliases={0: 0},
        vmem=16,
    )(back_send, got_g)
    back = swap(back_send)
    a_rows = call(
        backward_body,
        sds((N, U, S, HD), BF),
        grid=(2,),
        in_specs=[half_piece, by_slot(2 * SPAN, R), by_slot(R, 2 * HD), by_slot(R, 2 * HD)],
        out_specs=half_piece,
        scratch_shapes=[diagonal, pltpu.VMEM((HALF, H, SPAN, HD), BF)],
        flops=1e9,
        nbytes=2e7,
        vmem=26,
    )(cut(got_g), expo, keys, values)

    back, a_rows = lax.optimization_barrier((back, a_rows))
    span_table = pltpu.VMEM((SPANS, W), F32)
    column = pltpu.VMEM((SPANS, 1), F32)
    cat = pltpu.VMEM((SLOTS, W), BF)
    wd_send, wts = call(
        weight_body,
        (sds((N, C, HD), BF), sds((SPANS, HD), BF)),
        grid=(1,),
        in_specs=[
            pl.BlockSpec((N, C, HD), lambda i: (0, U * S // C, 0)),
            whole(8, SPANS),
            whole(SPANS, HD),
        ],
        out_specs=(whole(N, C, HD), whole(SPANS, HD)),
        scratch_shapes=[pltpu.VMEM((N * C, HD), F32)],
        vmem=20,
    )(back, rowv, colv)
    wd = swap(wd_send)
    attended = call(
        attended_body,
        sds((N, U * C, HD), BF),
        scratch_shapes=[cat, span_table, span_table, column, column],
        flops=2.2e9,
        vmem=24,
    )(back, colv, wts)
    terms = call(
        scale_body,
        sds((N, U * S, HD), BF),
        grid=(N // group,),
        in_specs=[k_block(group, C), k_block(group, U * S), k_block(group, U * S)],
        out_specs=k_block(group, U * S),
        vmem=60,
    )(wd, a_rows.reshape(N, U * S, HD), b_rows.reshape(N, U * S, HD))
    last = call(
        sum_body,
        sds((N, 2 * U * C, HD), BF),
        scratch_shapes=[cat, span_table, column, column],
        flops=1.1e9,
        vmem=20,
    )(swap(terms), attended, colv)
    return call(
        final_body,
        (sds(queries.shape, BF), sds(queries.shape, BF)),
        grid=(H,),
        in_specs=[k_block(TB, 2 * U * C)],
        out_specs=(one_head, one_head),
        scratch_shapes=[order],
        flops=5e8,
    )(swap(last))


def solution(mesh):
    in_specs = (P("seq", "head"), P("seq", "head"), P("seq", None, "head"), P("seq", None))
    out_specs = (P("seq", "head"), P("seq", "head"))
    return jax.shard_map(local, mesh=mesh, in_specs=in_specs, out_specs=out_specs, check_vma=False)
```

```python
import functools
import math

import jax
import jax.numpy as jnp
from jax import lax
from jax.experimental import pallas as pl
from jax.experimental.pallas import tpu as pltpu
from jax.sharding import PartitionSpec as P

D = 4096
HD = 128
SPAN = 64
R = 128
N = 64
C = 8
S = 32
H = 4
U = 4
TB = SPAN // U
W = U * HD
SPANS = N * C
SLOTS = N * S
HALF = S // 2
ROUTE_STEPS = 8
PRODUCT_STEPS = 8
SCALE = 1.0 / math.sqrt(HD)
BF = jnp.bfloat16
F32 = jnp.float32
MIB = 1 << 20


def iota(shape, dim):
    return lax.broadcasted_iota(jnp.int32, shape, dim)


def hot(mask):
    return jnp.where(mask, 1.0, 0.0).astype(BF)


def mm(a, b):
    return jnp.dot(a, b, preferred_element_type=F32)


def mm_t(a, b):
    return lax.dot_general(a, b, (((1,), (1,)), ((), ())), preferred_element_type=F32)


def t_mm(a, b):
    return lax.dot_general(a, b, (((0,), (0,)), ((), ())), preferred_element_type=F32)


def call(body, out_shape, flops=1e8, nbytes=4e6, vmem=40, **kw):
    return pl.pallas_call(
        body,
        out_shape=out_shape,
        compiler_params=pltpu.CompilerParams(vmem_limit_bytes=vmem * MIB),
        cost_estimate=pl.CostEstimate(
            flops=int(flops), bytes_accessed=int(nbytes), transcendentals=0
        ),
        **kw,
    )


def sds(shape, dtype):
    return jax.ShapeDtypeStruct(shape, dtype)


def token_row(piece_row):
    return (piece_row % C) * SPAN + ((piece_row // C) % U) * TB + piece_row // (U * C)


def prep_body(q_hbm, g_hbm, digits_ref, out_hbm, q_ref, g_ref, order, stage, in_sem, out_sem):
    size = C * SPAN
    loads = [
        pltpu.make_async_copy(src, dst, in_sem.at[i])
        for i, (src, dst) in enumerate(((q_hbm, q_ref), (g_hbm, g_ref)))
    ]
    for load in loads:
        load.start()
    order[...] = hot(iota((size, size), 1) == token_row(iota((size, size), 0)))
    stage[:, 2 * U * C :, :] = jnp.broadcast_to(digits_ref[...][None], (N, C, HD))
    for load in loads:
        load.wait()
    stores = []
    half = H // 2
    for i in range(2):
        lanes = slice(i * half * HD, (i + 1) * half * HD)
        for base, ref in ((0, q_ref), (U * C, g_ref)):
            rows = mm(order[...], ref[:, lanes]).astype(BF)
            for j in range(half):
                h = i * half + j
                stage[h * TB : (h + 1) * TB, base : base + U * C, :] = rows[
                    :, j * HD : (j + 1) * HD
                ].reshape(TB, U * C, HD)
        part = pl.ds(i * half * TB, half * TB)
        stores.append(pltpu.make_async_copy(stage.at[part], out_hbm.at[part], out_sem.at[i]))
        stores[-1].start()
    for store in stores:
        store.wait()


def final_body(in_ref, att_ref, qg_ref):
    size = C * SPAN
    order = hot(iota((size, size), 0) == token_row(iota((size, size), 1)))
    for base, ref in ((0, att_ref), (U * C, qg_ref)):
        cat = jnp.concatenate(
            [
                in_ref[h * TB : (h + 1) * TB, base : base + U * C, :].reshape(size, HD)
                for h in range(H)
            ],
            axis=1,
        )
        ref[...] = mm(order, cat).astype(BF)


def span_rows(block):
    wide = block.astype(F32)
    return [wide[:, u * C : (u + 1) * C, :].reshape(SPANS, HD) for u in range(U)]


def route_body(base, first_ref, out_hbm, row_ref, x_ref, out_ref, out_sem):
    digits = first_ref[:, 2 * U * C :, :].astype(F32).reshape(SPANS, HD)
    lane = iota((SPANS, HD), 1)
    slot_part = pltpu.roll(digits, HD - 2, 1)
    cols = jnp.where(lane < 2, digits * float(S) + slot_part, 0.0)
    cols = cols + jnp.where((lane >= 2) & (lane < 6), pltpu.roll(digits, 2, 1), 0.0)
    rows = jnp.transpose(cols)[:8]
    row_ref[...] = rows
    for u, part in enumerate(span_rows(first_ref[:, base : base + U * C, :])):
        x_ref[:, u * HD : (u + 1) * HD] = part.astype(BF)
    per = N // ROUTE_STEPS
    slot_a = rows[0:1]
    slot_b = rows[1:2]

    def store(j):
        at = pl.ds(pl.multiple_of(j * per, per), per)
        return pltpu.make_async_copy(out_ref.at[at], out_hbm.at[at], out_sem.at[j])

    def step(j, _):
        ids = (iota((per * S, SPANS), 0) + j * (per * S)).astype(F32)
        hit = hot((ids == slot_a) | (ids == slot_b))
        got = mm(hit, x_ref[...]).astype(BF)
        at = pl.ds(pl.multiple_of(j * per, per), per)
        for u in range(U):
            out_ref[at, u * S : (u + 1) * S, :] = got[:, u * HD : (u + 1) * HD].reshape(
                per, S, HD
            )
        store(j).start()
        return 0

    lax.fori_loop(0, ROUTE_STEPS, step, 0)
    for j in range(ROUTE_STEPS):
        store(j).wait()


def swap_order():
    size = TB * HALF
    a, b = iota((size, size), 0), iota((size, size), 1)
    return hot((a // TB == b % TB) & (a % TB == b // TB))


def to_slots(order, src_ref, dst_ref):
    for h in range(H):
        pair, i = h // 2, h % 2
        for u in range(0, U, 2):
            block = jnp.concatenate(
                [
                    src_ref[h * TB : (h + 1) * TB, v, :, :].reshape(TB * HALF, HD)
                    for v in (u, u + 1)
                ],
                axis=1,
            )
            rows = mm(order, block).astype(BF)
            for j in range(2):
                lo = i * SPAN + (u + j) * TB
                dst_ref[:, pair, lo : lo + TB, i * HD : (i + 1) * HD] = rows[
                    :, j * HD : (j + 1) * HD
                ].reshape(HALF, TB, HD)


def in_hbm(rows):
    return pltpu.with_memory_space_constraint(rows, pltpu.HBM)


def load_half(src_hbm, dst_ref, sem):
    part = pl.ds(pl.multiple_of(pl.program_id(0) * HALF, HALF), HALF)
    return pltpu.make_async_copy(src_hbm.at[:, :, part, :], dst_ref, sem)


def forward_body(
    q_hbm, nb_ref, rs_ref, e_ref, k_ref, v_ref, p_ref, b_ref, stat_ref, q_ref, qs, pbs, tops, totals, sem
):
    step = pl.program_id(0)
    load = load_half(q_hbm, q_ref, sem)
    load.start()
    order = swap_order()

    @pl.when(step == 0)
    def _():
        tops[...] = jnp.zeros_like(tops)
        totals[...] = jnp.zeros_like(totals)
        qs[...] = jnp.zeros_like(qs)

    load.wait()
    to_slots(order, q_ref, qs)
    row = iota((2 * SPAN, HD), 0) % SPAN

    def slot(s, _):
        at = step * HALF + s
        scale = jnp.sum(
            jnp.where(iota((R, HD), 1) == at, rs_ref[...], 0.0), axis=1, keepdims=True
        )
        mark = iota((2 * SPAN, HD), 1) == (row // TB) * S + at
        for pair in range(H // 2):
            lo = 4 * pair * HD
            part = [
                nb_ref[s, :, lo + i * HD : lo + (i + 1) * HD].astype(F32) * scale
                for i in range(4)
            ]
            keys = [part[0].astype(BF), part[2].astype(BF)]
            key2 = jnp.concatenate(keys, axis=1)
            q2 = qs[s, pair]
            scores = mm_t(q2, key2) * SCALE
            split = scores.reshape(2, SPAN, R)
            cond = jnp.exp(split - jnp.max(split, axis=1, keepdims=True))
            cond = cond / jnp.sum(cond, axis=1, keepdims=True)
            cond = t_mm(cond.reshape(2 * SPAN, R).astype(BF), q2)
            values = [
                (part[2 * i + 1] + cond[:, i * HD : (i + 1) * HD]).astype(BF) for i in range(2)
            ]
            top = jnp.max(scores, axis=1, keepdims=True).astype(BF).astype(F32)
            expo = jnp.exp(scores - top)
            total = jnp.sum(expo, axis=1, keepdims=True)
            low = expo.astype(BF)
            e_ref[s, pair] = expo
            k_ref[s, pair] = key2
            v_ref[s, pair] = jnp.concatenate(values, axis=1)
            for i in range(2):
                pbs[s, 2 * pair + i] = mm(
                    low[i * SPAN : (i + 1) * SPAN], jnp.concatenate([values[i], keys[i]], axis=1)
                ).astype(BF)
            tops[pair] = jnp.where(mark, top, tops[pair])
            totals[pair] = jnp.where(mark, total, totals[pair])
        return 0

    lax.fori_loop(0, HALF, slot, 0, unroll=2)
    for h in range(H):
        for u in range(U):
            block = pbs[:, h, u * TB : (u + 1) * TB, :].reshape(HALF * TB, 2 * HD)
            rows = mm(order, block).astype(BF)
            for i, dst_ref in enumerate((p_ref, b_ref)):
                dst_ref[h * TB : (h + 1) * TB, u, :, :] = rows[
                    :, i * HD : (i + 1) * HD
                ].reshape(TB, HALF, HD)

    @pl.when(step == 1)
    def _():
        place = iota((TB, C, HD), 1)
        for h in range(H):
            lo = (h % 2) * SPAN
            rows = []
            for acc in (tops, totals):
                total = acc[h // 2, lo : lo + TB]
                for u in range(1, U):
                    total = total + acc[h // 2, lo + u * TB : lo + (u + 1) * TB]
                rows.append(total[:, None, :])
            stat_ref[h * TB : (h + 1) * TB] = jnp.where(
                place == 0, rows[0], jnp.where(place == 1, rows[1], 0.0)
            )


def backward_body(g_ref, e_ref, k_ref, v_ref, a_ref, gs, as_):
    order = swap_order()

    @pl.when(pl.program_id(0) == 0)
    def _():
        gs[...] = jnp.zeros_like(gs)

    to_slots(order, g_ref, gs)

    def slot(s, _):
        for pair in range(H // 2):
            grad = mm_t(gs[s, pair], v_ref[s, pair])
            both = mm((e_ref[s, pair] * grad).astype(BF), k_ref[s, pair]).astype(BF)
            for i in range(2):
                as_[s, 2 * pair + i] = both[i * SPAN : (i + 1) * SPAN, i * HD : (i + 1) * HD]
        return 0

    lax.fori_loop(0, HALF, slot, 0, unroll=2)
    for h in range(H):
        for u in range(0, U, 2):
            block = jnp.concatenate(
                [
                    as_[:, h, v * TB : (v + 1) * TB, :].reshape(HALF * TB, HD)
                    for v in (u, u + 1)
                ],
                axis=1,
            )
            rows = mm(order, block).astype(BF)
            for j in range(2):
                a_ref[h * TB : (h + 1) * TB, u + j, :, :] = rows[
                    :, j * HD : (j + 1) * HD
                ].reshape(TB, HALF, HD)


def choose_rows(in_ref, picks, out_refs, cat_ref, size=128):
    for u in range(U):
        cat_ref[:, u * HD : (u + 1) * HD] = in_ref[:, u * S : (u + 1) * S, :].reshape(SLOTS, HD)
    for cols, out_ref in zip(picks, out_refs):

        def step(i, _, cols=cols, out_ref=out_ref):
            at = pl.ds(pl.multiple_of(i * size, size), size)
            ids = iota((size, SLOTS), 1).astype(F32)
            mask = ids == cols[0][at, :]
            for col in cols[1:]:
                mask = mask | (ids == col[at, :])
            out_ref[at, :] = mm(hot(mask), cat_ref[...])
            return 0

        lax.fori_loop(0, SPANS // size, step, 0)


def product_body(p_hbm, stat_hbm, g_ref, out_hbm, rows_ref, stat_ref, in_sem, out_sem):
    size = U * S
    per = N // PRODUCT_STEPS
    diagonal = iota((size, HD), 0) == iota((size, HD), 1)
    row = iota((C, HD), 0)

    def load(i):
        at = pl.ds(i * per, per)
        return (
            pltpu.make_async_copy(p_hbm.at[at], rows_ref.at[at, pl.ds(0, size)], in_sem.at[0, i]),
            pltpu.make_async_copy(stat_hbm.at[at], stat_ref.at[at], in_sem.at[1, i]),
        )

    def store(i):
        at = pl.ds(i * per, per)
        return pltpu.make_async_copy(rows_ref.at[at], out_hbm.at[at], out_sem.at[i])

    for i in range(PRODUCT_STEPS):
        for copy in load(i):
            copy.start()
    for i in range(PRODUCT_STEPS):
        for copy in load(i):
            copy.wait()
        for k in range(i * per, (i + 1) * per):
            prod = rows_ref[k, :size, :].astype(F32) * g_ref[k].astype(F32)
            prod = jnp.where(diagonal, jnp.sum(prod, axis=1, keepdims=True), 0.0)
            total = jnp.sum(prod, axis=0, keepdims=True)
            high = total.astype(BF).astype(F32)
            rows_ref[k, size:, :] = jnp.where(
                row == 2, high, jnp.where(row == 3, total - high, stat_ref[k])
            ).astype(BF)
        store(i).start()
    for i in range(PRODUCT_STEPS):
        store(i).wait()


def weight_body(stat_ref, row_ref, a_hbm, b_hbm, wd_ref, wts_ref, a_ref, b_ref, flat, sem):
    loads = [
        pltpu.make_async_copy(src, dst, sem.at[i])
        for i, (src, dst) in enumerate(((a_hbm, a_ref), (b_hbm, b_ref)))
    ]
    for load in loads:
        load.start()
    cols = jnp.transpose(row_ref[...])
    lane = iota((SPANS, HD), 1)
    flat[...] = stat_ref[...].astype(F32).reshape(N * C, HD)
    stats = jnp.concatenate(
        [flat[pl.ds(i, N, stride=C), :].astype(BF) for i in range(4)], axis=1
    )
    row, col = iota((4 * HD, HD), 0), iota((4 * HD, HD), 1)
    stat = jnp.minimum(row // HD, 2)
    group = hot(stat * U + row % HD // S == col)
    slot_lane = (iota((SPANS, 4 * HD), 1) % S).astype(F32)
    tops, totals, products = [], [], []
    for n in range(2):
        owner = hot(iota((SPANS, N), 1).astype(F32) == cols[:, 2 + n : 3 + n])
        rows = mm(owner, stats)
        rows = jnp.where(slot_lane == cols[:, 4 + n : 5 + n], rows, 0.0).astype(BF)
        rows = mm(rows, group)
        tops.append(rows)
        totals.append(pltpu.roll(rows, HD - U, 1))
        products.append(pltpu.roll(rows, HD - 2 * U, 1))
    highest = jnp.maximum(tops[0], tops[1])
    factor = [jnp.exp(t - highest) for t in tops]
    denominator = factor[0] * totals[0] + factor[1] * totals[1]
    low = [jnp.where(lane < U, f / denominator, 0.0).astype(BF).astype(F32) for f in factor]
    delta = jnp.where(lane < U, low[0] * products[0] + low[1] * products[1], 0.0)
    wts_ref[...] = (low[0] + pltpu.roll(low[1], U, 1)).astype(BF)
    delta = pltpu.roll(delta, U, 1)
    spread = hot(iota((HD, 2 * HD), 0) == iota((HD, 2 * HD), 1) // S)
    out = jnp.zeros((N, 2 * HD), F32)
    for n in range(2):
        rows = mm((low[n] + delta).astype(BF), spread)
        rows = jnp.where(slot_lane[:, : 2 * HD] == cols[:, 4 + n : 5 + n], rows, 0.0)
        owners = hot(iota((N, SPANS), 0).astype(F32) == row_ref[2 + n : 3 + n, :])
        out = out + mm(owners, rows.astype(BF))
    place = iota((N, C, HD), 1)
    wd_ref[...] = jnp.where(
        place == 0, out[:, None, :HD], jnp.where(place == 1, out[:, None, HD:], 0.0)
    ).astype(BF)
    for load in loads:
        load.wait()


def attended_body(
    back_ref, row_ref, wts_ref, att_ref, cat, pa, pb, ca, cb
):
    cols = jnp.transpose(row_ref[...])
    ca[...] = cols[:, 0:1]
    cb[...] = cols[:, 1:2]
    choose_rows(back_ref, ((ca,), (cb,)), (pa, pb), cat)
    wide = hot(iota((HD, 2 * W), 0) == iota((HD, 2 * W), 1) // HD)
    weight = mm(wts_ref[...], wide)
    attended = weight[:, :W] * pa[...] + weight[:, W:] * pb[...]
    for u in range(0, U, 2):
        att_ref[:, u * C : (u + 2) * C, :] = jnp.concatenate(
            [
                attended[:, v * HD : (v + 1) * HD].reshape(N, C, HD)
                for v in (u, u + 1)
            ],
            axis=1,
        ).astype(BF)


def scale_body(wd_ref, a_ref, b_ref, out_hbm, out_ref, sem):
    per = N // PRODUCT_STEPS

    def store(i):
        at = pl.ds(i * per, per)
        return pltpu.make_async_copy(out_ref.at[at], out_hbm.at[at], sem.at[i])

    flat = wd_ref[...].astype(F32).reshape(C * N, HD)
    cols = jnp.transpose(flat)
    for i in range(PRODUCT_STEPS):
        for k in range(i * per, (i + 1) * per):
            w = cols[:, C * k : C * k + 1]
            delta = cols[:, C * k + 1 : C * k + 2]
            out_ref[k] = (
                w * (a_ref[k].astype(F32) - delta * b_ref[k].astype(F32)) * SCALE
            ).astype(BF)
        store(i).start()
    for i in range(PRODUCT_STEPS):
        store(i).wait()


def sum_body(terms_ref, att_ref, row_ref, out_ref, cat, acc, ca, cb):
    cols = jnp.transpose(row_ref[...])
    ca[...] = cols[:, 0:1]
    cb[...] = cols[:, 1:2]
    choose_rows(terms_ref, ((ca, cb),), (acc,), cat, 256)
    out_ref[:, : U * C, :] = att_ref[...]
    for u in range(0, U, 2):
        base = U * C + u * C
        out_ref[:, base : base + 2 * C, :] = jnp.concatenate(
            [acc[:, v * HD : (v + 1) * HD].reshape(N, C, HD) for v in (u, u + 1)], axis=1
        ).astype(BF)


def swap(rows):
    return lax.all_to_all(rows, "seq", split_axis=0, concat_axis=0, tiled=True)


HBM = pl.BlockSpec(memory_space=pltpu.HBM)
VMEM = pl.BlockSpec(memory_space=pltpu.VMEM)


def whole(*shape):
    return pl.BlockSpec(shape, lambda i: (0,) * len(shape))


def route(first, base):
    return call(
        functools.partial(route_body, base),
        (pltpu.HBM((N, U * S, HD), BF), sds((8, SPANS), F32)),
        in_specs=[VMEM],
        out_specs=(HBM, VMEM),
        scratch_shapes=[
            pltpu.VMEM((SPANS, W), BF),
            pltpu.VMEM((N, U * S, HD), BF),
            pltpu.SemaphoreType.DMA((ROUTE_STEPS,)),
        ],
        flops=1.1e9,
    )(first)


def local(queries, out_grad, neighbours, placement):
    owner, place = placement // S, placement % S
    digits = jnp.concatenate([owner, place], axis=1).astype(BF)
    digits = jnp.pad(digits, ((0, 0), (0, HD - 4)))
    rows_in = 2 * U * C + C
    tokens = pltpu.VMEM(queries.shape, BF)
    first = swap(
        call(
            prep_body,
            pltpu.HBM((N, rows_in, HD), BF),
            in_specs=[HBM, HBM, VMEM],
            out_specs=HBM,
            scratch_shapes=[
                tokens,
                tokens,
                pltpu.VMEM((C * SPAN, C * SPAN), BF),
                pltpu.VMEM((N, rows_in, HD), BF),
                pltpu.SemaphoreType.DMA((2,)),
                pltpu.SemaphoreType.DMA((2,)),
            ],
            flops=5e8,
        )(in_hbm(queries), in_hbm(out_grad), digits)
    )
    square_sums = jnp.sum(jnp.square(neighbours.astype(F32)), axis=-1)
    row_scale = lax.rsqrt(lax.psum(square_sums, "head") / D + 1e-06)
    row_scale = jnp.pad(row_scale.T, ((0, 0), (0, HD - S)))

    first, row_scale = lax.optimization_barrier((first, row_scale))
    q_send, rowv = route(first, 0)
    got_q = swap(q_send)
    g_send = route(first, U * C)[0]
    got_g = swap(g_send)

    def cut(rows):
        return rows.reshape(N, U, S, HD)

    half_piece = pl.BlockSpec((N, U, HALF, HD), lambda i: (0, 0, i, 0))
    by_slot = lambda *tail: pl.BlockSpec((HALF, H // 2) + tail, lambda i: (i, 0, 0, 0))
    half_rows = pltpu.VMEM((N, U, HALF, HD), BF)
    diagonal = pltpu.VMEM((HALF, H // 2, 2 * SPAN, 2 * HD), BF)
    stat_acc = pltpu.VMEM((H // 2, 2 * SPAN, HD), F32)
    expo, keys, values, p_send, b_rows, stats = call(
        forward_body,
        (
            sds((S, H // 2, 2 * SPAN, R), F32),
            sds((S, H // 2, R, 2 * HD), BF),
            sds((S, H // 2, R, 2 * HD), BF),
            pltpu.HBM((N, U, S, HD), BF),
            pltpu.HBM((N, U, S, HD), BF),
            pltpu.HBM((N, C, HD), F32),
        ),
        grid=(2,),
        in_specs=[
            HBM,
            pl.BlockSpec((HALF, R, 2 * H * HD), lambda i: (i, 0, 0)),
            whole(R, HD),
        ],
        out_specs=(
            by_slot(2 * SPAN, R),
            by_slot(R, 2 * HD),
            by_slot(R, 2 * HD),
            half_piece,
            half_piece,
            whole(N, C, HD),
        ),
        scratch_shapes=[
            half_rows,
            diagonal,
            pltpu.VMEM((HALF, H, SPAN, 2 * HD), BF),
            stat_acc,
            stat_acc,
            pltpu.SemaphoreType.DMA,
        ],
        flops=2e9,
        nbytes=3e7,
        vmem=56,
    )(in_hbm(cut(got_q)), neighbours, row_scale)
    back = swap(
        call(
            product_body,
            pltpu.HBM((N, U * S + C, HD), BF),
            in_specs=[HBM, HBM, VMEM],
            out_specs=HBM,
            scratch_shapes=[
                pltpu.VMEM((N, U * S + C, HD), BF),
                pltpu.VMEM((N, C, HD), F32),
                pltpu.SemaphoreType.DMA((2, PRODUCT_STEPS)),
                pltpu.SemaphoreType.DMA((PRODUCT_STEPS,)),
            ],
        )(in_hbm(p_send.reshape(N, U * S, HD)), in_hbm(stats), got_g)
    )
    a_rows = call(
        backward_body,
        pltpu.HBM((N, U, S, HD), BF),
        grid=(2,),
        in_specs=[half_piece, by_slot(2 * SPAN, R), by_slot(R, 2 * HD), by_slot(R, 2 * HD)],
        out_specs=half_piece,
        scratch_shapes=[diagonal, pltpu.VMEM((HALF, H, SPAN, HD), BF)],
        flops=1e9,
        nbytes=2e7,
        vmem=48,
    )(cut(got_g), expo, keys, values)

    back, a_rows = lax.optimization_barrier((back, a_rows))
    span_table = pltpu.VMEM((SPANS, W), F32)
    column = pltpu.VMEM((SPANS, 1), F32)
    cat = pltpu.VMEM((SLOTS, W), BF)
    rows = sds((N, U * S, HD), BF)
    wd_send, wts, a_rows, b_rows = call(
        weight_body,
        (sds((N, C, HD), BF), sds((SPANS, HD), BF), rows, rows),
        grid=(1,),
        in_specs=[
            pl.BlockSpec((N, C, HD), lambda i: (0, U * S // C, 0)),
            whole(8, SPANS),
            HBM,
            HBM,
        ],
        out_specs=(whole(N, C, HD), whole(SPANS, HD), VMEM, VMEM),
        scratch_shapes=[pltpu.VMEM((N * C, HD), F32), pltpu.SemaphoreType.DMA((2,))],
        vmem=40,
    )(
        back,
        rowv,
        in_hbm(a_rows.reshape(N, U * S, HD)),
        in_hbm(b_rows.reshape(N, U * S, HD)),
    )
    wd = swap(wd_send)
    terms = call(
        scale_body,
        pltpu.HBM((N, U * S, HD), BF),
        in_specs=[VMEM, VMEM, VMEM],
        out_specs=HBM,
        scratch_shapes=[
            pltpu.VMEM((N, U * S, HD), BF),
            pltpu.SemaphoreType.DMA((PRODUCT_STEPS,)),
        ],
    )(wd, a_rows, b_rows)
    terms, wts = lax.optimization_barrier((terms, wts))
    attended = call(
        attended_body,
        sds((N, U * C, HD), BF),
        scratch_shapes=[cat, span_table, span_table, column, column],
        flops=2.2e9,
        vmem=40,
    )(back, rowv, wts)
    last = call(
        sum_body,
        sds((N, 2 * U * C, HD), BF),
        scratch_shapes=[cat, span_table, column, column],
        flops=1.1e9,
        vmem=48,
    )(swap(terms), attended, rowv)
    return call(
        final_body, (sds(queries.shape, BF), sds(queries.shape, BF)), flops=5e8
    )(swap(last))


def solution(mesh):
    in_specs = (P("seq", "head"), P("seq", "head"), P("seq", None, "head"), P("seq", None))
    out_specs = (P("seq", "head"), P("seq", "head"))
    return jax.shard_map(local, mesh=mesh, in_specs=in_specs, out_specs=out_specs, check_vma=False)
```

```python
import functools
import math

import jax
import jax.numpy as jnp
from jax import lax
from jax.experimental import pallas as pl
from jax.experimental.pallas import tpu as pltpu
from jax.sharding import PartitionSpec as P

D = 4096
HD = 128
SPAN = 64
R = 128
N = 64
C = 8
S = 32
H = 4
U = 4
TB = SPAN // U
W = U * HD
SPANS = N * C
SLOTS = N * S
HALF = S // 2
ROUTE_STEPS = 8
PRODUCT_STEPS = 8
SCALE = 1.0 / math.sqrt(HD)
BF = jnp.bfloat16
F32 = jnp.float32
MIB = 1 << 20


def iota(shape, dim):
    return lax.broadcasted_iota(jnp.int32, shape, dim)


def hot(mask):
    return jnp.where(mask, 1.0, 0.0).astype(BF)


def mm(a, b):
    return jnp.dot(a, b, preferred_element_type=F32)


def mm_t(a, b):
    return lax.dot_general(a, b, (((1,), (1,)), ((), ())), preferred_element_type=F32)


def t_mm(a, b):
    return lax.dot_general(a, b, (((0,), (0,)), ((), ())), preferred_element_type=F32)


def call(body, out_shape, flops=1e8, nbytes=4e6, vmem=40, **kw):
    return pl.pallas_call(
        body,
        out_shape=out_shape,
        compiler_params=pltpu.CompilerParams(vmem_limit_bytes=vmem * MIB),
        cost_estimate=pl.CostEstimate(
            flops=int(flops), bytes_accessed=int(nbytes), transcendentals=0
        ),
        **kw,
    )


def sds(shape, dtype):
    return jax.ShapeDtypeStruct(shape, dtype)


def token_row(piece_row):
    return (piece_row % C) * SPAN + ((piece_row // C) % U) * TB + piece_row // (U * C)


def prep_body(q_hbm, g_hbm, digits_ref, out_hbm, q_ref, g_ref, order, stage, in_sem, out_sem):
    size = C * SPAN
    loads = [
        pltpu.make_async_copy(src, dst, in_sem.at[i])
        for i, (src, dst) in enumerate(((q_hbm, q_ref), (g_hbm, g_ref)))
    ]
    for load in loads:
        load.start()
    order[...] = hot(iota((size, size), 1) == token_row(iota((size, size), 0)))
    stage[:, 2 * U * C :, :] = jnp.broadcast_to(digits_ref[...][None], (N, C, HD))
    for load in loads:
        load.wait()
    stores = []
    half = H // 2
    for i in range(2):
        lanes = slice(i * half * HD, (i + 1) * half * HD)
        for base, ref in ((0, q_ref), (U * C, g_ref)):
            rows = mm(order[...], ref[:, lanes]).astype(BF)
            for j in range(half):
                h = i * half + j
                stage[h * TB : (h + 1) * TB, base : base + U * C, :] = rows[
                    :, j * HD : (j + 1) * HD
                ].reshape(TB, U * C, HD)
        part = pl.ds(i * half * TB, half * TB)
        stores.append(pltpu.make_async_copy(stage.at[part], out_hbm.at[part], out_sem.at[i]))
        stores[-1].start()
    for store in stores:
        store.wait()


def final_body(in_ref, att_ref, qg_ref):
    size = C * SPAN
    order = hot(iota((size, size), 0) == token_row(iota((size, size), 1)))
    for base, ref in ((0, att_ref), (U * C, qg_ref)):
        cat = jnp.concatenate(
            [
                in_ref[h * TB : (h + 1) * TB, base : base + U * C, :].reshape(size, HD)
                for h in range(H)
            ],
            axis=1,
        )
        ref[...] = mm(order, cat).astype(BF)


def span_rows(block):
    wide = block.astype(F32)
    return [wide[:, u * C : (u + 1) * C, :].reshape(SPANS, HD) for u in range(U)]


def route_body(base, first_ref, out_hbm, row_ref, x_ref, out_ref, out_sem):
    digits = first_ref[:, 2 * U * C :, :].astype(F32).reshape(SPANS, HD)
    lane = iota((SPANS, HD), 1)
    slot_part = pltpu.roll(digits, HD - 2, 1)
    cols = jnp.where(lane < 2, digits * float(S) + slot_part, 0.0)
    cols = cols + jnp.where((lane >= 2) & (lane < 6), pltpu.roll(digits, 2, 1), 0.0)
    rows = jnp.transpose(cols)[:8]
    row_ref[...] = rows
    for u, part in enumerate(span_rows(first_ref[:, base : base + U * C, :])):
        x_ref[:, u * HD : (u + 1) * HD] = part.astype(BF)
    per = N // ROUTE_STEPS
    slot_a = rows[0:1]
    slot_b = rows[1:2]

    def store(j):
        at = pl.ds(pl.multiple_of(j * per, per), per)
        return pltpu.make_async_copy(out_ref.at[at], out_hbm.at[at], out_sem.at[j])

    def step(j, _):
        ids = (iota((per * S, SPANS), 0) + j * (per * S)).astype(F32)
        hit = hot((ids == slot_a) | (ids == slot_b))
        got = mm(hit, x_ref[...]).astype(BF)
        at = pl.ds(pl.multiple_of(j * per, per), per)
        for u in range(U):
            out_ref[at, u * S : (u + 1) * S, :] = got[:, u * HD : (u + 1) * HD].reshape(
                per, S, HD
            )
        store(j).start()
        return 0

    lax.fori_loop(0, ROUTE_STEPS, step, 0)
    for j in range(ROUTE_STEPS):
        store(j).wait()


def swap_order():
    size = TB * HALF
    a, b = iota((size, size), 0), iota((size, size), 1)
    return hot((a // TB == b % TB) & (a % TB == b // TB))


def to_slots(order, src_ref, dst_ref):
    for h in range(H):
        pair, i = h // 2, h % 2
        for u in range(0, U, 2):
            block = jnp.concatenate(
                [
                    src_ref[h * TB : (h + 1) * TB, v, :, :].reshape(TB * HALF, HD)
                    for v in (u, u + 1)
                ],
                axis=1,
            )
            rows = mm(order, block).astype(BF)
            for j in range(2):
                lo = i * SPAN + (u + j) * TB
                dst_ref[:, pair, lo : lo + TB, i * HD : (i + 1) * HD] = rows[
                    :, j * HD : (j + 1) * HD
                ].reshape(HALF, TB, HD)


def in_hbm(rows):
    return pltpu.with_memory_space_constraint(rows, pltpu.HBM)


def load_half(src_hbm, dst_ref, sem):
    part = pl.ds(pl.multiple_of(pl.program_id(0) * HALF, HALF), HALF)
    return pltpu.make_async_copy(src_hbm.at[:, :, part, :], dst_ref, sem)


def forward_body(
    q_hbm, nb_ref, rs_ref, e_ref, k_ref, v_ref, p_ref, b_ref, stat_ref, q_ref, qs, pbs, tops, totals, sem
):
    step = pl.program_id(0)
    load = load_half(q_hbm, q_ref, sem)
    load.start()
    order = swap_order()

    @pl.when(step == 0)
    def _():
        tops[...] = jnp.zeros_like(tops)
        totals[...] = jnp.zeros_like(totals)
        qs[...] = jnp.zeros_like(qs)

    load.wait()
    to_slots(order, q_ref, qs)
    row = iota((2 * SPAN, HD), 0) % SPAN

    def slot(s, _):
        at = step * HALF + s
        scale = jnp.sum(
            jnp.where(iota((R, HD), 1) == at, rs_ref[...], 0.0), axis=1, keepdims=True
        )
        mark = iota((2 * SPAN, HD), 1) == (row // TB) * S + at
        for pair in range(H // 2):
            lo = 4 * pair * HD
            part = [
                nb_ref[s, :, lo + i * HD : lo + (i + 1) * HD].astype(F32) * scale
                for i in range(4)
            ]
            keys = [part[0].astype(BF), part[2].astype(BF)]
            key2 = jnp.concatenate(keys, axis=1)
            q2 = qs[s, pair]
            scores = mm_t(q2, key2) * SCALE
            split = scores.reshape(2, SPAN, R)
            cond = jnp.exp(split - jnp.max(split, axis=1, keepdims=True))
            cond = cond / jnp.sum(cond, axis=1, keepdims=True)
            cond = t_mm(cond.reshape(2 * SPAN, R).astype(BF), q2)
            values = [
                (part[2 * i + 1] + cond[:, i * HD : (i + 1) * HD]).astype(BF) for i in range(2)
            ]
            top = jnp.max(scores, axis=1, keepdims=True).astype(BF).astype(F32)
            expo = jnp.exp(scores - top)
            total = jnp.sum(expo, axis=1, keepdims=True)
            low = expo.astype(BF)
            e_ref[s, pair] = expo
            k_ref[s, pair] = key2
            v_ref[s, pair] = jnp.concatenate(values, axis=1)
            for i in range(2):
                pbs[s, 2 * pair + i] = mm(
                    low[i * SPAN : (i + 1) * SPAN], jnp.concatenate([values[i], keys[i]], axis=1)
                ).astype(BF)
            tops[pair] = jnp.where(mark, top, tops[pair])
            totals[pair] = jnp.where(mark, total, totals[pair])
        return 0

    lax.fori_loop(0, HALF, slot, 0, unroll=2)
    for h in range(H):
        for u in range(U):
            block = pbs[:, h, u * TB : (u + 1) * TB, :].reshape(HALF * TB, 2 * HD)
            rows = mm(order, block).astype(BF)
            for i, dst_ref in enumerate((p_ref, b_ref)):
                dst_ref[h * TB : (h + 1) * TB, u, :, :] = rows[
                    :, i * HD : (i + 1) * HD
                ].reshape(TB, HALF, HD)

    @pl.when(step == 1)
    def _():
        place = iota((TB, C, HD), 1)
        for h in range(H):
            lo = (h % 2) * SPAN
            rows = []
            for acc in (tops, totals):
                total = acc[h // 2, lo : lo + TB]
                for u in range(1, U):
                    total = total + acc[h // 2, lo + u * TB : lo + (u + 1) * TB]
                rows.append(total[:, None, :])
            stat_ref[h * TB : (h + 1) * TB] = jnp.where(
                place == 0, rows[0], jnp.where(place == 1, rows[1], 0.0)
            ).astype(BF)


def backward_body(g_ref, e_ref, k_ref, v_ref, a_ref, gs, as_):
    order = swap_order()

    @pl.when(pl.program_id(0) == 0)
    def _():
        gs[...] = jnp.zeros_like(gs)

    to_slots(order, g_ref, gs)

    def slot(s, _):
        for pair in range(H // 2):
            grad = mm_t(gs[s, pair], v_ref[s, pair])
            both = mm((e_ref[s, pair] * grad).astype(BF), k_ref[s, pair]).astype(BF)
            for i in range(2):
                as_[s, 2 * pair + i] = both[i * SPAN : (i + 1) * SPAN, i * HD : (i + 1) * HD]
        return 0

    lax.fori_loop(0, HALF, slot, 0, unroll=2)
    for h in range(H):
        for u in range(0, U, 2):
            block = jnp.concatenate(
                [
                    as_[:, h, v * TB : (v + 1) * TB, :].reshape(HALF * TB, HD)
                    for v in (u, u + 1)
                ],
                axis=1,
            )
            rows = mm(order, block).astype(BF)
            for j in range(2):
                a_ref[h * TB : (h + 1) * TB, u + j, :, :] = rows[
                    :, j * HD : (j + 1) * HD
                ].reshape(TB, HALF, HD)


def choose_rows(in_ref, picks, out_refs, cat_ref, size=128):
    for u in range(U):
        cat_ref[:, u * HD : (u + 1) * HD] = in_ref[:, u * S : (u + 1) * S, :].reshape(SLOTS, HD)
    for cols, out_ref in zip(picks, out_refs):

        def step(i, _, cols=cols, out_ref=out_ref):
            at = pl.ds(pl.multiple_of(i * size, size), size)
            ids = iota((size, SLOTS), 1).astype(F32)
            mask = ids == cols[0][at, :]
            for col in cols[1:]:
                mask = mask | (ids == col[at, :])
            out_ref[at, :] = mm(hot(mask), cat_ref[...])
            return 0

        lax.fori_loop(0, SPANS // size, step, 0)


def weight_body(
    back_ref, g_hbm, row_ref, a_hbm, b_hbm, wd_ref, wts_ref, a_ref, b_ref, g_ref, flat, in_sem, sem
):
    size = U * S
    per = N // PRODUCT_STEPS

    def load(i):
        at = pl.ds(i * per, per)
        return pltpu.make_async_copy(g_hbm.at[at], g_ref.at[at], in_sem.at[i])

    later = [
        pltpu.make_async_copy(src, dst, sem.at[i])
        for i, (src, dst) in enumerate(((a_hbm, a_ref), (b_hbm, b_ref)))
    ]
    for i in range(PRODUCT_STEPS):
        load(i).start()
    cols = jnp.transpose(row_ref[...])
    lane = iota((SPANS, HD), 1)
    diagonal = iota((size, HD), 0) == iota((size, HD), 1)
    place = iota((C, HD), 0)
    for i in range(PRODUCT_STEPS):
        load(i).wait()
        if i == PRODUCT_STEPS // 2:
            for copy in later:
                copy.start()
        for j in range(i * per, (i + 1) * per):
            prod = back_ref[j, :size, :].astype(F32) * g_ref[j].astype(F32)
            prod = jnp.where(diagonal, jnp.sum(prod, axis=1, keepdims=True), 0.0)
            total = jnp.sum(prod, axis=0, keepdims=True)
            high = total.astype(BF).astype(F32)
            flat[j * C : (j + 1) * C, :] = jnp.where(
                place == 2,
                high,
                jnp.where(place == 3, total - high, back_ref[j, size:, :].astype(F32)),
            )
    stats = jnp.concatenate(
        [flat[pl.ds(i, N, stride=C), :].astype(BF) for i in range(4)], axis=1
    )
    row, col = iota((4 * HD, HD), 0), iota((4 * HD, HD), 1)
    stat = jnp.minimum(row // HD, 2)
    group = hot(stat * U + row % HD // S == col)
    slot_lane = (iota((SPANS, 4 * HD), 1) % S).astype(F32)
    tops, totals, products = [], [], []
    for n in range(2):
        owner = hot(iota((SPANS, N), 1).astype(F32) == cols[:, 2 + n : 3 + n])
        rows = mm(owner, stats)
        rows = jnp.where(slot_lane == cols[:, 4 + n : 5 + n], rows, 0.0).astype(BF)
        rows = mm(rows, group)
        tops.append(rows)
        totals.append(pltpu.roll(rows, HD - U, 1))
        products.append(pltpu.roll(rows, HD - 2 * U, 1))
    highest = jnp.maximum(tops[0], tops[1])
    factor = [jnp.exp(t - highest) for t in tops]
    denominator = factor[0] * totals[0] + factor[1] * totals[1]
    low = [jnp.where(lane < U, f / denominator, 0.0).astype(BF).astype(F32) for f in factor]
    delta = jnp.where(lane < U, low[0] * products[0] + low[1] * products[1], 0.0)
    wts_ref[...] = (low[0] + pltpu.roll(low[1], U, 1)).astype(BF)
    delta = pltpu.roll(delta, U, 1)
    spread = hot(iota((HD, 2 * HD), 0) == iota((HD, 2 * HD), 1) // S)
    out = jnp.zeros((N, 2 * HD), F32)
    for n in range(2):
        rows = mm((low[n] + delta).astype(BF), spread)
        rows = jnp.where(slot_lane[:, : 2 * HD] == cols[:, 4 + n : 5 + n], rows, 0.0)
        owners = hot(iota((N, SPANS), 0).astype(F32) == row_ref[2 + n : 3 + n, :])
        out = out + mm(owners, rows.astype(BF))
    place = iota((N, C, HD), 1)
    wd_ref[...] = jnp.where(
        place == 0, out[:, None, :HD], jnp.where(place == 1, out[:, None, HD:], 0.0)
    ).astype(BF)
    for copy in later:
        copy.wait()


def attended_body(
    back_ref, row_ref, wts_ref, att_ref, cat, pa, pb, ca, cb
):
    cols = jnp.transpose(row_ref[...])
    ca[...] = cols[:, 0:1]
    cb[...] = cols[:, 1:2]
    choose_rows(back_ref, ((ca,), (cb,)), (pa, pb), cat)
    wide = hot(iota((HD, 2 * W), 0) == iota((HD, 2 * W), 1) // HD)
    weight = mm(wts_ref[...], wide)
    attended = weight[:, :W] * pa[...] + weight[:, W:] * pb[...]
    for u in range(0, U, 2):
        att_ref[:, u * C : (u + 2) * C, :] = jnp.concatenate(
            [
                attended[:, v * HD : (v + 1) * HD].reshape(N, C, HD)
                for v in (u, u + 1)
            ],
            axis=1,
        ).astype(BF)


def scale_body(wd_ref, a_ref, b_ref, out_hbm, out_ref, sem):
    per = N // PRODUCT_STEPS

    def store(i):
        at = pl.ds(i * per, per)
        return pltpu.make_async_copy(out_ref.at[at], out_hbm.at[at], sem.at[i])

    flat = wd_ref[...].astype(F32).reshape(C * N, HD)
    cols = jnp.transpose(flat)
    for i in range(PRODUCT_STEPS):
        for k in range(i * per, (i + 1) * per):
            w = cols[:, C * k : C * k + 1]
            delta = cols[:, C * k + 1 : C * k + 2]
            out_ref[k] = (
                w * (a_ref[k].astype(F32) - delta * b_ref[k].astype(F32)) * SCALE
            ).astype(BF)
        store(i).start()
    for i in range(PRODUCT_STEPS):
        store(i).wait()


def sum_body(terms_ref, att_ref, row_ref, out_ref, cat, acc, ca, cb):
    cols = jnp.transpose(row_ref[...])
    ca[...] = cols[:, 0:1]
    cb[...] = cols[:, 1:2]
    choose_rows(terms_ref, ((ca, cb),), (acc,), cat, 256)
    out_ref[:, : U * C, :] = att_ref[...]
    for u in range(0, U, 2):
        base = U * C + u * C
        out_ref[:, base : base + 2 * C, :] = jnp.concatenate(
            [acc[:, v * HD : (v + 1) * HD].reshape(N, C, HD) for v in (u, u + 1)], axis=1
        ).astype(BF)


def swap(rows):
    return lax.all_to_all(rows, "seq", split_axis=0, concat_axis=0, tiled=True)


HBM = pl.BlockSpec(memory_space=pltpu.HBM)
VMEM = pl.BlockSpec(memory_space=pltpu.VMEM)


def whole(*shape):
    return pl.BlockSpec(shape, lambda i: (0,) * len(shape))


def route(first, base):
    return call(
        functools.partial(route_body, base),
        (pltpu.HBM((N, U * S, HD), BF), sds((8, SPANS), F32)),
        in_specs=[VMEM],
        out_specs=(HBM, VMEM),
        scratch_shapes=[
            pltpu.VMEM((SPANS, W), BF),
            pltpu.VMEM((N, U * S, HD), BF),
            pltpu.SemaphoreType.DMA((ROUTE_STEPS,)),
        ],
        flops=1.1e9,
    )(first)


def local(queries, out_grad, neighbours, placement):
    owner, place = placement // S, placement % S
    digits = jnp.concatenate([owner, place], axis=1).astype(BF)
    digits = jnp.pad(digits, ((0, 0), (0, HD - 4)))
    rows_in = 2 * U * C + C
    tokens = pltpu.VMEM(queries.shape, BF)
    first = swap(
        call(
            prep_body,
            pltpu.HBM((N, rows_in, HD), BF),
            in_specs=[HBM, HBM, VMEM],
            out_specs=HBM,
            scratch_shapes=[
                tokens,
                tokens,
                pltpu.VMEM((C * SPAN, C * SPAN), BF),
                pltpu.VMEM((N, rows_in, HD), BF),
                pltpu.SemaphoreType.DMA((2,)),
                pltpu.SemaphoreType.DMA((2,)),
            ],
            flops=5e8,
        )(in_hbm(queries), in_hbm(out_grad), digits)
    )
    square_sums = jnp.sum(jnp.square(neighbours.astype(F32)), axis=-1)
    row_scale = lax.rsqrt(lax.psum(square_sums, "head") / D + 1e-06)
    row_scale = jnp.pad(row_scale.T, ((0, 0), (0, HD - S)))

    first, row_scale = lax.optimization_barrier((first, row_scale))
    q_send, rowv = route(first, 0)
    got_q = swap(q_send)
    g_send = route(first, U * C)[0]
    got_g = swap(g_send)

    def cut(rows):
        return rows.reshape(N, U, S, HD)

    half_piece = pl.BlockSpec((N, U, HALF, HD), lambda i: (0, 0, i, 0))
    by_slot = lambda *tail: pl.BlockSpec((HALF, H // 2) + tail, lambda i: (i, 0, 0, 0))
    half_rows = pltpu.VMEM((N, U, HALF, HD), BF)
    diagonal = pltpu.VMEM((HALF, H // 2, 2 * SPAN, 2 * HD), BF)
    stat_acc = pltpu.VMEM((H // 2, 2 * SPAN, HD), F32)
    expo, keys, values, p_send, b_rows, stats = call(
        forward_body,
        (
            sds((S, H // 2, 2 * SPAN, R), F32),
            sds((S, H // 2, R, 2 * HD), BF),
            sds((S, H // 2, R, 2 * HD), BF),
            pltpu.HBM((N, U, S, HD), BF),
            pltpu.HBM((N, U, S, HD), BF),
            sds((N, C, HD), BF),
        ),
        grid=(2,),
        in_specs=[
            HBM,
            pl.BlockSpec((HALF, R, 2 * H * HD), lambda i: (i, 0, 0)),
            whole(R, HD),
        ],
        out_specs=(
            by_slot(2 * SPAN, R),
            by_slot(R, 2 * HD),
            by_slot(R, 2 * HD),
            half_piece,
            half_piece,
            whole(N, C, HD),
        ),
        scratch_shapes=[
            half_rows,
            diagonal,
            pltpu.VMEM((HALF, H, SPAN, 2 * HD), BF),
            stat_acc,
            stat_acc,
            pltpu.SemaphoreType.DMA,
        ],
        flops=2e9,
        nbytes=3e7,
        vmem=56,
    )(in_hbm(cut(got_q)), neighbours, row_scale)
    back_send = jnp.concatenate([p_send.reshape(N, U * S, HD), stats], axis=1)
    back_send, got_g = lax.optimization_barrier((back_send, got_g))
    back = swap(back_send)
    a_rows = call(
        backward_body,
        pltpu.HBM((N, U, S, HD), BF),
        grid=(2,),
        in_specs=[half_piece, by_slot(2 * SPAN, R), by_slot(R, 2 * HD), by_slot(R, 2 * HD)],
        out_specs=half_piece,
        scratch_shapes=[diagonal, pltpu.VMEM((HALF, H, SPAN, HD), BF)],
        flops=1e9,
        nbytes=2e7,
        vmem=48,
    )(cut(got_g), expo, keys, values)

    back, a_rows = lax.optimization_barrier((back, a_rows))
    span_table = pltpu.VMEM((SPANS, W), F32)
    column = pltpu.VMEM((SPANS, 1), F32)
    cat = pltpu.VMEM((SLOTS, W), BF)
    rows = sds((N, U * S, HD), BF)
    wd_send, wts, a_rows, b_rows = call(
        weight_body,
        (sds((N, C, HD), BF), sds((SPANS, HD), BF), rows, rows),
        in_specs=[VMEM, HBM, VMEM, HBM, HBM],
        scratch_shapes=[
            pltpu.VMEM((N, U * S, HD), BF),
            pltpu.VMEM((N * C, HD), F32),
            pltpu.SemaphoreType.DMA((PRODUCT_STEPS,)),
            pltpu.SemaphoreType.DMA((2,)),
        ],
    )(
        back,
        in_hbm(g_send),
        rowv,
        in_hbm(a_rows.reshape(N, U * S, HD)),
        in_hbm(b_rows.reshape(N, U * S, HD)),
    )
    wd = swap(wd_send)
    terms = call(
        scale_body,
        pltpu.HBM((N, U * S, HD), BF),
        in_specs=[VMEM, VMEM, VMEM],
        out_specs=HBM,
        scratch_shapes=[
            pltpu.VMEM((N, U * S, HD), BF),
            pltpu.SemaphoreType.DMA((PRODUCT_STEPS,)),
        ],
    )(wd, a_rows, b_rows)
    terms, wts = lax.optimization_barrier((terms, wts))
    attended = call(
        attended_body,
        sds((N, U * C, HD), BF),
        scratch_shapes=[cat, span_table, span_table, column, column],
        flops=2.2e9,
        vmem=40,
    )(in_hbm(back), rowv, wts)
    last = call(
        sum_body,
        sds((N, 2 * U * C, HD), BF),
        scratch_shapes=[cat, span_table, column, column],
        flops=1.1e9,
        vmem=48,
    )(swap(terms), attended, rowv)
    return call(
        final_body, (sds(queries.shape, BF), sds(queries.shape, BF)), flops=5e8
    )(swap(last))


def solution(mesh):
    in_specs = (P("seq", "head"), P("seq", "head"), P("seq", None, "head"), P("seq", None))
    out_specs = (P("seq", "head"), P("seq", "head"))
    return jax.shard_map(local, mesh=mesh, in_specs=in_specs, out_specs=out_specs, check_vma=False)
```

```python
import functools
import math

import jax
import jax.numpy as jnp
from jax import lax
from jax.experimental import pallas as pl
from jax.experimental.pallas import tpu as pltpu
from jax.sharding import PartitionSpec as P

D = 4096
HD = 128
SPAN = 64
R = 128
N = 64
C = 8
S = 32
H = 4
U = 4
TB = SPAN // U
W = U * HD
SPANS = N * C
SLOTS = N * S
HALF = S // 2
ROUTE_STEPS = 8
PRODUCT_STEPS = 8
SCALE = 1.0 / math.sqrt(HD)
BF = jnp.bfloat16
F32 = jnp.float32
MIB = 1 << 20


def iota(shape, dim):
    return lax.broadcasted_iota(jnp.int32, shape, dim)


def hot(mask):
    return jnp.where(mask, 1.0, 0.0).astype(BF)


def mm(a, b):
    return jnp.dot(a, b, preferred_element_type=F32)


def mm_t(a, b):
    return lax.dot_general(a, b, (((1,), (1,)), ((), ())), preferred_element_type=F32)


def t_mm(a, b):
    return lax.dot_general(a, b, (((0,), (0,)), ((), ())), preferred_element_type=F32)


def call(body, out_shape, flops=1e8, nbytes=4e6, vmem=40, **kw):
    return pl.pallas_call(
        body,
        out_shape=out_shape,
        compiler_params=pltpu.CompilerParams(vmem_limit_bytes=vmem * MIB),
        cost_estimate=pl.CostEstimate(
            flops=int(flops), bytes_accessed=int(nbytes), transcendentals=0
        ),
        **kw,
    )


def sds(shape, dtype):
    return jax.ShapeDtypeStruct(shape, dtype)


def token_row(piece_row):
    return (piece_row % C) * SPAN + ((piece_row // C) % U) * TB + piece_row // (U * C)


def prep_body(
    q_hbm, g_hbm, slot_hbm, out_hbm, q_ref, g_ref, slot_ref, table, order, stage, in_sem, out_sem
):
    size = C * SPAN
    loads = [
        pltpu.make_async_copy(src, dst, in_sem.at[i])
        for i, (src, dst) in enumerate(
            ((slot_hbm, slot_ref), (q_hbm, q_ref), (g_hbm, g_ref))
        )
    ]
    for load in loads:
        load.start()
    order[...] = hot(iota((size, size), 1) == token_row(iota((size, size), 0)))
    loads[0].wait()
    table[...] = jnp.zeros_like(table)
    table[0:2, 0:C] = (slot_ref[...] // S).astype(F32)
    table[2:4, 0:C] = (slot_ref[...] % S).astype(F32)
    digits = jnp.transpose(table[...])[:C]
    table[...] = jnp.zeros_like(table)
    table[:, 0:C] = digits
    stage[:, 2 * U * C :, :] = jnp.broadcast_to(table[...][None], (N, C, HD)).astype(BF)
    for load in loads[1:]:
        load.wait()
    stores = []
    half = H // 2
    for i in range(2):
        lanes = slice(i * half * HD, (i + 1) * half * HD)
        for base, ref in ((0, q_ref), (U * C, g_ref)):
            rows = mm(order[...], ref[:, lanes]).astype(BF)
            for j in range(half):
                h = i * half + j
                stage[h * TB : (h + 1) * TB, base : base + U * C, :] = rows[
                    :, j * HD : (j + 1) * HD
                ].reshape(TB, U * C, HD)
        part = pl.ds(i * half * TB, half * TB)
        stores.append(pltpu.make_async_copy(stage.at[part], out_hbm.at[part], out_sem.at[i]))
        stores[-1].start()
    for store in stores:
        store.wait()


def final_body(in_ref, att_ref, qg_ref):
    size = C * SPAN
    order = hot(iota((size, size), 0) == token_row(iota((size, size), 1)))
    for base, ref in ((0, att_ref), (U * C, qg_ref)):
        cat = jnp.concatenate(
            [
                in_ref[h * TB : (h + 1) * TB, base : base + U * C, :].reshape(size, HD)
                for h in range(H)
            ],
            axis=1,
        )
        ref[...] = mm(order, cat).astype(BF)


def span_rows(block):
    wide = block.astype(F32)
    return [wide[:, u * C : (u + 1) * C, :].reshape(SPANS, HD) for u in range(U)]


def route_body(base, first_ref, out_hbm, row_ref, x_ref, ids_ref, out_ref, out_sem):
    digits = first_ref[:, 2 * U * C :, :].astype(F32).reshape(SPANS, HD)
    lane = iota((SPANS, HD), 1)
    slot_part = pltpu.roll(digits, HD - 2, 1)
    cols = jnp.where(lane < 2, digits * float(S) + slot_part, 0.0)
    cols = cols + jnp.where((lane >= 2) & (lane < 6), pltpu.roll(digits, 2, 1), 0.0)
    rows = jnp.transpose(cols)[:8]
    row_ref[...] = rows
    for u, part in enumerate(span_rows(first_ref[:, base : base + U * C, :])):
        x_ref[:, u * HD : (u + 1) * HD] = part.astype(BF)
    per = N // ROUTE_STEPS
    slot_a = rows[0:1]
    slot_b = rows[1:2]

    def store(j):
        at = pl.ds(pl.multiple_of(j * per, per), per)
        return pltpu.make_async_copy(out_ref.at[at], out_hbm.at[at], out_sem.at[j])

    ids_ref[...] = iota((per * S, SPANS), 0).astype(F32).astype(BF)

    def step(j, _):
        first_id = (j * (per * S)).astype(F32)
        ids = ids_ref[...]
        hit = (ids == (slot_a - first_id).astype(BF)) | (ids == (slot_b - first_id).astype(BF))
        hit = jnp.where(hit, jnp.ones_like(ids), jnp.zeros_like(ids))
        got = mm(hit, x_ref[...]).astype(BF)
        at = pl.ds(pl.multiple_of(j * per, per), per)
        for u in range(U):
            out_ref[at, u * S : (u + 1) * S, :] = got[:, u * HD : (u + 1) * HD].reshape(
                per, S, HD
            )
        store(j).start()
        return 0

    lax.fori_loop(0, ROUTE_STEPS, step, 0)
    for j in range(ROUTE_STEPS):
        store(j).wait()


def swap_order():
    size = TB * HALF
    a, b = iota((size, size), 0), iota((size, size), 1)
    return hot((a // TB == b % TB) & (a % TB == b // TB))


def to_slots(order, src_ref, dst_ref):
    for h in range(H):
        pair, i = h // 2, h % 2
        for u in range(0, U, 2):
            block = jnp.concatenate(
                [
                    src_ref[h * TB : (h + 1) * TB, v, :, :].reshape(TB * HALF, HD)
                    for v in (u, u + 1)
                ],
                axis=1,
            )
            rows = mm(order, block).astype(BF)
            for j in range(2):
                lo = i * SPAN + (u + j) * TB
                dst_ref[:, pair, lo : lo + TB, i * HD : (i + 1) * HD] = rows[
                    :, j * HD : (j + 1) * HD
                ].reshape(HALF, TB, HD)


def in_hbm(rows):
    return pltpu.with_memory_space_constraint(rows, pltpu.HBM)


def load_half(src_hbm, dst_ref, sem):
    part = pl.ds(pl.multiple_of(pl.program_id(0) * HALF, HALF), HALF)
    return pltpu.make_async_copy(src_hbm.at[:, :, part, :], dst_ref, sem)


def forward_body(
    q_hbm, nb_ref, rs_ref, e_ref, k_ref, v_ref, p_ref, b_ref, stat_ref, q_ref, qs, pbs, tops, totals, sem
):
    step = pl.program_id(0)
    load = load_half(q_hbm, q_ref, sem)
    load.start()
    order = swap_order()

    @pl.when(step == 0)
    def _():
        tops[...] = jnp.zeros_like(tops)
        totals[...] = jnp.zeros_like(totals)
        qs[...] = jnp.zeros_like(qs)

    load.wait()
    to_slots(order, q_ref, qs)
    row = iota((2 * SPAN, HD), 0) % SPAN

    def slot(s, _):
        at = step * HALF + s
        scale = jnp.sum(
            jnp.where(iota((R, HD), 1) == at, rs_ref[...], 0.0), axis=1, keepdims=True
        )
        mark = iota((2 * SPAN, HD), 1) == (row // TB) * S + at
        for pair in range(H // 2):
            lo = 4 * pair * HD
            part = [
                nb_ref[s, :, lo + i * HD : lo + (i + 1) * HD].astype(F32) * scale
                for i in range(4)
            ]
            keys = [part[0].astype(BF), part[2].astype(BF)]
            key2 = jnp.concatenate(keys, axis=1)
            q2 = qs[s, pair]
            scores = mm_t(q2, key2) * SCALE
            split = scores.reshape(2, SPAN, R)
            cond = jnp.exp(split - jnp.max(split, axis=1, keepdims=True))
            cond = cond / jnp.sum(cond, axis=1, keepdims=True)
            cond = t_mm(cond.reshape(2 * SPAN, R).astype(BF), q2)
            values = [
                (part[2 * i + 1] + cond[:, i * HD : (i + 1) * HD]).astype(BF) for i in range(2)
            ]
            top = jnp.max(scores, axis=1, keepdims=True).astype(BF).astype(F32)
            expo = jnp.exp(scores - top)
            total = jnp.sum(expo, axis=1, keepdims=True)
            low = expo.astype(BF)
            e_ref[s, pair] = expo
            k_ref[s, pair] = key2
            v_ref[s, pair] = jnp.concatenate(values, axis=1)
            for i in range(2):
                pbs[s, 2 * pair + i] = mm(
                    low[i * SPAN : (i + 1) * SPAN], jnp.concatenate([values[i], keys[i]], axis=1)
                ).astype(BF)
            tops[pair] = jnp.where(mark, top, tops[pair])
            totals[pair] = jnp.where(mark, total, totals[pair])
        return 0

    lax.fori_loop(0, HALF, slot, 0, unroll=2)
    for h in range(H):
        for u in range(U):
            block = pbs[:, h, u * TB : (u + 1) * TB, :].reshape(HALF * TB, 2 * HD)
            rows = mm(order, block).astype(BF)
            for i, dst_ref in enumerate((p_ref, b_ref)):
                dst_ref[h * TB : (h + 1) * TB, u, :, :] = rows[
                    :, i * HD : (i + 1) * HD
                ].reshape(TB, HALF, HD)

    @pl.when(step == 1)
    def _():
        place = iota((TB, C, HD), 1)
        for h in range(H):
            lo = (h % 2) * SPAN
            rows = []
            for acc in (tops, totals):
                total = acc[h // 2, lo : lo + TB]
                for u in range(1, U):
                    total = total + acc[h // 2, lo + u * TB : lo + (u + 1) * TB]
                rows.append(total[:, None, :])
            stat_ref[h * TB : (h + 1) * TB] = jnp.where(
                place == 0, rows[0], jnp.where(place == 1, rows[1], 0.0)
            ).astype(BF)


def backward_body(g_ref, e_ref, k_ref, v_ref, a_ref, gs, as_):
    order = swap_order()

    @pl.when(pl.program_id(0) == 0)
    def _():
        gs[...] = jnp.zeros_like(gs)

    to_slots(order, g_ref, gs)

    def slot(s, _):
        for pair in range(H // 2):
            grad = mm_t(gs[s, pair], v_ref[s, pair])
            both = mm((e_ref[s, pair] * grad).astype(BF), k_ref[s, pair]).astype(BF)
            for i in range(2):
                as_[s, 2 * pair + i] = both[i * SPAN : (i + 1) * SPAN, i * HD : (i + 1) * HD]
        return 0

    lax.fori_loop(0, HALF, slot, 0, unroll=2)
    for h in range(H):
        for u in range(0, U, 2):
            block = jnp.concatenate(
                [
                    as_[:, h, v * TB : (v + 1) * TB, :].reshape(HALF * TB, HD)
                    for v in (u, u + 1)
                ],
                axis=1,
            )
            rows = mm(order, block).astype(BF)
            for j in range(2):
                a_ref[h * TB : (h + 1) * TB, u + j, :, :] = rows[
                    :, j * HD : (j + 1) * HD
                ].reshape(TB, HALF, HD)


def choose_rows(in_ref, picks, out_refs, cat_ref, size=128):
    for u in range(U):
        cat_ref[:, u * HD : (u + 1) * HD] = in_ref[:, u * S : (u + 1) * S, :].reshape(SLOTS, HD)
    for cols, out_ref in zip(picks, out_refs):

        def step(i, _, cols=cols, out_ref=out_ref):
            at = pl.ds(pl.multiple_of(i * size, size), size)
            ids = iota((size, SLOTS), 1).astype(F32)
            mask = ids == cols[0][at, :]
            for col in cols[1:]:
                mask = mask | (ids == col[at, :])
            out_ref[at, :] = mm(hot(mask), cat_ref[...])
            return 0

        lax.fori_loop(0, SPANS // size, step, 0)


def weight_body(
    back_ref, g_hbm, row_ref, a_hbm, b_hbm, wd_ref, wts_ref, a_ref, b_ref, g_ref, flat, in_sem, sem
):
    size = U * S
    per = N // PRODUCT_STEPS

    def load(i):
        at = pl.ds(i * per, per)
        return pltpu.make_async_copy(g_hbm.at[at], g_ref.at[at], in_sem.at[i])

    later = [
        pltpu.make_async_copy(src, dst, sem.at[i])
        for i, (src, dst) in enumerate(((a_hbm, a_ref), (b_hbm, b_ref)))
    ]
    for i in range(PRODUCT_STEPS):
        load(i).start()
    cols = jnp.transpose(row_ref[...])
    lane = iota((SPANS, HD), 1)
    diagonal = iota((size, HD), 0) == iota((size, HD), 1)
    place = iota((C, HD), 0)
    for i in range(PRODUCT_STEPS):
        load(i).wait()
        if i == PRODUCT_STEPS // 2:
            for copy in later:
                copy.start()
        for j in range(i * per, (i + 1) * per):
            prod = back_ref[j, :size, :].astype(F32) * g_ref[j].astype(F32)
            prod = jnp.where(diagonal, jnp.sum(prod, axis=1, keepdims=True), 0.0)
            total = jnp.sum(prod, axis=0, keepdims=True)
            high = total.astype(BF).astype(F32)
            flat[j * C : (j + 1) * C, :] = jnp.where(
                place == 2,
                high,
                jnp.where(place == 3, total - high, back_ref[j, size:, :].astype(F32)),
            )
    stats = jnp.concatenate(
        [flat[pl.ds(i, N, stride=C), :].astype(BF) for i in range(4)], axis=1
    )
    row, col = iota((4 * HD, HD), 0), iota((4 * HD, HD), 1)
    stat = jnp.minimum(row // HD, 2)
    group = hot(stat * U + row % HD // S == col)
    slot_lane = (iota((SPANS, 4 * HD), 1) % S).astype(F32)
    tops, totals, products = [], [], []
    for n in range(2):
        owner = hot(iota((SPANS, N), 1).astype(F32) == cols[:, 2 + n : 3 + n])
        rows = mm(owner, stats)
        rows = jnp.where(slot_lane == cols[:, 4 + n : 5 + n], rows, 0.0).astype(BF)
        rows = mm(rows, group)
        tops.append(rows)
        totals.append(pltpu.roll(rows, HD - U, 1))
        products.append(pltpu.roll(rows, HD - 2 * U, 1))
    highest = jnp.maximum(tops[0], tops[1])
    factor = [jnp.exp(t - highest) for t in tops]
    denominator = factor[0] * totals[0] + factor[1] * totals[1]
    low = [jnp.where(lane < U, f / denominator, 0.0).astype(BF).astype(F32) for f in factor]
    delta = jnp.where(lane < U, low[0] * products[0] + low[1] * products[1], 0.0)
    wts_ref[...] = (low[0] + pltpu.roll(low[1], U, 1)).astype(BF)
    delta = pltpu.roll(delta, U, 1)
    spread = hot(iota((HD, 2 * HD), 0) == iota((HD, 2 * HD), 1) // S)
    out = jnp.zeros((N, 2 * HD), F32)
    for n in range(2):
        rows = mm((low[n] + delta).astype(BF), spread)
        rows = jnp.where(slot_lane[:, : 2 * HD] == cols[:, 4 + n : 5 + n], rows, 0.0)
        owners = hot(iota((N, SPANS), 0).astype(F32) == row_ref[2 + n : 3 + n, :])
        out = out + mm(owners, rows.astype(BF))
    place = iota((N, C, HD), 1)
    wd_ref[...] = jnp.where(
        place == 0, out[:, None, :HD], jnp.where(place == 1, out[:, None, HD:], 0.0)
    ).astype(BF)
    for copy in later:
        copy.wait()


def attended_body(
    back_ref, row_ref, wts_ref, att_ref, cat, pa, pb, ca, cb
):
    cols = jnp.transpose(row_ref[...])
    ca[...] = cols[:, 0:1]
    cb[...] = cols[:, 1:2]
    choose_rows(back_ref, ((ca,), (cb,)), (pa, pb), cat)
    wide = hot(iota((HD, 2 * W), 0) == iota((HD, 2 * W), 1) // HD)
    weight = mm(wts_ref[...], wide)
    attended = weight[:, :W] * pa[...] + weight[:, W:] * pb[...]
    for u in range(0, U, 2):
        att_ref[:, u * C : (u + 2) * C, :] = jnp.concatenate(
            [
                attended[:, v * HD : (v + 1) * HD].reshape(N, C, HD)
                for v in (u, u + 1)
            ],
            axis=1,
        ).astype(BF)


def scale_body(wd_ref, a_ref, b_ref, out_hbm, out_ref, sem):
    per = N // PRODUCT_STEPS

    def store(i):
        at = pl.ds(i * per, per)
        return pltpu.make_async_copy(out_ref.at[at], out_hbm.at[at], sem.at[i])

    flat = wd_ref[...].astype(F32).reshape(C * N, HD)
    cols = jnp.transpose(flat)
    for i in range(PRODUCT_STEPS):
        for k in range(i * per, (i + 1) * per):
            w = cols[:, C * k : C * k + 1]
            delta = cols[:, C * k + 1 : C * k + 2]
            out_ref[k] = (
                w * (a_ref[k].astype(F32) - delta * b_ref[k].astype(F32)) * SCALE
            ).astype(BF)
        store(i).start()
    for i in range(PRODUCT_STEPS):
        store(i).wait()


def sum_body(terms_ref, att_ref, row_ref, out_ref, cat, acc, ca, cb):
    cols = jnp.transpose(row_ref[...])
    ca[...] = cols[:, 0:1]
    cb[...] = cols[:, 1:2]
    choose_rows(terms_ref, ((ca, cb),), (acc,), cat, 256)
    out_ref[:, : U * C, :] = att_ref[...]
    for u in range(0, U, 2):
        base = U * C + u * C
        out_ref[:, base : base + 2 * C, :] = jnp.concatenate(
            [acc[:, v * HD : (v + 1) * HD].reshape(N, C, HD) for v in (u, u + 1)], axis=1
        ).astype(BF)


def swap(rows):
    return lax.all_to_all(rows, "seq", split_axis=0, concat_axis=0, tiled=True)


HBM = pl.BlockSpec(memory_space=pltpu.HBM)
VMEM = pl.BlockSpec(memory_space=pltpu.VMEM)


def whole(*shape):
    return pl.BlockSpec(shape, lambda i: (0,) * len(shape))


def route(first, base):
    return call(
        functools.partial(route_body, base),
        (pltpu.HBM((N, U * S, HD), BF), sds((8, SPANS), F32)),
        in_specs=[VMEM],
        out_specs=(HBM, VMEM),
        scratch_shapes=[
            pltpu.VMEM((SPANS, W), BF),
            pltpu.VMEM((SLOTS // ROUTE_STEPS, SPANS), BF),
            pltpu.VMEM((N, U * S, HD), BF),
            pltpu.SemaphoreType.DMA((ROUTE_STEPS,)),
        ],
        flops=1.1e9,
    )(first)


def local(queries, out_grad, neighbours, placement):
    rows_in = 2 * U * C + C
    tokens = pltpu.VMEM(queries.shape, BF)
    first = swap(
        call(
            prep_body,
            pltpu.HBM((N, rows_in, HD), BF),
            in_specs=[HBM, HBM, HBM],
            out_specs=HBM,
            scratch_shapes=[
                tokens,
                tokens,
                pltpu.VMEM((2, C), jnp.int32),
                pltpu.VMEM((C, HD), F32),
                pltpu.VMEM((C * SPAN, C * SPAN), BF),
                pltpu.VMEM((N, rows_in, HD), BF),
                pltpu.SemaphoreType.DMA((3,)),
                pltpu.SemaphoreType.DMA((2,)),
            ],
            flops=5e8,
        )(in_hbm(queries), in_hbm(out_grad), in_hbm(placement.T))
    )
    square_sums = jnp.sum(jnp.square(neighbours.astype(F32)), axis=-1)
    row_scale = lax.rsqrt(lax.psum(square_sums, "head") / D + 1e-06)
    row_scale = jnp.pad(row_scale.T, ((0, 0), (0, HD - S)))

    first, row_scale = lax.optimization_barrier((first, row_scale))
    q_send, rowv = route(first, 0)
    got_q = swap(q_send)
    g_send = route(first, U * C)[0]
    got_g = swap(g_send)

    def cut(rows):
        return rows.reshape(N, U, S, HD)

    half_piece = pl.BlockSpec((N, U, HALF, HD), lambda i: (0, 0, i, 0))
    by_slot = lambda *tail: pl.BlockSpec((HALF, H // 2) + tail, lambda i: (i, 0, 0, 0))
    half_rows = pltpu.VMEM((N, U, HALF, HD), BF)
    diagonal = pltpu.VMEM((HALF, H // 2, 2 * SPAN, 2 * HD), BF)
    stat_acc = pltpu.VMEM((H // 2, 2 * SPAN, HD), F32)
    expo, keys, values, p_send, b_rows, stats = call(
        forward_body,
        (
            sds((S, H // 2, 2 * SPAN, R), F32),
            sds((S, H // 2, R, 2 * HD), BF),
            sds((S, H // 2, R, 2 * HD), BF),
            pltpu.HBM((N, U, S, HD), BF),
            pltpu.HBM((N, U, S, HD), BF),
            sds((N, C, HD), BF),
        ),
        grid=(2,),
        in_specs=[
            HBM,
            pl.BlockSpec((HALF, R, 2 * H * HD), lambda i: (i, 0, 0)),
            whole(R, HD),
        ],
        out_specs=(
            by_slot(2 * SPAN, R),
            by_slot(R, 2 * HD),
            by_slot(R, 2 * HD),
            half_piece,
            half_piece,
            whole(N, C, HD),
        ),
        scratch_shapes=[
            half_rows,
            diagonal,
            pltpu.VMEM((HALF, H, SPAN, 2 * HD), BF),
            stat_acc,
            stat_acc,
            pltpu.SemaphoreType.DMA,
        ],
        flops=2e9,
        nbytes=3e7,
        vmem=56,
    )(in_hbm(cut(got_q)), neighbours, row_scale)
    back_send = jnp.concatenate([p_send.reshape(N, U * S, HD), stats], axis=1)
    back_send, got_g = lax.optimization_barrier((back_send, got_g))
    back = swap(back_send)
    a_rows = call(
        backward_body,
        pltpu.HBM((N, U, S, HD), BF),
        grid=(2,),
        in_specs=[half_piece, by_slot(2 * SPAN, R), by_slot(R, 2 * HD), by_slot(R, 2 * HD)],
        out_specs=half_piece,
        scratch_shapes=[diagonal, pltpu.VMEM((HALF, H, SPAN, HD), BF)],
        flops=1e9,
        nbytes=2e7,
        vmem=48,
    )(cut(got_g), expo, keys, values)

    back, a_rows = lax.optimization_barrier((back, a_rows))
    span_table = pltpu.VMEM((SPANS, W), F32)
    column = pltpu.VMEM((SPANS, 1), F32)
    cat = pltpu.VMEM((SLOTS, W), BF)
    rows = sds((N, U * S, HD), BF)
    wd_send, wts, a_rows, b_rows = call(
        weight_body,
        (sds((N, C, HD), BF), sds((SPANS, HD), BF), rows, rows),
        in_specs=[VMEM, HBM, VMEM, HBM, HBM],
        scratch_shapes=[
            pltpu.VMEM((N, U * S, HD), BF),
            pltpu.VMEM((N * C, HD), F32),
            pltpu.SemaphoreType.DMA((PRODUCT_STEPS,)),
            pltpu.SemaphoreType.DMA((2,)),
        ],
    )(
        back,
        in_hbm(g_send),
        rowv,
        in_hbm(a_rows.reshape(N, U * S, HD)),
        in_hbm(b_rows.reshape(N, U * S, HD)),
    )
    wd = swap(wd_send)
    terms = call(
        scale_body,
        pltpu.HBM((N, U * S, HD), BF),
        in_specs=[VMEM, VMEM, VMEM],
        out_specs=HBM,
        scratch_shapes=[
            pltpu.VMEM((N, U * S, HD), BF),
            pltpu.SemaphoreType.DMA((PRODUCT_STEPS,)),
        ],
    )(wd, a_rows, b_rows)
    terms, wts = lax.optimization_barrier((terms, wts))
    attended = call(
        attended_body,
        sds((N, U * C, HD), BF),
        scratch_shapes=[cat, span_table, span_table, column, column],
        flops=2.2e9,
        vmem=40,
    )(in_hbm(back), rowv, wts)
    last = call(
        sum_body,
        sds((N, 2 * U * C, HD), BF),
        scratch_shapes=[cat, span_table, column, column],
        flops=1.1e9,
        vmem=48,
    )(swap(terms), attended, rowv)
    return call(
        final_body, (sds(queries.shape, BF), sds(queries.shape, BF)), flops=5e8
    )(swap(last))


def solution(mesh):
    in_specs = (P("seq", "head"), P("seq", "head"), P("seq", None, "head"), P("seq", None))
    out_specs = (P("seq", "head"), P("seq", "head"))
    return jax.shard_map(local, mesh=mesh, in_specs=in_specs, out_specs=out_specs, check_vma=False)
```

```python
import functools
import math

import jax
import jax.numpy as jnp
from jax import lax
from jax.experimental import pallas as pl
from jax.experimental.pallas import tpu as pltpu
from jax.sharding import PartitionSpec as P

D = 4096
HD = 128
SPAN = 64
R = 128
N = 64
C = 8
S = 32
H = 4
U = 4
TB = SPAN // U
W = U * HD
SPANS = N * C
SLOTS = N * S
HALF = S // 2
ROUTE_STEPS = 8
PRODUCT_STEPS = 8
SCALE = 1.0 / math.sqrt(HD)
BF = jnp.bfloat16
F32 = jnp.float32
MIB = 1 << 20


def iota(shape, dim):
    return lax.broadcasted_iota(jnp.int32, shape, dim)


def hot(mask):
    return jnp.where(mask, 1.0, 0.0).astype(BF)


def mm(a, b):
    return jnp.dot(a, b, preferred_element_type=F32)


def mm_t(a, b):
    return lax.dot_general(a, b, (((1,), (1,)), ((), ())), preferred_element_type=F32)


def t_mm(a, b):
    return lax.dot_general(a, b, (((0,), (0,)), ((), ())), preferred_element_type=F32)


def call(body, out_shape, flops=1e8, nbytes=4e6, vmem=40, **kw):
    return pl.pallas_call(
        body,
        out_shape=out_shape,
        compiler_params=pltpu.CompilerParams(vmem_limit_bytes=vmem * MIB),
        cost_estimate=pl.CostEstimate(
            flops=int(flops), bytes_accessed=int(nbytes), transcendentals=0
        ),
        **kw,
    )


def sds(shape, dtype):
    return jax.ShapeDtypeStruct(shape, dtype)


def token_row(piece_row):
    return (piece_row % C) * SPAN + ((piece_row // C) % U) * TB + piece_row // (U * C)


def prep_body(
    q_hbm, g_hbm, slot_hbm, out_hbm, q_ref, g_ref, slot_ref, table, order, stage, in_sem, out_sem
):
    size = C * SPAN
    loads = [
        pltpu.make_async_copy(src, dst, in_sem.at[i])
        for i, (src, dst) in enumerate(
            ((slot_hbm, slot_ref), (q_hbm, q_ref), (g_hbm, g_ref))
        )
    ]
    for load in loads:
        load.start()
    order[...] = hot(iota((size, size), 1) == token_row(iota((size, size), 0)))
    loads[0].wait()
    table[...] = jnp.zeros_like(table)
    table[0:2, 0:C] = (slot_ref[...] // S).astype(F32)
    table[2:4, 0:C] = (slot_ref[...] % S).astype(F32)
    digits = jnp.transpose(table[...])[:C]
    table[...] = jnp.zeros_like(table)
    table[:, 0:C] = digits
    stage[:, 2 * U * C :, :] = jnp.broadcast_to(table[...][None], (N, C, HD)).astype(BF)
    for load in loads[1:]:
        load.wait()
    stores = []
    half = H // 2
    for i in range(2):
        lanes = slice(i * half * HD, (i + 1) * half * HD)
        for base, ref in ((0, q_ref), (U * C, g_ref)):
            rows = mm(order[...], ref[:, lanes]).astype(BF)
            for j in range(half):
                h = i * half + j
                stage[h * TB : (h + 1) * TB, base : base + U * C, :] = rows[
                    :, j * HD : (j + 1) * HD
                ].reshape(TB, U * C, HD)
        part = pl.ds(i * half * TB, half * TB)
        stores.append(pltpu.make_async_copy(stage.at[part], out_hbm.at[part], out_sem.at[i]))
        stores[-1].start()
    for store in stores:
        store.wait()


def final_body(in_ref, att_ref, qg_ref):
    size = C * SPAN
    order = hot(iota((size, size), 0) == token_row(iota((size, size), 1)))
    for base, ref in ((0, att_ref), (U * C, qg_ref)):
        cat = jnp.concatenate(
            [
                in_ref[h * TB : (h + 1) * TB, base : base + U * C, :].reshape(size, HD)
                for h in range(H)
            ],
            axis=1,
        )
        ref[...] = mm(order, cat).astype(BF)


def span_rows(block):
    wide = block.astype(F32)
    return [wide[:, u * C : (u + 1) * C, :].reshape(SPANS, HD) for u in range(U)]


def route_body(base, first_ref, out_hbm, row_ref, x_ref, ids_ref, out_ref, out_sem):
    digits = first_ref[:, 2 * U * C :, :].astype(F32).reshape(SPANS, HD)
    lane = iota((SPANS, HD), 1)
    slot_part = pltpu.roll(digits, HD - 2, 1)
    cols = jnp.where(lane < 2, digits * float(S) + slot_part, 0.0)
    cols = cols + jnp.where((lane >= 2) & (lane < 6), pltpu.roll(digits, 2, 1), 0.0)
    rows = jnp.transpose(cols)[:8]
    row_ref[...] = rows
    for u, part in enumerate(span_rows(first_ref[:, base : base + U * C, :])):
        x_ref[:, u * HD : (u + 1) * HD] = part.astype(BF)
    per = N // ROUTE_STEPS
    slot_a = rows[0:1]
    slot_b = rows[1:2]

    def store(j):
        at = pl.ds(pl.multiple_of(j * per, per), per)
        return pltpu.make_async_copy(out_ref.at[at], out_hbm.at[at], out_sem.at[j])

    ids_ref[...] = iota((per * S, SPANS), 0).astype(F32).astype(BF)

    def step(j, _):
        first_id = (j * (per * S)).astype(F32)
        ids = ids_ref[...]
        hit = (ids == (slot_a - first_id).astype(BF)) | (ids == (slot_b - first_id).astype(BF))
        hit = jnp.where(hit, jnp.ones_like(ids), jnp.zeros_like(ids))
        got = mm(hit, x_ref[...]).astype(BF)
        at = pl.ds(pl.multiple_of(j * per, per), per)
        for u in range(U):
            out_ref[at, u * S : (u + 1) * S, :] = got[:, u * HD : (u + 1) * HD].reshape(
                per, S, HD
            )
        store(j).start()
        return 0

    lax.fori_loop(0, ROUTE_STEPS, step, 0)
    for j in range(ROUTE_STEPS):
        store(j).wait()


def swap_order():
    size = TB * HALF
    a, b = iota((size, size), 0), iota((size, size), 1)
    return hot((a // TB == b % TB) & (a % TB == b // TB))


def to_slots(order, src_ref, dst_ref):
    for h in range(H):
        pair, i = h // 2, h % 2
        for u in range(0, U, 2):
            block = jnp.concatenate(
                [
                    src_ref[h * TB : (h + 1) * TB, v, :, :].reshape(TB * HALF, HD)
                    for v in (u, u + 1)
                ],
                axis=1,
            )
            rows = mm(order, block).astype(BF)
            for j in range(2):
                lo = i * SPAN + (u + j) * TB
                dst_ref[:, pair, lo : lo + TB, i * HD : (i + 1) * HD] = rows[
                    :, j * HD : (j + 1) * HD
                ].reshape(HALF, TB, HD)


def in_hbm(rows):
    return pltpu.with_memory_space_constraint(rows, pltpu.HBM)


def load_half(src_hbm, dst_ref, sem):
    part = pl.ds(pl.multiple_of(pl.program_id(0) * HALF, HALF), HALF)
    return pltpu.make_async_copy(src_hbm.at[:, :, part, :], dst_ref, sem)


def forward_body(
    q_hbm, nb_ref, rs_ref, e_ref, k_ref, v_ref, p_ref, b_ref, stat_ref, q_ref, qs, pbs, tops, totals, sem
):
    step = pl.program_id(0)
    load = load_half(q_hbm, q_ref, sem)
    load.start()
    order = swap_order()

    @pl.when(step == 0)
    def _():
        tops[...] = jnp.zeros_like(tops)
        totals[...] = jnp.zeros_like(totals)
        qs[...] = jnp.zeros_like(qs)

    load.wait()
    to_slots(order, q_ref, qs)
    row = iota((2 * SPAN, HD), 0) % SPAN

    def slot(s, _):
        at = step * HALF + s
        scale = jnp.sum(
            jnp.where(iota((R, HD), 1) == at, rs_ref[...], 0.0), axis=1, keepdims=True
        )
        mark = iota((2 * SPAN, HD), 1) == (row // TB) * S + at
        for pair in range(H // 2):
            lo = 4 * pair * HD
            part = [
                nb_ref[s, :, lo + i * HD : lo + (i + 1) * HD].astype(F32) * scale
                for i in range(4)
            ]
            keys = [part[0].astype(BF), part[2].astype(BF)]
            key2 = jnp.concatenate(keys, axis=1)
            q2 = qs[s, pair]
            scores = mm_t(q2, key2) * SCALE
            split = scores.reshape(2, SPAN, R)
            cond = jnp.exp(split - jnp.max(split, axis=1, keepdims=True))
            cond = cond / jnp.sum(cond, axis=1, keepdims=True)
            cond = t_mm(cond.reshape(2 * SPAN, R).astype(BF), q2)
            values = [
                (part[2 * i + 1] + cond[:, i * HD : (i + 1) * HD]).astype(BF) for i in range(2)
            ]
            top = jnp.max(scores, axis=1, keepdims=True).astype(BF).astype(F32)
            expo = jnp.exp(scores - top)
            total = jnp.sum(expo, axis=1, keepdims=True)
            low = expo.astype(BF)
            e_ref[s, pair] = expo
            k_ref[s, pair] = key2
            v_ref[s, pair] = jnp.concatenate(values, axis=1)
            for i in range(2):
                pbs[s, 2 * pair + i] = mm(
                    low[i * SPAN : (i + 1) * SPAN], jnp.concatenate([values[i], keys[i]], axis=1)
                ).astype(BF)
            tops[pair] = jnp.where(mark, top, tops[pair])
            totals[pair] = jnp.where(mark, total, totals[pair])
        return 0

    lax.fori_loop(0, HALF, slot, 0, unroll=2)
    for h in range(H):
        for u in range(U):
            block = pbs[:, h, u * TB : (u + 1) * TB, :].reshape(HALF * TB, 2 * HD)
            rows = mm(order, block).astype(BF)
            for i, dst_ref in enumerate((p_ref, b_ref)):
                dst_ref[h * TB : (h + 1) * TB, u, :, :] = rows[
                    :, i * HD : (i + 1) * HD
                ].reshape(TB, HALF, HD)

    @pl.when(step == 1)
    def _():
        place = iota((TB, C, HD), 1)
        for h in range(H):
            lo = (h % 2) * SPAN
            rows = []
            for acc in (tops, totals):
                total = acc[h // 2, lo : lo + TB]
                for u in range(1, U):
                    total = total + acc[h // 2, lo + u * TB : lo + (u + 1) * TB]
                rows.append(total[:, None, :])
            stat_ref[h * TB : (h + 1) * TB] = jnp.where(
                place == 0, rows[0], jnp.where(place == 1, rows[1], 0.0)
            ).astype(BF)


def backward_body(g_ref, e_ref, k_ref, v_ref, a_ref, gs, as_):
    order = swap_order()

    @pl.when(pl.program_id(0) == 0)
    def _():
        gs[...] = jnp.zeros_like(gs)

    to_slots(order, g_ref, gs)

    def slot(s, _):
        for pair in range(H // 2):
            grad = mm_t(gs[s, pair], v_ref[s, pair])
            both = mm((e_ref[s, pair] * grad).astype(BF), k_ref[s, pair]).astype(BF)
            for i in range(2):
                as_[s, 2 * pair + i] = both[i * SPAN : (i + 1) * SPAN, i * HD : (i + 1) * HD]
        return 0

    lax.fori_loop(0, HALF, slot, 0, unroll=2)
    for h in range(H):
        for u in range(0, U, 2):
            block = jnp.concatenate(
                [
                    as_[:, h, v * TB : (v + 1) * TB, :].reshape(HALF * TB, HD)
                    for v in (u, u + 1)
                ],
                axis=1,
            )
            rows = mm(order, block).astype(BF)
            for j in range(2):
                a_ref[h * TB : (h + 1) * TB, u + j, :, :] = rows[
                    :, j * HD : (j + 1) * HD
                ].reshape(TB, HALF, HD)


def choose_rows(in_ref, picks, out_refs, cat_ref, size=128):
    for u in range(U):
        cat_ref[:, u * HD : (u + 1) * HD] = in_ref[:, u * S : (u + 1) * S, :].reshape(SLOTS, HD)
    for cols, out_ref in zip(picks, out_refs):

        def step(i, _, cols=cols, out_ref=out_ref):
            at = pl.ds(pl.multiple_of(i * size, size), size)
            ids = iota((size, SLOTS), 1).astype(F32)
            mask = ids == cols[0][at, :]
            for col in cols[1:]:
                mask = mask | (ids == col[at, :])
            out_ref[at, :] = mm(hot(mask), cat_ref[...])
            return 0

        lax.fori_loop(0, SPANS // size, step, 0)


def weight_body(
    back_ref, g_hbm, row_ref, a_hbm, b_hbm, wd_ref, wts_ref, a_ref, b_ref, g_ref, flat, in_sem, sem
):
    size = U * S
    per = N // PRODUCT_STEPS

    def load(i):
        at = pl.ds(i * per, per)
        return pltpu.make_async_copy(g_hbm.at[at], g_ref.at[at], in_sem.at[i])

    later = [
        pltpu.make_async_copy(src, dst, sem.at[i])
        for i, (src, dst) in enumerate(((a_hbm, a_ref), (b_hbm, b_ref)))
    ]
    for i in range(PRODUCT_STEPS):
        load(i).start()
    cols = jnp.transpose(row_ref[...])
    lane = iota((SPANS, HD), 1)
    slot_lane = (iota((SPANS, 2 * HD), 1) % S).astype(F32)
    owner = [hot(iota((SPANS, N), 1).astype(F32) == cols[:, 2 + n : 3 + n]) for n in range(2)]

    def span_stats(first, lanes):
        rows = jnp.concatenate(
            [flat[pl.ds(first + i, N, stride=C), :].astype(BF) for i in range(2)], axis=1
        )
        row, col = iota((2 * HD, HD), 0), iota((2 * HD, HD), 1)
        group = hot(lanes * (row // HD) + row % HD // S == col)
        out = []
        for n in range(2):
            got = mm(owner[n], rows)
            got = jnp.where(slot_lane == cols[:, 4 + n : 5 + n], got, 0.0).astype(BF)
            out.append(mm(got, group))
        return out

    for j in range(N):
        flat[j * C : (j + 1) * C, :] = back_ref[j, size:, :].astype(F32)
    tops = span_stats(0, U)
    totals = [pltpu.roll(rows, HD - U, 1) for rows in tops]
    highest = jnp.maximum(tops[0], tops[1])
    factor = [jnp.exp(t - highest) for t in tops]
    denominator = factor[0] * totals[0] + factor[1] * totals[1]
    low = [jnp.where(lane < U, f / denominator, 0.0).astype(BF).astype(F32) for f in factor]
    wts_ref[...] = (low[0] + pltpu.roll(low[1], U, 1)).astype(BF)
    diagonal = iota((size, HD), 0) == iota((size, HD), 1)
    place = iota((C, HD), 0)
    for i in range(PRODUCT_STEPS):
        load(i).wait()
        if i == PRODUCT_STEPS // 2:
            for copy in later:
                copy.start()
        for j in range(i * per, (i + 1) * per):
            prod = back_ref[j, :size, :].astype(F32) * g_ref[j].astype(F32)
            prod = jnp.where(diagonal, jnp.sum(prod, axis=1, keepdims=True), 0.0)
            total = jnp.sum(prod, axis=0, keepdims=True)
            high = total.astype(BF).astype(F32)
            flat[j * C : (j + 1) * C, :] = jnp.where(place == 2, high, total - high)
    products = span_stats(2, 0)
    delta = jnp.where(lane < U, low[0] * products[0] + low[1] * products[1], 0.0)
    delta = pltpu.roll(delta, U, 1)
    spread = hot(iota((HD, 2 * HD), 0) == iota((HD, 2 * HD), 1) // S)
    out = jnp.zeros((N, 2 * HD), F32)
    for n in range(2):
        rows = mm((low[n] + delta).astype(BF), spread)
        rows = jnp.where(slot_lane == cols[:, 4 + n : 5 + n], rows, 0.0)
        owners = hot(iota((N, SPANS), 0).astype(F32) == row_ref[2 + n : 3 + n, :])
        out = out + mm(owners, rows.astype(BF))
    place = iota((N, 2, HD), 1)
    wd_ref[...] = jnp.where(place == 0, out[:, None, :HD], out[:, None, HD:]).astype(BF)
    for copy in later:
        copy.wait()


def attended_body(
    back_ref, row_ref, wts_ref, att_ref, cat, pa, pb, ca, cb
):
    cols = jnp.transpose(row_ref[...])
    ca[...] = cols[:, 0:1]
    cb[...] = cols[:, 1:2]
    choose_rows(back_ref, ((ca,), (cb,)), (pa, pb), cat)
    wide = hot(iota((HD, 2 * W), 0) == iota((HD, 2 * W), 1) // HD)
    weight = mm(wts_ref[...], wide)
    attended = weight[:, :W] * pa[...] + weight[:, W:] * pb[...]
    for u in range(0, U, 2):
        att_ref[:, u * C : (u + 2) * C, :] = jnp.concatenate(
            [
                attended[:, v * HD : (v + 1) * HD].reshape(N, C, HD)
                for v in (u, u + 1)
            ],
            axis=1,
        ).astype(BF)


def scale_body(wd_ref, a_ref, b_ref, out_hbm, out_ref, sem):
    per = N // PRODUCT_STEPS

    def store(i):
        at = pl.ds(i * per, per)
        return pltpu.make_async_copy(out_ref.at[at], out_hbm.at[at], sem.at[i])

    flat = wd_ref[...].astype(F32).reshape(2 * N, HD)
    cols = jnp.transpose(flat)
    for i in range(PRODUCT_STEPS):
        for k in range(i * per, (i + 1) * per):
            w = cols[:, 2 * k : 2 * k + 1]
            delta = cols[:, 2 * k + 1 : 2 * k + 2]
            out_ref[k] = (
                w * (a_ref[k].astype(F32) - delta * b_ref[k].astype(F32)) * SCALE
            ).astype(BF)
        store(i).start()
    for i in range(PRODUCT_STEPS):
        store(i).wait()


def sum_body(terms_ref, att_ref, row_ref, out_ref, cat, acc, ca, cb):
    cols = jnp.transpose(row_ref[...])
    ca[...] = cols[:, 0:1]
    cb[...] = cols[:, 1:2]
    choose_rows(terms_ref, ((ca, cb),), (acc,), cat, 256)
    out_ref[:, : U * C, :] = att_ref[...]
    for u in range(0, U, 2):
        base = U * C + u * C
        out_ref[:, base : base + 2 * C, :] = jnp.concatenate(
            [acc[:, v * HD : (v + 1) * HD].reshape(N, C, HD) for v in (u, u + 1)], axis=1
        ).astype(BF)


def swap(rows):
    return lax.all_to_all(rows, "seq", split_axis=0, concat_axis=0, tiled=True)


HBM = pl.BlockSpec(memory_space=pltpu.HBM)
VMEM = pl.BlockSpec(memory_space=pltpu.VMEM)


def whole(*shape):
    return pl.BlockSpec(shape, lambda i: (0,) * len(shape))


def route(first, base):
    return call(
        functools.partial(route_body, base),
        (pltpu.HBM((N, U * S, HD), BF), sds((8, SPANS), F32)),
        in_specs=[VMEM],
        out_specs=(HBM, VMEM),
        scratch_shapes=[
            pltpu.VMEM((SPANS, W), BF),
            pltpu.VMEM((SLOTS // ROUTE_STEPS, SPANS), BF),
            pltpu.VMEM((N, U * S, HD), BF),
            pltpu.SemaphoreType.DMA((ROUTE_STEPS,)),
        ],
        flops=1.1e9,
    )(first)


def local(queries, out_grad, neighbours, placement):
    rows_in = 2 * U * C + C
    tokens = pltpu.VMEM(queries.shape, BF)
    first = swap(
        call(
            prep_body,
            pltpu.HBM((N, rows_in, HD), BF),
            in_specs=[HBM, HBM, HBM],
            out_specs=HBM,
            scratch_shapes=[
                tokens,
                tokens,
                pltpu.VMEM((2, C), jnp.int32),
                pltpu.VMEM((C, HD), F32),
                pltpu.VMEM((C * SPAN, C * SPAN), BF),
                pltpu.VMEM((N, rows_in, HD), BF),
                pltpu.SemaphoreType.DMA((3,)),
                pltpu.SemaphoreType.DMA((2,)),
            ],
            flops=5e8,
        )(in_hbm(queries), in_hbm(out_grad), in_hbm(placement.T))
    )
    square_sums = jnp.sum(jnp.square(neighbours.astype(F32)), axis=-1)
    row_scale = lax.rsqrt(lax.psum(square_sums, "head") / D + 1e-06)
    row_scale = jnp.pad(row_scale.T, ((0, 0), (0, HD - S)))

    first, row_scale = lax.optimization_barrier((first, row_scale))
    q_send, rowv = route(first, 0)
    got_q = swap(q_send)
    g_send = route(first, U * C)[0]
    got_g = swap(g_send)

    def cut(rows):
        return rows.reshape(N, U, S, HD)

    half_piece = pl.BlockSpec((N, U, HALF, HD), lambda i: (0, 0, i, 0))
    by_slot = lambda *tail: pl.BlockSpec((HALF, H // 2) + tail, lambda i: (i, 0, 0, 0))
    half_rows = pltpu.VMEM((N, U, HALF, HD), BF)
    diagonal = pltpu.VMEM((HALF, H // 2, 2 * SPAN, 2 * HD), BF)
    stat_acc = pltpu.VMEM((H // 2, 2 * SPAN, HD), F32)
    expo, keys, values, p_send, b_rows, stats = call(
        forward_body,
        (
            sds((S, H // 2, 2 * SPAN, R), F32),
            sds((S, H // 2, R, 2 * HD), BF),
            sds((S, H // 2, R, 2 * HD), BF),
            pltpu.HBM((N, U, S, HD), BF),
            pltpu.HBM((N, U, S, HD), BF),
            sds((N, C, HD), BF),
        ),
        grid=(2,),
        in_specs=[
            HBM,
            pl.BlockSpec((HALF, R, 2 * H * HD), lambda i: (i, 0, 0)),
            whole(R, HD),
        ],
        out_specs=(
            by_slot(2 * SPAN, R),
            by_slot(R, 2 * HD),
            by_slot(R, 2 * HD),
            half_piece,
            half_piece,
            whole(N, C, HD),
        ),
        scratch_shapes=[
            half_rows,
            diagonal,
            pltpu.VMEM((HALF, H, SPAN, 2 * HD), BF),
            stat_acc,
            stat_acc,
            pltpu.SemaphoreType.DMA,
        ],
        flops=2e9,
        nbytes=3e7,
        vmem=56,
    )(in_hbm(cut(got_q)), neighbours, row_scale)
    back_send = jnp.concatenate([p_send.reshape(N, U * S, HD), stats], axis=1)
    back_send, got_g = lax.optimization_barrier((back_send, got_g))
    back = swap(back_send)
    a_rows = call(
        backward_body,
        pltpu.HBM((N, U, S, HD), BF),
        grid=(2,),
        in_specs=[half_piece, by_slot(2 * SPAN, R), by_slot(R, 2 * HD), by_slot(R, 2 * HD)],
        out_specs=half_piece,
        scratch_shapes=[diagonal, pltpu.VMEM((HALF, H, SPAN, HD), BF)],
        flops=1e9,
        nbytes=2e7,
        vmem=48,
    )(cut(got_g), expo, keys, values)

    back, a_rows = lax.optimization_barrier((back, a_rows))
    span_table = pltpu.VMEM((SPANS, W), F32)
    column = pltpu.VMEM((SPANS, 1), F32)
    cat = pltpu.VMEM((SLOTS, W), BF)
    rows = sds((N, U * S, HD), BF)
    wd_send, wts, a_rows, b_rows = call(
        weight_body,
        (sds((N, 2, HD), BF), sds((SPANS, HD), BF), rows, rows),
        in_specs=[VMEM, HBM, VMEM, HBM, HBM],
        scratch_shapes=[
            pltpu.VMEM((N, U * S, HD), BF),
            pltpu.VMEM((N * C, HD), F32),
            pltpu.SemaphoreType.DMA((PRODUCT_STEPS,)),
            pltpu.SemaphoreType.DMA((2,)),
        ],
    )(
        back,
        in_hbm(g_send),
        rowv,
        in_hbm(a_rows.reshape(N, U * S, HD)),
        in_hbm(b_rows.reshape(N, U * S, HD)),
    )
    wd = swap(wd_send)
    terms = call(
        scale_body,
        pltpu.HBM((N, U * S, HD), BF),
        in_specs=[VMEM, VMEM, VMEM],
        out_specs=HBM,
        scratch_shapes=[
            pltpu.VMEM((N, U * S, HD), BF),
            pltpu.SemaphoreType.DMA((PRODUCT_STEPS,)),
        ],
    )(wd, a_rows, b_rows)
    terms, wts = lax.optimization_barrier((terms, wts))
    attended = call(
        attended_body,
        sds((N, U * C, HD), BF),
        scratch_shapes=[cat, span_table, span_table, column, column],
        flops=2.2e9,
        vmem=40,
    )(in_hbm(back), rowv, wts)
    last = call(
        sum_body,
        sds((N, 2 * U * C, HD), BF),
        scratch_shapes=[cat, span_table, column, column],
        flops=1.1e9,
        vmem=48,
    )(swap(terms), attended, rowv)
    return call(
        final_body, (sds(queries.shape, BF), sds(queries.shape, BF)), flops=5e8
    )(swap(last))


def solution(mesh):
    in_specs = (P("seq", "head"), P("seq", "head"), P("seq", None, "head"), P("seq", None))
    out_specs = (P("seq", "head"), P("seq", "head"))
    return jax.shard_map(local, mesh=mesh, in_specs=in_specs, out_specs=out_specs, check_vma=False)
```

```python
import functools
import math

import jax
import jax.numpy as jnp
from jax import lax
from jax.experimental import pallas as pl
from jax.experimental.pallas import tpu as pltpu
from jax.sharding import PartitionSpec as P

D = 4096
HD = 128
SPAN = 64
R = 128
N = 64
C = 8
S = 32
H = 4
U = 4
TB = SPAN // U
W = U * HD
SPANS = N * C
SLOTS = N * S
HALF = S // 2
ROUTE_STEPS = 8
PRODUCT_STEPS = 8
SCALE = 1.0 / math.sqrt(HD)
BF = jnp.bfloat16
F32 = jnp.float32
MIB = 1 << 20


def iota(shape, dim):
    return lax.broadcasted_iota(jnp.int32, shape, dim)


def hot(mask):
    return jnp.where(mask, 1.0, 0.0).astype(BF)


def mm(a, b):
    return jnp.dot(a, b, preferred_element_type=F32)


def mm_t(a, b):
    return lax.dot_general(a, b, (((1,), (1,)), ((), ())), preferred_element_type=F32)


def t_mm(a, b):
    return lax.dot_general(a, b, (((0,), (0,)), ((), ())), preferred_element_type=F32)


def call(body, out_shape, flops=1e8, nbytes=4e6, vmem=40, **kw):
    return pl.pallas_call(
        body,
        out_shape=out_shape,
        compiler_params=pltpu.CompilerParams(vmem_limit_bytes=vmem * MIB),
        cost_estimate=pl.CostEstimate(
            flops=int(flops), bytes_accessed=int(nbytes), transcendentals=0
        ),
        **kw,
    )


def sds(shape, dtype):
    return jax.ShapeDtypeStruct(shape, dtype)


def token_row(piece_row):
    return (piece_row % C) * SPAN + ((piece_row // C) % U) * TB + piece_row // (U * C)


def prep_body(
    q_hbm, g_hbm, slot_hbm, out_hbm, q_ref, g_ref, slot_ref, table, order, stage, in_sem, out_sem
):
    size = C * SPAN
    loads = [
        pltpu.make_async_copy(src, dst, in_sem.at[i])
        for i, (src, dst) in enumerate(
            ((slot_hbm, slot_ref), (q_hbm, q_ref), (g_hbm, g_ref))
        )
    ]
    for load in loads:
        load.start()
    order[...] = hot(iota((size, size), 1) == token_row(iota((size, size), 0)))
    loads[0].wait()
    table[...] = jnp.zeros_like(table)
    table[0:2, 0:C] = (slot_ref[...] // S).astype(F32)
    table[2:4, 0:C] = (slot_ref[...] % S).astype(F32)
    digits = jnp.transpose(table[...])[:C]
    table[...] = jnp.zeros_like(table)
    table[:, 0:C] = digits
    stage[:, 2 * U * C :, :] = jnp.broadcast_to(table[...][None], (N, C, HD)).astype(BF)
    for load in loads[1:]:
        load.wait()
    stores = []
    half = H // 2
    for i in range(2):
        lanes = slice(i * half * HD, (i + 1) * half * HD)
        for base, ref in ((0, q_ref), (U * C, g_ref)):
            rows = mm(order[...], ref[:, lanes]).astype(BF)
            for j in range(half):
                h = i * half + j
                stage[h * TB : (h + 1) * TB, base : base + U * C, :] = rows[
                    :, j * HD : (j + 1) * HD
                ].reshape(TB, U * C, HD)
        part = pl.ds(i * half * TB, half * TB)
        stores.append(pltpu.make_async_copy(stage.at[part], out_hbm.at[part], out_sem.at[i]))
        stores[-1].start()
    for store in stores:
        store.wait()


def final_body(in_ref, att_ref, qg_ref):
    size = C * SPAN
    order = hot(iota((size, size), 0) == token_row(iota((size, size), 1)))
    for base, ref in ((0, att_ref), (U * C, qg_ref)):
        cat = jnp.concatenate(
            [
                in_ref[h * TB : (h + 1) * TB, base : base + U * C, :].reshape(size, HD)
                for h in range(H)
            ],
            axis=1,
        )
        ref[...] = mm(order, cat).astype(BF)


def span_rows(block):
    wide = block.astype(F32)
    return [wide[:, u * C : (u + 1) * C, :].reshape(SPANS, HD) for u in range(U)]


def route_body(base, first_ref, out_hbm, row_ref, x_ref, ids_ref, out_ref, out_sem):
    digits = first_ref[:, 2 * U * C :, :].astype(F32).reshape(SPANS, HD)
    lane = iota((SPANS, HD), 1)
    slot_part = pltpu.roll(digits, HD - 2, 1)
    cols = jnp.where(lane < 2, digits * float(S) + slot_part, 0.0)
    cols = cols + jnp.where((lane >= 2) & (lane < 6), pltpu.roll(digits, 2, 1), 0.0)
    rows = jnp.transpose(cols)[:8]
    row_ref[...] = rows
    for u, part in enumerate(span_rows(first_ref[:, base : base + U * C, :])):
        x_ref[:, u * HD : (u + 1) * HD] = part.astype(BF)
    per = N // ROUTE_STEPS
    slot_a = rows[0:1]
    slot_b = rows[1:2]

    def store(j):
        at = pl.ds(pl.multiple_of(j * per, per), per)
        return pltpu.make_async_copy(out_ref.at[at], out_hbm.at[at], out_sem.at[j])

    ids_ref[...] = iota((per * S, SPANS), 0).astype(F32).astype(BF)

    def step(j, _):
        first_id = (j * (per * S)).astype(F32)
        ids = ids_ref[...]
        hit = (ids == (slot_a - first_id).astype(BF)) | (ids == (slot_b - first_id).astype(BF))
        hit = jnp.where(hit, jnp.ones_like(ids), jnp.zeros_like(ids))
        got = mm(hit, x_ref[...]).astype(BF)
        at = pl.ds(pl.multiple_of(j * per, per), per)
        for u in range(U):
            out_ref[at, u * S : (u + 1) * S, :] = got[:, u * HD : (u + 1) * HD].reshape(
                per, S, HD
            )
        store(j).start()
        return 0

    lax.fori_loop(0, ROUTE_STEPS, step, 0)
    for j in range(ROUTE_STEPS):
        store(j).wait()


def swap_order():
    size = TB * HALF
    a, b = iota((size, size), 0), iota((size, size), 1)
    return hot((a // TB == b % TB) & (a % TB == b // TB))


def to_slots(order, src_ref, dst_ref):
    for h in range(H):
        pair, i = h // 2, h % 2
        for u in range(0, U, 2):
            block = jnp.concatenate(
                [
                    src_ref[h * TB : (h + 1) * TB, v, :, :].reshape(TB * HALF, HD)
                    for v in (u, u + 1)
                ],
                axis=1,
            )
            rows = mm(order, block).astype(BF)
            for j in range(2):
                lo = i * SPAN + (u + j) * TB
                dst_ref[:, pair, lo : lo + TB, i * HD : (i + 1) * HD] = rows[
                    :, j * HD : (j + 1) * HD
                ].reshape(HALF, TB, HD)


def in_hbm(rows):
    return pltpu.with_memory_space_constraint(rows, pltpu.HBM)


def load_half(src_hbm, dst_ref, sem):
    part = pl.ds(pl.multiple_of(pl.program_id(0) * HALF, HALF), HALF)
    return pltpu.make_async_copy(src_hbm.at[:, :, part, :], dst_ref, sem)


def forward_body(
    q_hbm, nb_ref, rs_ref, e_ref, k_ref, v_ref, p_ref, b_ref, stat_ref, q_ref, qs, pbs, tops, totals, sem
):
    step = pl.program_id(0)
    load = load_half(q_hbm, q_ref, sem)
    load.start()
    order = swap_order()

    @pl.when(step == 0)
    def _():
        tops[...] = jnp.zeros_like(tops)
        totals[...] = jnp.zeros_like(totals)
        qs[...] = jnp.zeros_like(qs)

    load.wait()
    to_slots(order, q_ref, qs)
    row = iota((2 * SPAN, HD), 0) % SPAN

    def slot(s, _):
        at = step * HALF + s
        scale = jnp.sum(
            jnp.where(iota((R, HD), 1) == at, rs_ref[...], 0.0), axis=1, keepdims=True
        )
        mark = iota((2 * SPAN, HD), 1) == (row // TB) * S + at
        for pair in range(H // 2):
            lo = 4 * pair * HD
            part = [
                nb_ref[s, :, lo + i * HD : lo + (i + 1) * HD].astype(F32) * scale
                for i in range(4)
            ]
            keys = [part[0].astype(BF), part[2].astype(BF)]
            key2 = jnp.concatenate(keys, axis=1)
            q2 = qs[s, pair]
            scores = mm_t(q2, key2) * SCALE
            split = scores.reshape(2, SPAN, R)
            cond = jnp.exp(split - jnp.max(split, axis=1, keepdims=True))
            cond = cond / jnp.sum(cond, axis=1, keepdims=True)
            cond = t_mm(cond.reshape(2 * SPAN, R).astype(BF), q2)
            values = [
                (part[2 * i + 1] + cond[:, i * HD : (i + 1) * HD]).astype(BF) for i in range(2)
            ]
            top = jnp.max(scores, axis=1, keepdims=True).astype(BF).astype(F32)
            expo = jnp.exp(scores - top)
            total = jnp.sum(expo, axis=1, keepdims=True)
            low = expo.astype(BF)
            e_ref[s, pair] = expo
            k_ref[s, pair] = key2
            v_ref[s, pair] = jnp.concatenate(values, axis=1)
            for i in range(2):
                pbs[s, 2 * pair + i] = mm(
                    low[i * SPAN : (i + 1) * SPAN], jnp.concatenate([values[i], keys[i]], axis=1)
                ).astype(BF)
            tops[pair] = jnp.where(mark, top, tops[pair])
            totals[pair] = jnp.where(mark, total, totals[pair])
        return 0

    lax.fori_loop(0, HALF, slot, 0, unroll=2)
    for h in range(H):
        for u in range(U):
            block = pbs[:, h, u * TB : (u + 1) * TB, :].reshape(HALF * TB, 2 * HD)
            rows = mm(order, block).astype(BF)
            for i, dst_ref in enumerate((p_ref, b_ref)):
                dst_ref[h * TB : (h + 1) * TB, u, :, :] = rows[
                    :, i * HD : (i + 1) * HD
                ].reshape(TB, HALF, HD)

    @pl.when(step == 1)
    def _():
        place = iota((TB, C, HD), 1)
        for h in range(H):
            lo = (h % 2) * SPAN
            rows = []
            for acc in (tops, totals):
                total = acc[h // 2, lo : lo + TB]
                for u in range(1, U):
                    total = total + acc[h // 2, lo + u * TB : lo + (u + 1) * TB]
                rows.append(total[:, None, :])
            stat_ref[h * TB : (h + 1) * TB] = jnp.where(
                place == 0, rows[0], jnp.where(place == 1, rows[1], 0.0)
            ).astype(BF)


def backward_body(g_ref, e_ref, k_ref, v_ref, a_ref, gs, as_):
    order = swap_order()

    @pl.when(pl.program_id(0) == 0)
    def _():
        gs[...] = jnp.zeros_like(gs)

    to_slots(order, g_ref, gs)

    def slot(s, _):
        for pair in range(H // 2):
            grad = mm_t(gs[s, pair], v_ref[s, pair])
            both = mm((e_ref[s, pair] * grad).astype(BF), k_ref[s, pair]).astype(BF)
            for i in range(2):
                as_[s, 2 * pair + i] = both[i * SPAN : (i + 1) * SPAN, i * HD : (i + 1) * HD]
        return 0

    lax.fori_loop(0, HALF, slot, 0, unroll=2)
    for h in range(H):
        for u in range(0, U, 2):
            block = jnp.concatenate(
                [
                    as_[:, h, v * TB : (v + 1) * TB, :].reshape(HALF * TB, HD)
                    for v in (u, u + 1)
                ],
                axis=1,
            )
            rows = mm(order, block).astype(BF)
            for j in range(2):
                a_ref[h * TB : (h + 1) * TB, u + j, :, :] = rows[
                    :, j * HD : (j + 1) * HD
                ].reshape(TB, HALF, HD)


def choose_rows(in_ref, picks, out_refs, cat_ref, size=128):
    for u in range(U):
        cat_ref[:, u * HD : (u + 1) * HD] = in_ref[:, u * S : (u + 1) * S, :].reshape(SLOTS, HD)
    for cols, out_ref in zip(picks, out_refs):

        def step(i, _, cols=cols, out_ref=out_ref):
            at = pl.ds(pl.multiple_of(i * size, size), size)
            ids = iota((size, SLOTS), 1).astype(F32)
            mask = ids == cols[0][at, :]
            for col in cols[1:]:
                mask = mask | (ids == col[at, :])
            out_ref[at, :] = mm(hot(mask), cat_ref[...])
            return 0

        lax.fori_loop(0, SPANS // size, step, 0)


def weight_body(
    back_ref, g_hbm, row_ref, a_hbm, b_hbm, wd_ref, wts_ref, a_ref, b_ref, g_ref, flat, in_sem, sem
):
    size = U * S
    per = N // PRODUCT_STEPS

    def load(i):
        at = pl.ds(i * per, per)
        return pltpu.make_async_copy(g_hbm.at[at], g_ref.at[at], in_sem.at[i])

    later = [
        pltpu.make_async_copy(src, dst, sem.at[i])
        for i, (src, dst) in enumerate(((a_hbm, a_ref), (b_hbm, b_ref)))
    ]
    for i in range(PRODUCT_STEPS):
        load(i).start()
    cols = jnp.transpose(row_ref[...])
    lane = iota((SPANS, HD), 1)
    slot_lane = (iota((SPANS, 2 * HD), 1) % S).astype(F32)
    owner = [hot(iota((SPANS, N), 1).astype(F32) == cols[:, 2 + n : 3 + n]) for n in range(2)]

    def span_stats(first, lanes):
        rows = jnp.concatenate(
            [flat[pl.ds(first + i, N, stride=C), :].astype(BF) for i in range(2)], axis=1
        )
        row, col = iota((2 * HD, HD), 0), iota((2 * HD, HD), 1)
        group = hot(lanes * (row // HD) + row % HD // S == col)
        out = []
        for n in range(2):
            got = mm(owner[n], rows)
            got = jnp.where(slot_lane == cols[:, 4 + n : 5 + n], got, 0.0).astype(BF)
            out.append(mm(got, group))
        return out

    for j in range(N):
        flat[j * C : (j + 1) * C, :] = back_ref[j, size:, :].astype(F32)
    tops = span_stats(0, U)
    totals = [pltpu.roll(rows, HD - U, 1) for rows in tops]
    highest = jnp.maximum(tops[0], tops[1])
    factor = [jnp.exp(t - highest) for t in tops]
    denominator = factor[0] * totals[0] + factor[1] * totals[1]
    low = [jnp.where(lane < U, f / denominator, 0.0).astype(BF).astype(F32) for f in factor]
    wts_ref[...] = (low[0] + pltpu.roll(low[1], U, 1)).astype(BF)
    diagonal = iota((size, HD), 0) == iota((size, HD), 1)
    place = iota((C, HD), 0)
    for i in range(PRODUCT_STEPS):
        load(i).wait()
        if i == PRODUCT_STEPS // 2:
            for copy in later:
                copy.start()
        for j in range(i * per, (i + 1) * per):
            prod = back_ref[j, :size, :].astype(F32) * g_ref[j].astype(F32)
            prod = jnp.where(diagonal, jnp.sum(prod, axis=1, keepdims=True), 0.0)
            total = jnp.sum(prod, axis=0, keepdims=True)
            high = total.astype(BF).astype(F32)
            flat[j * C : (j + 1) * C, :] = jnp.where(place == 2, high, total - high)
    products = span_stats(2, 0)
    delta = jnp.where(lane < U, low[0] * products[0] + low[1] * products[1], 0.0)
    delta = pltpu.roll(delta, U, 1)
    spread = hot(iota((HD, 2 * HD), 0) == iota((HD, 2 * HD), 1) // S)
    out = jnp.zeros((N, 2 * HD), F32)
    for n in range(2):
        rows = mm((low[n] + delta).astype(BF), spread)
        rows = jnp.where(slot_lane == cols[:, 4 + n : 5 + n], rows, 0.0)
        owners = hot(iota((N, SPANS), 0).astype(F32) == row_ref[2 + n : 3 + n, :])
        out = out + mm(owners, rows.astype(BF))
    place = iota((N, C, HD), 1)
    wd_ref[...] = jnp.where(
        place == 0, out[:, None, :HD], jnp.where(place == 1, out[:, None, HD:], 0.0)
    ).astype(BF)
    for copy in later:
        copy.wait()


def attended_body(
    back_ref, row_ref, wts_ref, att_ref, cat, pa, pb, ca, cb
):
    cols = jnp.transpose(row_ref[...])
    ca[...] = cols[:, 0:1]
    cb[...] = cols[:, 1:2]
    choose_rows(back_ref, ((ca,), (cb,)), (pa, pb), cat)
    wide = hot(iota((HD, 2 * W), 0) == iota((HD, 2 * W), 1) // HD)
    weight = mm(wts_ref[...], wide)
    attended = weight[:, :W] * pa[...] + weight[:, W:] * pb[...]
    for u in range(0, U, 2):
        att_ref[:, u * C : (u + 2) * C, :] = jnp.concatenate(
            [
                attended[:, v * HD : (v + 1) * HD].reshape(N, C, HD)
                for v in (u, u + 1)
            ],
            axis=1,
        ).astype(BF)


def scale_body(wd_ref, a_ref, b_ref, out_hbm, out_ref, sem):
    per = N // PRODUCT_STEPS

    def store(i):
        at = pl.ds(i * per, per)
        return pltpu.make_async_copy(out_ref.at[at], out_hbm.at[at], sem.at[i])

    flat = wd_ref[...].astype(F32).reshape(C * N, HD)
    cols = jnp.transpose(flat)
    for i in range(PRODUCT_STEPS):
        for k in range(i * per, (i + 1) * per):
            w = cols[:, C * k : C * k + 1]
            delta = cols[:, C * k + 1 : C * k + 2]
            out_ref[k] = (
                w * (a_ref[k].astype(F32) - delta * b_ref[k].astype(F32)) * SCALE
            ).astype(BF)
        store(i).start()
    for i in range(PRODUCT_STEPS):
        store(i).wait()


def sum_body(terms_ref, att_ref, row_ref, out_ref, cat, acc, ca, cb):
    cols = jnp.transpose(row_ref[...])
    ca[...] = cols[:, 0:1]
    cb[...] = cols[:, 1:2]
    choose_rows(terms_ref, ((ca, cb),), (acc,), cat, 256)
    out_ref[:, : U * C, :] = att_ref[...]
    for u in range(0, U, 2):
        base = U * C + u * C
        out_ref[:, base : base + 2 * C, :] = jnp.concatenate(
            [acc[:, v * HD : (v + 1) * HD].reshape(N, C, HD) for v in (u, u + 1)], axis=1
        ).astype(BF)


def swap(rows):
    return lax.all_to_all(rows, "seq", split_axis=0, concat_axis=0, tiled=True)


HBM = pl.BlockSpec(memory_space=pltpu.HBM)
VMEM = pl.BlockSpec(memory_space=pltpu.VMEM)


def whole(*shape):
    return pl.BlockSpec(shape, lambda i: (0,) * len(shape))


def route(first, base):
    return call(
        functools.partial(route_body, base),
        (pltpu.HBM((N, U * S, HD), BF), sds((8, SPANS), F32)),
        in_specs=[VMEM],
        out_specs=(HBM, VMEM),
        scratch_shapes=[
            pltpu.VMEM((SPANS, W), BF),
            pltpu.VMEM((SLOTS // ROUTE_STEPS, SPANS), BF),
            pltpu.VMEM((N, U * S, HD), BF),
            pltpu.SemaphoreType.DMA((ROUTE_STEPS,)),
        ],
        flops=1.1e9,
    )(first)


def local(queries, out_grad, neighbours, placement):
    rows_in = 2 * U * C + C
    tokens = pltpu.VMEM(queries.shape, BF)
    first = swap(
        call(
            prep_body,
            pltpu.HBM((N, rows_in, HD), BF),
            in_specs=[HBM, HBM, HBM],
            out_specs=HBM,
            scratch_shapes=[
                tokens,
                tokens,
                pltpu.VMEM((2, C), jnp.int32),
                pltpu.VMEM((C, HD), F32),
                pltpu.VMEM((C * SPAN, C * SPAN), BF),
                pltpu.VMEM((N, rows_in, HD), BF),
                pltpu.SemaphoreType.DMA((3,)),
                pltpu.SemaphoreType.DMA((2,)),
            ],
            flops=5e8,
        )(in_hbm(queries), in_hbm(out_grad), in_hbm(placement.T))
    )
    square_sums = jnp.sum(jnp.square(neighbours.astype(F32)), axis=-1)
    row_scale = lax.rsqrt(lax.psum(square_sums, "head") / D + 1e-06)
    row_scale = jnp.pad(row_scale.T, ((0, 0), (0, HD - S)))

    first, row_scale = lax.optimization_barrier((first, row_scale))
    q_send, rowv = route(first, 0)
    got_q = swap(q_send)
    g_send = route(first, U * C)[0]
    got_g = swap(g_send)

    def cut(rows):
        return rows.reshape(N, U, S, HD)

    half_piece = pl.BlockSpec((N, U, HALF, HD), lambda i: (0, 0, i, 0))
    by_slot = lambda *tail: pl.BlockSpec((HALF, H // 2) + tail, lambda i: (i, 0, 0, 0))
    half_rows = pltpu.VMEM((N, U, HALF, HD), BF)
    diagonal = pltpu.VMEM((HALF, H // 2, 2 * SPAN, 2 * HD), BF)
    stat_acc = pltpu.VMEM((H // 2, 2 * SPAN, HD), F32)
    expo, keys, values, p_send, b_rows, stats = call(
        forward_body,
        (
            sds((S, H // 2, 2 * SPAN, R), F32),
            sds((S, H // 2, R, 2 * HD), BF),
            sds((S, H // 2, R, 2 * HD), BF),
            pltpu.HBM((N, U, S, HD), BF),
            pltpu.HBM((N, U, S, HD), BF),
            sds((N, C, HD), BF),
        ),
        grid=(2,),
        in_specs=[
            HBM,
            pl.BlockSpec((HALF, R, 2 * H * HD), lambda i: (i, 0, 0)),
            whole(R, HD),
        ],
        out_specs=(
            by_slot(2 * SPAN, R),
            by_slot(R, 2 * HD),
            by_slot(R, 2 * HD),
            half_piece,
            half_piece,
            whole(N, C, HD),
        ),
        scratch_shapes=[
            half_rows,
            diagonal,
            pltpu.VMEM((HALF, H, SPAN, 2 * HD), BF),
            stat_acc,
            stat_acc,
            pltpu.SemaphoreType.DMA,
        ],
        flops=2e9,
        nbytes=3e7,
        vmem=56,
    )(in_hbm(cut(got_q)), neighbours, row_scale)
    back_send = jnp.concatenate([p_send.reshape(N, U * S, HD), stats], axis=1)
    back_send, got_g = lax.optimization_barrier((back_send, got_g))
    back = swap(back_send)
    a_rows = call(
        backward_body,
        pltpu.HBM((N, U, S, HD), BF),
        grid=(2,),
        in_specs=[half_piece, by_slot(2 * SPAN, R), by_slot(R, 2 * HD), by_slot(R, 2 * HD)],
        out_specs=half_piece,
        scratch_shapes=[diagonal, pltpu.VMEM((HALF, H, SPAN, HD), BF)],
        flops=1e9,
        nbytes=2e7,
        vmem=48,
    )(cut(got_g), expo, keys, values)

    back, a_rows = lax.optimization_barrier((back, a_rows))
    span_table = pltpu.VMEM((SPANS, W), F32)
    column = pltpu.VMEM((SPANS, 1), F32)
    cat = pltpu.VMEM((SLOTS, W), BF)
    rows = sds((N, U * S, HD), BF)
    wd_send, wts, a_rows, b_rows = call(
        weight_body,
        (sds((N, C, HD), BF), sds((SPANS, HD), BF), rows, rows),
        in_specs=[VMEM, HBM, VMEM, HBM, HBM],
        scratch_shapes=[
            pltpu.VMEM((N, U * S, HD), BF),
            pltpu.VMEM((N * C, HD), F32),
            pltpu.SemaphoreType.DMA((PRODUCT_STEPS,)),
            pltpu.SemaphoreType.DMA((2,)),
        ],
    )(
        back,
        in_hbm(g_send),
        rowv,
        in_hbm(a_rows.reshape(N, U * S, HD)),
        in_hbm(b_rows.reshape(N, U * S, HD)),
    )
    wd = swap(wd_send)
    terms = call(
        scale_body,
        pltpu.HBM((N, U * S, HD), BF),
        in_specs=[VMEM, VMEM, VMEM],
        out_specs=HBM,
        scratch_shapes=[
            pltpu.VMEM((N, U * S, HD), BF),
            pltpu.SemaphoreType.DMA((PRODUCT_STEPS,)),
        ],
    )(wd, a_rows, b_rows)
    terms, wts = lax.optimization_barrier((terms, wts))
    attended = call(
        attended_body,
        sds((N, U * C, HD), BF),
        scratch_shapes=[cat, span_table, span_table, column, column],
        flops=2.2e9,
        vmem=40,
    )(in_hbm(back), rowv, wts)
    last = call(
        sum_body,
        sds((N, 2 * U * C, HD), BF),
        scratch_shapes=[cat, span_table, column, column],
        flops=1.1e9,
        vmem=48,
    )(swap(terms), attended, rowv)
    return call(
        final_body, (sds(queries.shape, BF), sds(queries.shape, BF)), flops=5e8
    )(swap(last))


def solution(mesh):
    in_specs = (P("seq", "head"), P("seq", "head"), P("seq", None, "head"), P("seq", None))
    out_specs = (P("seq", "head"), P("seq", "head"))
    return jax.shard_map(local, mesh=mesh, in_specs=in_specs, out_specs=out_specs, check_vma=False)
```
